256 devices in a mesh: scen: 64 (over x, z, core), inst: 4 (over y).
Axes of the slice: x: 4, y: 4, z: 8, core: 2. Of those that a mesh axis runs over, the one named last changes fastest.
Arguments:
- shocks: bfloat16 [262144, 128], P('scen'), may hold values from -6 to 6
- loadings: bfloat16 [128, 8192], P(None, ('inst', 'scen')), may hold values from -0.5 to 0.5
- greeks: bfloat16 [3, 8192], P(None, ('inst', 'scen')), may hold values from -6 to 6
- mean_return: float32 [8192], P('inst'), may hold values from -6 to 6
- weight_start: float32 [8, 8192], P(None, 'inst'), may hold values from 0 to 5.7
- dual_start: float32 [8, 262144], P(None, 'scen'), may hold values from 0 to 54
- level_start: float32 [8], replicated, may hold values from -4 to 4
- aversion: float32 [8], replicated, may hold values from 0.25 to 1.5
- primal_step: float32 [8], replicated, may hold values from 0.05 to 0.2
- dual_step: float32 [8], replicated, may hold values from 0.25 to 1
- restart_at: int32 [8], replicated, may hold values from 0 to 1
Outputs:
- weights: float32 [8, 8192], P(None, 'inst')
- duals: float32 [8, 262144], P(None, 'scen')
- shortfall: float32 [8, 262144], P(None, 'scen')
- threshold: float32 [8], replicated
The draws below stay inside these ranges and needn't reach their ends.
Inputs may be any that keep to these rules, and one draw needn't show every extreme that they name: `restart_at`: the iteration, counted from 0, after which the portfolio's state is replaced by the mean of its states since the start or its last replacement.
All inputs are finite; a program needn't handle non-finite values.
Results may differ from the reference program's by a relative error of at most 0.0003.
Values may be sent and summed in bfloat16 or wider, within the bound.
No kernel may reach another device: no remote copies, remote signals or barrier semaphores. Data moves between devices by JAX's collectives and lax.ppermute only.
A program may use at most 64 MiB of HBM per device.

```python
import math
import jax
import jax.numpy as jnp
from jax import lax

N = 8192
K = 128
PORT = 8
S_DEV = 4096
ITERS = 2
SCEN = 262144
N_SCEN = 64


def draw_weight_start(key, part):
    key = jax.random.fold_in(key, 11)
    column = jnp.arange(N, dtype=jnp.float32) / N
    noise = jax.random.uniform(key, (PORT, N), jnp.float32)
    return 2.0 * noise * (0.25 + 1.5 * column)[None, :]


def draw_dual_start(key, part):
    key = jax.random.fold_in(key, 23)
    position = jnp.arange(SCEN, dtype=jnp.float32) / SCEN
    noise = jax.random.uniform(key, (PORT, SCEN), jnp.float32)
    return 20.0 * noise * (0.45 + 1.1 * position)[None, :]


def place_ends(values, own_key, low, high):
    longest = values.shape.index(max(values.shape))
    spots = []
    for shift in (0, 1):
        where = [jax.random.randint(jax.random.fold_in(own_key, axis), (), 0, length) for axis, length in enumerate(values.shape)]
        where[longest] = (where[longest] + shift) % values.shape[longest]
        spots.append(tuple(where))
    return values.at[spots[0]].set(low).at[spots[1]].set(high)


def levels(rng, dims, shards, least, largest):
    gain, own = 1.0, jax.random.fold_in(rng, 6)
    for dim, blocks in shards:
        heights = jnp.exp(jax.random.uniform(jax.random.fold_in(own, dim), (blocks,), jnp.float32, least / len(shards), largest / len(shards)))
        gain = gain * jnp.repeat(heights, dims[dim] // blocks).reshape([-1 if axis == dim else 1 for axis in range(len(dims))])
    return gain


def gaussian(stream_key, shape, scale, bound, cuts=(), kind=jnp.bfloat16):
    drawn = scale * jax.random.normal(stream_key, shape, jnp.float32)
    if cuts:
        drawn = drawn * levels(stream_key, shape, cuts, -0.22, 0.18)
    return jnp.clip(drawn, -bound, bound).astype(kind)


def setup_inputs(seed: int = 0) -> dict:
    seeds = jax.random.split(jax.random.key(seed), 12)
    return {
        "shocks": gaussian(seeds[0], (SCEN, K), 1.0, 6.0, ((0, 64),)),
        "loadings": gaussian(seeds[1], (K, N), K ** -0.5, 0.5, ((1, 256),)),
        "greeks": gaussian(seeds[2], (3, N), 1.0, 6.0, ((1, 256),)),
        "mean_return": gaussian(seeds[3], (N,), 1.0, 6.0, ((0, 4),), jnp.float32),
        "weight_start": draw_weight_start(jax.random.fold_in(seeds[11], 71), 0),
        "dual_start": draw_dual_start(jax.random.fold_in(seeds[11], 71), 0),
        "level_start": gaussian(seeds[6], (PORT,), 1.0, 4.0, (), jnp.float32),
        "aversion": jnp.clip(jnp.exp(jax.random.uniform(seeds[7], (PORT,), jnp.float32, math.log(0.25), math.log(1.5))), 0.25, 1.5),
        "primal_step": jnp.clip(jnp.exp(jax.random.uniform(seeds[8], (PORT,), jnp.float32, math.log(0.05), math.log(0.2))), 0.05, 0.2),
        "dual_step": jnp.clip(jnp.exp(jax.random.uniform(seeds[9], (PORT,), jnp.float32, math.log(0.25), math.log(1.0))), 0.25, 1.0),
        "restart_at": place_ends(jax.random.randint(seeds[10], (PORT,), 0, ITERS), jax.random.fold_in(seeds[10], 1), 0, ITERS - 1).astype(jnp.int32),
    }


tail_weight = 20.0

def repricing(shock_rows, columns, sensitivity):
    moves = jnp.dot(shock_rows, columns, preferred_element_type=jnp.float32)
    delta = sensitivity[0].astype(jnp.float32)
    gamma = sensitivity[1].astype(jnp.float32)
    return (delta * moves + 0.5 * gamma * moves * moves).astype(jnp.bfloat16)

def spread(flags, value):
    return flags.reshape(flags.shape + (1,) * (value.ndim - 1))

def restart(state, totals, count, flags):
    totals = tuple((total + value for total, value in zip(totals, state)))
    count = count + 1.0
    means = tuple((total / spread(count, total) for total in totals))
    state = tuple((jnp.where(spread(flags, value), average, value) for value, average in zip(state, means)))
    totals = tuple((jnp.where(spread(flags, total), average, total) for total, average in zip(totals, means)))
    count = jnp.where(flags, 1.0, count)
    return (state, totals, count)

def primal_move(weight, level, excess, dual, unit_price, drift, back, mass, aversion, primal):
    weight_new = jnp.maximum(weight + primal[:, None] * (drift[None, :] + back + unit_price[:, None]), 0.0)
    level_new = level - primal * (aversion - mass)
    excess_new = jnp.maximum(excess - primal[:, None] * (tail_weight * aversion[:, None] - dual), 0.0)
    return (weight_new, level_new, excess_new)

def reference(shocks, loadings, greeks, mean_return, weight_start, dual_start, level_start, aversion, primal_step, dual_step, restart_at):
    scale = 1.0 / math.sqrt(N)
    shock_blocks = shocks.reshape(N_SCEN, S_DEV, K)

    def to_blocks(field):
        return field.reshape(PORT, N_SCEN, S_DEV).transpose(1, 0, 2)

    def from_blocks(field):
        return field.transpose(1, 0, 2).reshape(PORT, SCEN)

    def first_block(total, pieces):
        shock_rows, dual_rows = pieces
        pnl = repricing(shock_rows, loadings, greeks)
        return (total + jnp.dot(dual_rows.astype(jnp.bfloat16), pnl, preferred_element_type=jnp.float32), None)
    back, unused = lax.scan(first_block, jnp.zeros((PORT, N), jnp.float32), (shock_blocks, to_blocks(dual_start)))
    back = back / SCEN
    mass = lax.optimization_barrier(jnp.sum(dual_start, axis=1)) / SCEN
    weight = weight_start
    level = level_start
    excess = jnp.zeros((PORT, SCEN), jnp.float32)
    dual = dual_start
    unit_price = jnp.zeros((PORT,), jnp.float32)
    totals = (weight, level, excess, dual, unit_price)
    count = jnp.ones((PORT,), jnp.float32)
    for step in range(ITERS):
        weight_new, level_new, excess_new = primal_move(weight, level, excess, dual, unit_price, mean_return, back, mass, aversion, primal_step)
        weight_bar = 2.0 * weight_new - weight
        level_bar = 2.0 * level_new - level
        excess_bar = 2.0 * excess_new - excess
        rounded = weight_bar.astype(jnp.bfloat16)
        share = lax.optimization_barrier(jnp.sum(weight_bar, axis=1)) / N
        price_new = unit_price + dual_step * (1.0 - share)
        flags = restart_at == step
        later = step + 1 < ITERS
        count_next = count + 1.0

        def loss_block(total, pieces):
            shock_rows, excess_rows, dual_rows, kept_rows = pieces
            pnl = repricing(shock_rows, loadings, greeks)
            loss = lax.dot_general(rounded, pnl, (((1,), (1,)), ((), ())), preferred_element_type=jnp.float32) * scale
            dual_rows_new = jnp.maximum(dual_rows - dual_step[:, None] * (excess_rows + level_bar[:, None] + loss), 0.0)
            if later:
                used = jnp.where(flags[:, None], (kept_rows + dual_rows_new) / count_next[:, None], dual_rows_new)
                total = total + jnp.dot(used.astype(jnp.bfloat16), pnl, preferred_element_type=jnp.float32)
            return (total, dual_rows_new)
        total, dual_blocks = lax.scan(loss_block, jnp.zeros((PORT, N), jnp.float32), (shock_blocks, to_blocks(excess_bar), to_blocks(dual), to_blocks(totals[3])))
        dual_new = from_blocks(dual_blocks)
        state, totals, count = restart((weight_new, level_new, excess_new, dual_new, price_new), totals, count, flags)
        weight, level, excess, dual, unit_price = state
        if later:
            back = total / SCEN
            mass = lax.optimization_barrier(jnp.sum(dual, axis=1)) / SCEN
    return (weight, dual, excess, level)
```

```python
import math

import jax
import jax.numpy as jnp
from jax import lax
from jax.experimental import pallas as pl
from jax.experimental.pallas import tpu as pltpu
from jax.sharding import PartitionSpec as P

F32 = jnp.float32
BF16 = jnp.bfloat16
DEPTH = 128
SCEN_DEV = 4096
PEERS = 64
RING = 4
OWN = 2
PIECE = 16
HALF = PEERS * PIECE
BLOCK = 2 * HALF
ALL = RING * HALF
TOTAL_SCEN = float(PEERS * SCEN_DEV)
TOTAL_INST = float(RING * BLOCK)
SCALE = 1.0 / math.sqrt(TOTAL_INST)
TAIL = 20.0
CHUNK = 512
NCHUNK = SCEN_DEV // CHUNK
FIRST = 24
LATER = 8
PACK = HALF + PEERS + 80
VMEM = pltpu.CompilerParams(vmem_limit_bytes=48 * 1024 * 1024)


def dot(a, b):
    return jnp.dot(a, b, preferred_element_type=F32)


def dot_nt(a, b):
    return lax.dot_general(a, b, (((1,), (1,)), ((), ())), preferred_element_type=F32)


def split2(value):
    high = value.astype(BF16)
    return high, (value - high.astype(F32)).astype(BF16)


def split3(value):
    high = value.astype(BF16)
    rest = value - high.astype(F32)
    middle = rest.astype(BF16)
    return high, middle, (rest - middle.astype(F32)).astype(BF16)


def grid_iota(shape, axis):
    return lax.broadcasted_iota(jnp.int32, shape, axis)


def identity(size):
    return jnp.where(grid_iota((size, size), 0) == grid_iota((size, size), 1), 1.0, 0.0).astype(BF16)


def column(ref, place):
    return jnp.where(grid_iota((OWN, 1), 0) == 0, ref[OWN * place], ref[OWN * place + 1])


def turn_to(rows, y):
    return pltpu.roll(rows, (8 - OWN * y) & 7, axis=0)


def turn_back(rows, y):
    return pltpu.roll(rows, (OWN * y) & 7, axis=0)


def count_row(mass):
    lane = grid_iota((1, DEPTH), 1)
    row = jnp.zeros((1, DEPTH), F32)
    for own in range(OWN):
        for part, value in enumerate(split3(mass[own : own + 1, :])):
            row = jnp.where(lane == 32 + 3 * own + part, value.astype(F32), row)
    return row


def mass_of(stat):
    first = stat[6:7, 32:33] + stat[6:7, 33:34] + stat[6:7, 34:35]
    second = stat[6:7, 35:36] + stat[6:7, 36:37] + stat[6:7, 37:38]
    return jnp.where(grid_iota((OWN, 1), 0) == 0, first, second)


def tail_rows(rows):
    return jnp.concatenate([rows, jnp.zeros((16 - OWN, rows.shape[1]), rows.dtype)], axis=0)


def moments(dual_of, shocks_ref, turned_of):
    total = jnp.zeros((OWN * DEPTH + 16, DEPTH), F32)
    mass = jnp.zeros((OWN, 1), F32)
    for step in range(NCHUNK):
        cut = slice(step * CHUNK, (step + 1) * CHUNK)
        dual = dual_of(cut)
        rounded = dual.astype(BF16).astype(F32)
        turned = turned_of(cut)
        left = [(turned * rounded[own : own + 1, :]).astype(BF16) for own in range(OWN)]
        left = jnp.concatenate(left + [tail_rows(rounded).astype(BF16)], axis=0)
        total = total + dot(left, shocks_ref[cut, :])
        mass = mass + jnp.sum(dual, axis=1, keepdims=True)
    return total * (1.0 / TOTAL_SCEN), mass * (1.0 / TOTAL_SCEN)


def open_kernel(place, shocks, dual, loadings, greeks, send, turned, work):
    y = place[0]
    unit = identity(DEPTH)

    def turned_of(cut):
        value = dot_nt(unit, shocks[cut, :])
        turned[:, cut] = value.astype(BF16)
        return value

    total, mass = moments(lambda cut: turn_to(dual[:, cut], y)[0:OWN, :], shocks, turned_of)
    rows = dot_nt(identity(2 * PIECE), loadings[...])
    sens = greeks[...].astype(F32)
    delta, gamma = sens[0:1, :].astype(BF16), sens[1:2, :].astype(BF16)
    m = grid_iota((2 * PIECE, DEPTH), 0)
    lane = grid_iota((2 * PIECE, DEPTH), 1)
    tally = count_row(mass)
    notes = []
    for half in range(2):
        near = jnp.where((m == lane + PIECE * half) & (lane < PIECE), 1.0, 0.0).astype(BF16)
        far = jnp.where(
            (m == lane - PIECE + PIECE * half) & (lane >= PIECE) & (lane < 2 * PIECE), 1.0, 0.0
        ).astype(BF16)
        notes.append(dot(delta, near) + dot(gamma, far) + tally)
    blank = jnp.zeros((1, DEPTH), F32)
    for peer in range(PEERS):
        half = peer % 2
        work[peer, 0:16, :] = rows[PIECE * half : PIECE * (half + 1), :]
        work[peer, 16:20, :] = total[4 * peer : 4 * peer + 4, :]
        work[peer, 20:24, :] = jnp.concatenate([total[256:258, :], notes[half], blank], axis=0)
    send[...] = work[...].astype(BF16).reshape(PEERS * FIRST, DEPTH)


def sort_kernel(place, received, holdings, returns, spread, stat, *rest):
    packs, (work, chosen) = rest[:RING], rest[RING:]
    y, core = place[0], place[1]
    work[...] = received[...].astype(F32)
    whole = work[...].reshape(PEERS, FIRST, DEPTH)
    sums = jnp.sum(whole[:, 16:24, :], axis=0)
    stat[...] = sums
    spread[...] = jnp.broadcast_to(sums[0:4, :][None], (PEERS, 4, DEPTH)).reshape(PEERS * 4, DEPTH)
    rows = whole[:, 0:16, :].reshape(HALF, DEPTH).astype(BF16)
    notes = work[pl.ds(22, PEERS, stride=FIRST), :].astype(BF16)
    m = grid_iota((2 * DEPTH, DEPTH), 0)
    lane = grid_iota((2 * DEPTH, DEPTH), 1)
    pick = jnp.where(m == (lane >> 4) * 32 + core * PIECE + (lane & 15), 1.0, 0.0).astype(BF16)
    for part in range(BLOCK // 256):
        cut = slice(256 * part, 256 * (part + 1))
        both = jnp.concatenate(
            [turn_to(holdings[:, cut], y), returns[:, cut], jnp.zeros((7, 256), F32)], axis=0
        )
        for level, value in enumerate(split3(both)):
            chosen[16 * (8 * level + part) : 16 * (8 * level + part) + 16, :] = dot(value, pick)
    for hop in range(RING):
        pieces = [chosen[16 * n + OWN * hop : 16 * n + OWN * (hop + 1), :] for n in range(24)]
        pieces += [chosen[16 * n + 8 : 16 * n + 9, :] for n in range(24)]
        pieces.append(jnp.zeros((8, DEPTH), F32))
        packs[hop][0:HALF, :] = rows
        packs[hop][HALF : HALF + PEERS, :] = notes
        packs[hop][HALF + PEERS : PACK, :] = jnp.concatenate(pieces, axis=0).astype(BF16)


def later_kernel(received, spread, stat, work):
    work[...] = received[...].astype(F32)
    sums = jnp.sum(work[...].reshape(PEERS, LATER, DEPTH), axis=0)
    stat[...] = sums
    spread[...] = jnp.broadcast_to(sums[0:4, :][None], (PEERS, 4, DEPTH)).reshape(PEERS * 4, DEPTH)


def matrix_parts(moment, stat):
    whole = jnp.concatenate([moment, tail_rows(stat[4:6, :])], axis=0)
    return split2(whole)


def holdings_step(parts, turned, delta, gamma, weight, returns, price, primal):
    wide = turned.astype(BF16)
    form = dot(parts[0], wide) + dot(parts[1], wide)
    curve = [
        jnp.sum(form[DEPTH * own : DEPTH * (own + 1), :] * turned, axis=0, keepdims=True)
        for own in range(OWN)
    ]
    back = delta * form[OWN * DEPTH : OWN * DEPTH + OWN, :] + gamma * jnp.concatenate(curve, axis=0)
    fresh = jnp.maximum(weight + primal * (returns + back + price), 0.0)
    return fresh, 2.0 * fresh - weight


def holdings_matrix(bar, turned, rows, delta, gamma):
    rounded = bar.astype(BF16).astype(F32)
    curve = rounded * gamma
    left = [turned * curve[own : own + 1, :] for own in range(OWN)]
    left = jnp.concatenate(left + [tail_rows(rounded * delta)], axis=0)
    high, low = split2(left)
    return dot(high, rows) + dot(low, rows)


def share_rows(bar_sum):
    return jnp.broadcast_to(bar_sum, (OWN, DEPTH))


def first_primal(
    place, primal_step, restart_at, moment, stat, pack0, pack1, pack2, pack3,
    given, turned, sens, returns, weight, weight_sum,
):
    y = place[0]
    primal = column(primal_step, y)
    flag = column(restart_at, y) == 0
    parts = matrix_parts(moment[...], stat[...])
    unit = identity(DEPTH)
    total = jnp.zeros((OWN * DEPTH + 16, DEPTH), F32)
    bar_sum = jnp.zeros((OWN, 1), F32)
    row = grid_iota((PEERS, HALF), 0)
    col = grid_iota((PEERS, HALF), 1)
    mine = row == (col >> 4)
    m = grid_iota((DEPTH, HALF), 0)
    slot = grid_iota((DEPTH, HALF), 1) & 15
    near = jnp.where(m == slot, 1.0, 0.0).astype(BF16)
    far = jnp.where(m == slot + PIECE, 1.0, 0.0).astype(BF16)
    for hop, pack in enumerate((pack0, pack1, pack2, pack3)):
        cut = slice(HALF * hop, HALF * (hop + 1))
        rows = pack[0:HALF, :]
        notes = pack[HALF : HALF + PEERS, :]
        wide = dot_nt(unit, rows)
        turned[:, cut] = wide.astype(BF16)
        delta = jnp.sum(jnp.where(mine, dot(notes, near), 0.0), axis=0, keepdims=True)
        gamma = 0.5 * jnp.sum(jnp.where(mine, dot(notes, far), 0.0), axis=0, keepdims=True)
        sens[0:1, cut] = delta
        sens[1:2, cut] = gamma
        more = pack[HALF + PEERS : PACK, :].astype(F32)
        held = [
            more[2 * n : 2 * n + 2, :] + more[2 * n + 16 : 2 * n + 18, :] + more[2 * n + 32 : 2 * n + 34, :]
            for n in range(8)
        ]
        gain = [
            more[48 + n : 49 + n, :] + more[56 + n : 57 + n, :] + more[64 + n : 65 + n, :]
            for n in range(8)
        ]
        held = jnp.concatenate(held, axis=1)
        gain = jnp.concatenate(gain, axis=1)
        returns[:, cut] = gain
        fresh, bar = holdings_step(parts, wide, delta, gamma, held, gain, 0.0, primal)
        bar_sum = bar_sum + jnp.sum(bar, axis=1, keepdims=True)
        total = total + holdings_matrix(bar, wide, rows, delta, gamma)
        both = held + fresh
        weight[:, cut] = jnp.where(flag, both / 2.0, fresh)
        weight_sum[:, cut] = jnp.where(flag, both / 2.0, both)
    given[0:256, :] = total[0:256, :]
    given[256:264, :] = jnp.concatenate(
        [total[256:258, :], share_rows(bar_sum), jnp.zeros((4, DEPTH), F32)], axis=0
    )


def second_primal(
    place, primal_step, restart_at, moment, stat, pack0, pack1, pack2, pack3,
    turned, sens, returns, weight, weight_sum, small, given,
):
    y = place[0]
    primal = column(primal_step, y)
    first = column(restart_at, y) == 0
    flag = column(restart_at, y) == 1
    count = jnp.where(first, 2.0, 3.0)
    price = small[4:6, 0:1]
    parts = matrix_parts(moment[...], stat[...])
    total = jnp.zeros((OWN * DEPTH + 16, DEPTH), F32)
    bar_sum = jnp.zeros((OWN, 1), F32)
    for hop, pack in enumerate((pack0, pack1, pack2, pack3)):
        cut = slice(HALF * hop, HALF * (hop + 1))
        rows = pack[0:HALF, :]
        wide = turned[:, cut].astype(F32)
        delta, gamma = sens[0:1, cut], sens[1:2, cut]
        held = weight[:, cut]
        fresh, bar = holdings_step(parts, wide, delta, gamma, held, returns[:, cut], price, primal)
        bar_sum = bar_sum + jnp.sum(bar, axis=1, keepdims=True)
        total = total + holdings_matrix(bar, wide, rows, delta, gamma)
        last = jnp.where(flag, (weight_sum[:, cut] + fresh) / count, fresh)
        for part in range(8):
            spot = 264 + OWN * (8 * hop + part)
            given[spot : spot + OWN, :] = last[:, DEPTH * part : DEPTH * (part + 1)]
    given[0:256, :] = total[0:256, :]
    given[256:264, :] = jnp.concatenate(
        [total[256:258, :], share_rows(bar_sum), jnp.zeros((4, DEPTH), F32)], axis=0
    )


def losses(parts, turned):
    wide = turned.astype(F32)
    form = dot(parts[0], turned) + dot(parts[1], turned)
    rows = [
        jnp.sum(form[DEPTH * own : DEPTH * (own + 1), :] * wide, axis=0, keepdims=True)
        for own in range(OWN)
    ]
    return jnp.concatenate(rows, axis=0) + form[OWN * DEPTH : OWN * DEPTH + OWN, :]


def joint(given, other):
    whole = given[0:264, :] + other[0:264, :]
    share = whole[258:260, 0:1] * (1.0 / TOTAL_INST)
    matrix = jnp.concatenate([whole[0:256, :], tail_rows(whole[256:258, :])], axis=0)
    return split2(matrix * SCALE), share


def first_dual(
    place, primal_step, dual_step, aversion, level_start, restart_at, given, other, shocks, turned, dual_start, stat,
    send, dual, dual_sum, excess, excess_sum, small, work,
):
    y = place[0]
    primal, rate, averse = column(primal_step, y), column(dual_step, y), column(aversion, y)
    level = column(level_start, y)
    flag = column(restart_at, y) == 0
    parts, share = joint(given, other)
    level_new = level - primal * (averse - mass_of(stat))
    level_bar = 2.0 * level_new - level
    price_new = rate * (1.0 - share)

    def settle(old, new):
        both = old + new
        return jnp.where(flag, both / 2.0, new), jnp.where(flag, both / 2.0, both)

    def dual_of(cut):
        old = turn_to(dual_start[:, cut], y)[0:OWN, :]
        loss = losses(parts, turned[:, cut])
        extra = jnp.maximum(0.0 - primal * (TAIL * averse - old), 0.0)
        fresh = jnp.maximum(old - rate * (2.0 * extra + level_bar + loss), 0.0)
        state, both = settle(old, fresh)
        dual[:, cut] = state
        dual_sum[:, cut] = both
        state_extra, both_extra = settle(jnp.zeros_like(extra), extra)
        excess[:, cut] = state_extra
        excess_sum[:, cut] = both_extra
        return state

    total, mass = moments(dual_of, shocks, lambda cut: turned[:, cut].astype(F32))
    pieces = settle(level, level_new) + settle(jnp.zeros_like(price_new), price_new)
    small[...] = jnp.concatenate([jnp.broadcast_to(piece, (OWN, DEPTH)) for piece in pieces], axis=0)
    note = count_row(mass)
    blank = jnp.zeros((1, DEPTH), F32)
    for peer in range(PEERS):
        work[peer, 0:4, :] = total[4 * peer : 4 * peer + 4, :]
        work[peer, 4:8, :] = jnp.concatenate([total[256:258, :], note, blank], axis=0)
    send[...] = work[...].astype(BF16).reshape(PEERS * LATER, DEPTH)


def second_dual(
    place, primal_step, dual_step, aversion, restart_at, given, other, turned, dual, dual_sum, excess, excess_sum,
    small, stat, out0, out1, out2, out3,
):
    y, core = place[0], place[1]
    outs = (out0, out1, out2, out3)
    primal, rate, averse = column(primal_step, y), column(dual_step, y), column(aversion, y)
    flag = column(restart_at, y) == 1
    count = jnp.where(column(restart_at, y) == 0, 2.0, 3.0)
    parts, _ = joint(given, other)
    level = small[0:2, 0:1]
    level_new = level - primal * (averse - mass_of(stat))
    level_bar = 2.0 * level_new - level

    def settle(both, new):
        return jnp.where(flag, (both + new) / count, new)

    for step in range(NCHUNK):
        cut = slice(step * CHUNK, (step + 1) * CHUNK)
        old, old_extra = dual[:, cut], excess[:, cut]
        loss = losses(parts, turned[:, cut])
        extra = jnp.maximum(old_extra - primal * (TAIL * averse - old), 0.0)
        fresh = jnp.maximum(old - rate * ((2.0 * extra - old_extra) + level_bar + loss), 0.0)
        last = settle(dual_sum[:, cut], fresh)
        last_extra = settle(excess_sum[:, cut], extra)
        for out in outs:
            out[:, cut] = last
            out[:, SCEN_DEV + step * CHUNK : SCEN_DEV + (step + 1) * CHUNK] = last_extra
    last_level = jnp.broadcast_to(settle(small[2:4, 0:1], level_new), (OWN, DEPTH))
    m = grid_iota((DEPTH, 256), 0)
    lane = grid_iota((DEPTH, 256), 1)
    source = (lane >> 5) * PIECE + (lane & 15)
    mine = ((lane >> 4) & 1) == core
    own_pick = jnp.where((m == source) & mine, 1.0, 0.0).astype(BF16)
    other_pick = jnp.where((m == source) & jnp.logical_not(mine), 1.0, 0.0).astype(BF16)
    own_parts, other_parts = split3(given[264:328, :]), split3(other[264:328, :])
    pieces = [dot(a, own_pick) + dot(b, other_pick) for a, b in zip(own_parts, other_parts)]
    held = pieces[0] + pieces[1] + pieces[2]
    for hop, out in enumerate(outs):
        out[:, 2 * SCEN_DEV + BLOCK :] = last_level
        for part in range(8):
            spot = OWN * (8 * hop + part)
            start = 2 * SCEN_DEV + 256 * part
            out[:, start : start + 256] = held[spot : spot + OWN, :]


def close_kernel(place, in0, in1, in2, in3, weights, duals, shortfall, threshold):
    y = place[0]
    start = 0
    for out, width in ((duals, SCEN_DEV), (shortfall, SCEN_DEV), (weights, BLOCK), (threshold, DEPTH)):
        for left in range(0, width, CHUNK):
            right = min(left + CHUNK, width)
            cut = slice(start + left, start + right)
            rows = jnp.concatenate([taken[:, cut] for taken in (in0, in1, in2, in3)], axis=0)
            out[:, left:right] = turn_back(rows, y)
        start += width


def kernel(body, name, scalars, arrays, outs, scratch=()):
    small = pl.BlockSpec(memory_space=pltpu.SMEM)
    large = pl.BlockSpec(memory_space=pltpu.VMEM)
    call = pl.pallas_call(
        body,
        name=name,
        in_specs=[small] * len(scalars) + [large] * len(arrays),
        out_specs=[large] * len(outs),
        out_shape=[jax.ShapeDtypeStruct(shape, dtype) for shape, dtype in outs],
        scratch_shapes=list(scratch),
        compiler_params=VMEM,
    )
    return list(call(*scalars, *arrays))


def along(value, hop):
    return lax.ppermute(value, "inst", [(i, (i + hop) % RING) for i in range(RING)])


def across(value):
    return lax.ppermute(value, "scen", [(i, i ^ 1) for i in range(PEERS)])


def exchange(value):
    return lax.all_to_all(value, "scen", 0, 0, tiled=True)


def on_device(
    shocks, loadings, greeks, mean_return, weight_start, dual_start, level_start, aversion, primal_step, dual_step, restart_at,
):
    place = jnp.stack([lax.axis_index("inst"), lax.axis_index("scen") % 2]).astype(jnp.int32)
    row_count = OWN * DEPTH
    send, turned = kernel(
        open_kernel, "open", [place], [shocks, dual_start, loadings, greeks],
        [((PEERS * FIRST, DEPTH), BF16), ((DEPTH, SCEN_DEV), BF16)],
        [pltpu.VMEM((PEERS, FIRST, DEPTH), F32)],
    )
    received = exchange(send)
    spread, stat, *packs = kernel(
        sort_kernel, "sort", [place], [received, weight_start, mean_return[None, :]],
        [((row_count, DEPTH), F32), ((8, DEPTH), F32)] + [((PACK, DEPTH), BF16)] * RING,
        [pltpu.VMEM((PEERS * FIRST, DEPTH), F32), pltpu.VMEM((24 * 16, DEPTH), F32)],
    )
    packs = packs[:1] + [along(packs[hop], hop) for hop in range(1, RING)]
    moment = exchange(spread)
    given, loads, sens, returns, weight, weight_sum = kernel(
        first_primal, "first_primal", [place, primal_step, restart_at], [moment, stat, *packs],
        [((264, DEPTH), F32), ((DEPTH, ALL), BF16), ((2, ALL), F32), ((1, ALL), F32), ((OWN, ALL), F32), ((OWN, ALL), F32)],
    )
    other = across(given)
    send, dual, dual_sum, excess, excess_sum, small = kernel(
        first_dual, "first_dual", [place, primal_step, dual_step, aversion, level_start, restart_at],
        [given, other, shocks, turned, dual_start, stat],
        [((PEERS * LATER, DEPTH), BF16)] + [((OWN, SCEN_DEV), F32)] * 4 + [((8, DEPTH), F32)],
        [pltpu.VMEM((PEERS, LATER, DEPTH), F32)],
    )
    received = exchange(send)
    spread, stat = kernel(
        later_kernel, "later", [], [received], [((row_count, DEPTH), F32), ((8, DEPTH), F32)],
        [pltpu.VMEM((PEERS * LATER, DEPTH), F32)],
    )
    moment = exchange(spread)
    (given,) = kernel(
        second_primal, "second_primal", [place, primal_step, restart_at],
        [moment, stat, *packs, loads, sens, returns, weight, weight_sum, small],
        [((328, DEPTH), F32)],
    )
    other = across(given)
    outs = kernel(
        second_dual, "second_dual", [place, primal_step, dual_step, aversion, restart_at],
        [given, other, turned, dual, dual_sum, excess, excess_sum, small, stat],
        [((OWN, 2 * SCEN_DEV + BLOCK + DEPTH), F32)] * RING,
    )
    taken = outs[:1] + [along(outs[hop], -hop) for hop in range(1, RING)]
    weights, duals, shortfall, threshold = kernel(
        close_kernel, "close", [place], taken,
        [((8, BLOCK), F32), ((8, SCEN_DEV), F32), ((8, SCEN_DEV), F32), ((8, DEPTH), F32)],
    )
    return weights, duals, shortfall, threshold[:, 0]


def solution(mesh):
    placed = (
        P("scen", None),
        P(None, ("inst", "scen")),
        P(None, ("inst", "scen")),
        P("inst"),
        P(None, "inst"),
        P(None, "scen"),
        P(),
        P(),
        P(),
        P(),
        P(),
    )
    return jax.shard_map(
        on_device,
        mesh=mesh,
        in_specs=placed,
        out_specs=(P(None, "inst"), P(None, "scen"), P(None, "scen"), P()),
        check_vma=False,
    )
```

```python
import math

import jax
import jax.numpy as jnp
import numpy as np
from jax import lax
from jax.experimental import pallas as pl
from jax.experimental.pallas import tpu as pltpu
from jax.sharding import Mesh, PartitionSpec as P

F32 = jnp.float32
BF16 = jnp.bfloat16
DEPTH = 128
SCEN_DEV = 4096
GRID_X, GRID_Z, CORES = 4, 8, 2
PEERS = GRID_X * GRID_Z * CORES
RING = 4
OWN = 2
PIECE = 16
HALF = PEERS * PIECE
BLOCK = 2 * HALF
ALL = RING * HALF
TOTAL_SCEN = float(PEERS * SCEN_DEV)
TOTAL_INST = float(RING * BLOCK)
SCALE = 1.0 / math.sqrt(TOTAL_INST)
TAIL = 20.0
CHUNK = 512
NCHUNK = SCEN_DEV // CHUNK
FIRST = 24
LINES = OWN * ALL // DEPTH
SENT = LINES + 16
PACK = HALF + PEERS + 80
LIMIT = 48 * 1024 * 1024


def dot(a, b):
    return jnp.dot(a, b, preferred_element_type=F32)


def dot_nt(a, b):
    return lax.dot_general(a, b, (((1,), (1,)), ((), ())), preferred_element_type=F32)


def split2(value):
    high = value.astype(BF16)
    return high, (value - high.astype(F32)).astype(BF16)


def split3(value):
    high = value.astype(BF16)
    rest = value - high.astype(F32)
    middle = rest.astype(BF16)
    return high, middle, (rest - middle.astype(F32)).astype(BF16)


def grid_iota(shape, axis):
    return lax.broadcasted_iota(jnp.int32, shape, axis)


def identity(size):
    return jnp.where(grid_iota((size, size), 0) == grid_iota((size, size), 1), 1.0, 0.0).astype(BF16)


def column(ref, place):
    return jnp.where(grid_iota((OWN, 1), 0) == 0, ref[OWN * place], ref[OWN * place + 1])


def turn_to(rows, y):
    return pltpu.roll(rows, (8 - OWN * y) & 7, axis=0)


def turn_back(rows, y):
    return pltpu.roll(rows, (OWN * y) & 7, axis=0)


def count_row(mass):
    lane = grid_iota((1, DEPTH), 1)
    row = jnp.zeros((1, DEPTH), F32)
    for own in range(OWN):
        for part, value in enumerate(split3(mass[own : own + 1, :])):
            row = jnp.where(lane == 32 + 3 * own + part, value.astype(F32), row)
    return row


def mass_of(stat):
    first = stat[6:7, 32:33] + stat[6:7, 33:34] + stat[6:7, 34:35]
    second = stat[6:7, 35:36] + stat[6:7, 36:37] + stat[6:7, 37:38]
    return jnp.where(grid_iota((OWN, 1), 0) == 0, first, second)


def tail_rows(rows):
    return jnp.concatenate([rows, jnp.zeros((16 - OWN, rows.shape[1]), rows.dtype)], axis=0)


def moments(dual_of, shocks_ref, turned_of):
    total = jnp.zeros((OWN * DEPTH + 16, DEPTH), F32)
    mass = jnp.zeros((OWN, 1), F32)
    for step in range(NCHUNK):
        cut = slice(step * CHUNK, (step + 1) * CHUNK)
        dual = dual_of(cut)
        rounded = dual.astype(BF16).astype(F32)
        turned = turned_of(cut)
        left = [(turned * rounded[own : own + 1, :]).astype(BF16) for own in range(OWN)]
        left = jnp.concatenate(left + [tail_rows(rounded).astype(BF16)], axis=0)
        total = total + dot(left, shocks_ref[cut, :])
        mass = mass + jnp.sum(dual, axis=1, keepdims=True)
    return total * (1.0 / TOTAL_SCEN), mass * (1.0 / TOTAL_SCEN)


def open_kernel(place, shocks_in, dual_in, loadings_in, greeks_in, holdings_in, returns_in, *rest):
    send, turned, chosen, work, shocks, dual, loadings, greeks, holdings, returns, gates = rest
    y, core = place[0], place[1]
    unit = identity(DEPTH)
    pairs = (
        (shocks_in, shocks), (dual_in, dual), (loadings_in, loadings), (greeks_in, greeks), (holdings_in, holdings),
        (returns_in, returns),
    )
    copies = [pltpu.make_async_copy(a, b, gates.at[n]) for n, (a, b) in enumerate(pairs)]
    for copy in copies:
        copy.start()
    for copy in copies:
        copy.wait()
    m = grid_iota((2 * DEPTH, DEPTH), 0)
    lane = grid_iota((2 * DEPTH, DEPTH), 1)
    pick = jnp.where(m == (lane >> 4) * 32 + core * PIECE + (lane & 15), 1.0, 0.0).astype(BF16)
    for part in range(BLOCK // 256):
        cut = slice(256 * part, 256 * (part + 1))
        both = jnp.concatenate(
            [turn_to(holdings[:, cut], y), returns[:, cut], jnp.zeros((7, 256), F32)], axis=0
        )
        for level, value in enumerate(split3(both)):
            chosen[16 * (8 * level + part) : 16 * (8 * level + part) + 16, :] = dot(value, pick)

    def turned_of(cut):
        value = dot_nt(unit, shocks[cut, :])
        turned[:, cut] = value.astype(BF16)
        return value

    total, mass = moments(lambda cut: turn_to(dual[:, cut], y)[0:OWN, :], shocks, turned_of)
    rows = loadings[...].astype(F32)
    sens = greeks[...].astype(F32)
    delta, gamma = sens[0:1, :].astype(BF16), sens[1:2, :].astype(BF16)
    m = grid_iota((2 * PIECE, DEPTH), 0)
    lane = grid_iota((2 * PIECE, DEPTH), 1)
    tally = count_row(mass)
    notes = []
    for half in range(2):
        near = jnp.where((m == lane + PIECE * half) & (lane < PIECE), 1.0, 0.0).astype(BF16)
        far = jnp.where(
            (m == lane - PIECE + PIECE * half) & (lane >= PIECE) & (lane < 2 * PIECE), 1.0, 0.0
        ).astype(BF16)
        notes.append(dot(delta, near) + dot(gamma, far) + tally)
    blank = jnp.zeros((1, DEPTH), F32)
    for peer in range(PEERS):
        half = peer % 2
        work[peer, 0:16, :] = rows[PIECE * half : PIECE * (half + 1), :]
        work[peer, 16:20, :] = total[4 * peer : 4 * peer + 4, :]
        work[peer, 20:24, :] = jnp.concatenate([total[256:258, :], notes[half], blank], axis=0)
    send[...] = work[...].astype(BF16).reshape(PEERS * FIRST, DEPTH)


def sort_kernel(received, chosen, spread, stat, *rest):
    packs, work = rest[:RING], rest[RING]
    work[...] = received[...].astype(F32)
    whole = work[...].reshape(PEERS, FIRST, DEPTH)
    sums = jnp.sum(whole[:, 16:24, :], axis=0)
    stat[...] = sums
    spread[...] = jnp.broadcast_to(sums[0:4, :][None], (PEERS, 4, DEPTH)).reshape(PEERS * 4, DEPTH)
    rows = whole[:, 0:16, :].reshape(HALF, DEPTH).astype(BF16)
    notes = work[pl.ds(22, PEERS, stride=FIRST), :].astype(BF16)
    for hop in range(RING):
        pieces = [chosen[16 * n + OWN * hop : 16 * n + OWN * (hop + 1), :] for n in range(24)]
        pieces += [chosen[16 * n + 8 : 16 * n + 9, :] for n in range(24)]
        pieces.append(jnp.zeros((8, DEPTH), F32))
        packs[hop][0:HALF, :] = rows
        packs[hop][HALF : HALF + PEERS, :] = notes
        packs[hop][HALF + PEERS : PACK, :] = jnp.concatenate(pieces, axis=0).astype(BF16)


def matrix_parts(moment, linear):
    return jnp.concatenate(split2(jnp.concatenate([moment, tail_rows(linear)], axis=0)), axis=1)


def forms(parts, half):
    form = dot(parts, jnp.concatenate([half, half], axis=0))
    wide = half.astype(F32)
    curve = [
        jnp.sum(form[DEPTH * own : DEPTH * (own + 1), :] * wide, axis=0, keepdims=True)
        for own in range(OWN)
    ]
    return jnp.concatenate(curve, axis=0), form[OWN * DEPTH : OWN * DEPTH + OWN, :]


def holdings_matrix(bar, turned, rows, delta, gamma):
    rounded = bar.astype(BF16).astype(F32)
    curve = rounded * gamma
    left = [turned * curve[own : own + 1, :] for own in range(OWN)]
    left = jnp.concatenate(left + [tail_rows(rounded * delta)], axis=0)
    high, low = split2(left)
    return dot(high, rows) + dot(low, rows)


def share_rows(bar_sum):
    return jnp.broadcast_to(bar_sum, (OWN, DEPTH))


def first_primal(
    place, primal_step, restart_at, moment, stat, pack0, pack1, pack2, pack3,
    given, turned, sens, returns, weight, weight_sum,
):
    y = place[0]
    primal = column(primal_step, y)
    flag = column(restart_at, y) == 0
    parts = matrix_parts(moment[...], stat[4:6, :])
    unit = identity(DEPTH)
    total = jnp.zeros((OWN * DEPTH + 16, DEPTH), F32)
    bar_sum = jnp.zeros((OWN, 1), F32)
    row = grid_iota((PEERS, HALF), 0)
    col = grid_iota((PEERS, HALF), 1)
    mine = row == (col >> 4)
    m = grid_iota((DEPTH, HALF), 0)
    slot = grid_iota((DEPTH, HALF), 1) & 15
    near = jnp.where(m == slot, 1.0, 0.0).astype(BF16)
    far = jnp.where(m == slot + PIECE, 1.0, 0.0).astype(BF16)
    for hop, pack in enumerate((pack0, pack1, pack2, pack3)):
        cut = slice(HALF * hop, HALF * (hop + 1))
        rows = pack[0:HALF, :]
        notes = pack[HALF : HALF + PEERS, :]
        wide = dot_nt(unit, rows)
        half = wide.astype(BF16)
        turned[:, cut] = half
        delta = jnp.sum(jnp.where(mine, dot(notes, near), 0.0), axis=0, keepdims=True)
        gamma = 0.5 * jnp.sum(jnp.where(mine, dot(notes, far), 0.0), axis=0, keepdims=True)
        sens[0:1, cut] = delta
        sens[1:2, cut] = gamma
        more = pack[HALF + PEERS : PACK, :].astype(F32)
        held = [
            more[2 * n : 2 * n + 2, :] + more[2 * n + 16 : 2 * n + 18, :] + more[2 * n + 32 : 2 * n + 34, :]
            for n in range(8)
        ]
        gain = [
            more[48 + n : 49 + n, :] + more[56 + n : 57 + n, :] + more[64 + n : 65 + n, :]
            for n in range(8)
        ]
        held = jnp.concatenate(held, axis=1)
        gain = jnp.concatenate(gain, axis=1)
        returns[:, cut] = gain
        curve, line = forms(parts, half)
        fresh = jnp.maximum(held + primal * (gain + (delta * line + gamma * curve)), 0.0)
        bar = 2.0 * fresh - held
        bar_sum = bar_sum + jnp.sum(bar, axis=1, keepdims=True)
        total = total + holdings_matrix(bar, wide, rows, delta, gamma)
        both = held + fresh
        weight[:, cut] = jnp.where(flag, both / 2.0, fresh)
        weight_sum[:, cut] = jnp.where(flag, both / 2.0, both)
    given[0:256, :] = total[0:256, :]
    given[256:264, :] = jnp.concatenate(
        [total[256:258, :], share_rows(bar_sum), jnp.zeros((4, DEPTH), F32)], axis=0
    )


def partial_back(given, other, turned, sens, send, work):
    whole = given[...] + other[...]
    parts = matrix_parts(whole[0:256, :], whole[256:258, :])
    for hop in range(RING):
        cut = slice(HALF * hop, HALF * (hop + 1))
        curve, line = forms(parts, turned[:, cut])
        back = sens[0:1, cut] * line + sens[1:2, cut] * curve
        for part in range(8):
            spot = OWN * (8 * hop + part)
            work[spot : spot + OWN, :] = back[:, DEPTH * part : DEPTH * (part + 1)]
    work[LINES:SENT, :] = jnp.concatenate([count_row(whole[258:260, 0:1]), jnp.zeros((15, DEPTH), F32)], axis=0)
    rows = work[...].astype(BF16)
    for peer in range(GRID_Z):
        send[SENT * peer : SENT * (peer + 1), :] = rows


def sum_z(received, send):
    rows = received[0:SENT, :].astype(F32)
    for peer in range(1, GRID_Z):
        rows = rows + received[SENT * peer : SENT * (peer + 1), :].astype(F32)
    for peer in range(GRID_X):
        send[SENT * peer : SENT * (peer + 1), :] = rows


def second_primal(
    place, primal_step, restart_at, received, pack0, pack1, pack2, pack3,
    turned, sens, returns, weight, weight_sum, small, given, stat, work,
):
    y = place[0]
    primal = column(primal_step, y)
    first = column(restart_at, y) == 0
    flag = column(restart_at, y) == 1
    count = jnp.where(first, 2.0, 3.0)
    price = small[4:6, 0:1]
    total = jnp.zeros((OWN * DEPTH + 16, DEPTH), F32)
    bar_sum = jnp.zeros((OWN, 1), F32)
    sums = received[0:SENT, :]
    for peer in range(1, GRID_X):
        sums = sums + received[SENT * peer : SENT * (peer + 1), :]
    work[...] = sums
    stat[...] = jnp.broadcast_to(work[LINES : LINES + 1, :], (8, DEPTH))
    for hop, pack in enumerate((pack0, pack1, pack2, pack3)):
        cut = slice(HALF * hop, HALF * (hop + 1))
        lines = [work[16 * hop + OWN * part : 16 * hop + OWN * (part + 1), :] for part in range(8)]
        back = jnp.concatenate(lines, axis=1)
        wide = turned[:, cut].astype(F32)
        held = weight[:, cut]
        fresh = jnp.maximum(held + primal * (returns[:, cut] + back + price), 0.0)
        bar = 2.0 * fresh - held
        bar_sum = bar_sum + jnp.sum(bar, axis=1, keepdims=True)
        total = total + holdings_matrix(bar, wide, pack[0:HALF, :], sens[0:1, cut], sens[1:2, cut])
        last = jnp.where(flag, (weight_sum[:, cut] + fresh) / count, fresh)
        for part in range(8):
            spot = 264 + OWN * (8 * hop + part)
            given[spot : spot + OWN, :] = last[:, DEPTH * part : DEPTH * (part + 1)]
    given[0:256, :] = total[0:256, :]
    given[256:264, :] = jnp.concatenate(
        [total[256:258, :], share_rows(bar_sum), jnp.zeros((4, DEPTH), F32)], axis=0
    )


def joint(given, other):
    whole = given[0:264, :] + other[0:264, :]
    share = whole[258:260, 0:1] * (1.0 / TOTAL_INST)
    matrix = jnp.concatenate([whole[0:256, :], tail_rows(whole[256:258, :])], axis=0)
    return jnp.concatenate(split2(matrix * SCALE), axis=1), share


def first_dual(
    place, primal_step, dual_step, aversion, level_start, restart_at, given, other, shocks, turned, dual_start, stat,
    given_moment, dual, dual_sum, excess, excess_sum, small,
):
    y = place[0]
    primal, rate, averse = column(primal_step, y), column(dual_step, y), column(aversion, y)
    level = column(level_start, y)
    flag = column(restart_at, y) == 0
    parts, share = joint(given, other)
    level_new = level - primal * (averse - mass_of(stat))
    level_bar = 2.0 * level_new - level
    price_new = rate * (1.0 - share)

    def settle(old, new):
        both = old + new
        return jnp.where(flag, both / 2.0, new), jnp.where(flag, both / 2.0, both)

    def dual_of(cut):
        old = turn_to(dual_start[:, cut], y)[0:OWN, :]
        curve, line = forms(parts, turned[:, cut])
        loss = curve + line
        extra = jnp.maximum(0.0 - primal * (TAIL * averse - old), 0.0)
        fresh = jnp.maximum(old - rate * (2.0 * extra + level_bar + loss), 0.0)
        state, both = settle(old, fresh)
        dual[:, cut] = state
        dual_sum[:, cut] = both
        state_extra, both_extra = settle(jnp.zeros_like(extra), extra)
        excess[:, cut] = state_extra
        excess_sum[:, cut] = both_extra
        return state

    total, mass = moments(dual_of, shocks, lambda cut: turned[:, cut].astype(F32))
    pieces = settle(level, level_new) + settle(jnp.zeros_like(price_new), price_new)
    small[...] = jnp.concatenate([jnp.broadcast_to(piece, (OWN, DEPTH)) for piece in pieces], axis=0)
    given_moment[0:256, :] = total[0:256, :]
    given_moment[256:264, :] = jnp.concatenate(
        [total[256:258, :], share_rows(mass), jnp.zeros((4, DEPTH), F32)], axis=0
    )


def second_dual(
    place, primal_step, dual_step, aversion, restart_at, given, other, turned, dual, dual_sum, excess, excess_sum,
    small, stat, out0, out1, out2, out3,
):
    y, core = place[0], place[1]
    outs = (out0, out1, out2, out3)
    primal, rate, averse = column(primal_step, y), column(dual_step, y), column(aversion, y)
    flag = column(restart_at, y) == 1
    count = jnp.where(column(restart_at, y) == 0, 2.0, 3.0)
    parts, _ = joint(given, other)
    level = small[0:2, 0:1]
    level_new = level - primal * (averse - mass_of(stat))
    level_bar = 2.0 * level_new - level

    def settle(both, new):
        return jnp.where(flag, (both + new) / count, new)

    for step in range(NCHUNK):
        cut = slice(step * CHUNK, (step + 1) * CHUNK)
        old, old_extra = dual[:, cut], excess[:, cut]
        curve, line = forms(parts, turned[:, cut])
        loss = curve + line
        extra = jnp.maximum(old_extra - primal * (TAIL * averse - old), 0.0)
        fresh = jnp.maximum(old - rate * ((2.0 * extra - old_extra) + level_bar + loss), 0.0)
        last = settle(dual_sum[:, cut], fresh)
        last_extra = settle(excess_sum[:, cut], extra)
        for out in outs:
            out[:, cut] = last
            out[:, SCEN_DEV + step * CHUNK : SCEN_DEV + (step + 1) * CHUNK] = last_extra
    last_level = jnp.broadcast_to(settle(small[2:4, 0:1], level_new), (OWN, DEPTH))
    m = grid_iota((DEPTH, 256), 0)
    lane = grid_iota((DEPTH, 256), 1)
    source = (lane >> 5) * PIECE + (lane & 15)
    mine = ((lane >> 4) & 1) == core
    own_pick = jnp.where((m == source) & mine, 1.0, 0.0).astype(BF16)
    other_pick = jnp.where((m == source) & jnp.logical_not(mine), 1.0, 0.0).astype(BF16)
    own_parts, other_parts = split3(given[264:328, :]), split3(other[264:328, :])
    pieces = [dot(a, own_pick) + dot(b, other_pick) for a, b in zip(own_parts, other_parts)]
    held = pieces[0] + pieces[1] + pieces[2]
    for hop, out in enumerate(outs):
        out[:, 2 * SCEN_DEV + BLOCK :] = last_level
        for part in range(8):
            spot = OWN * (8 * hop + part)
            start = 2 * SCEN_DEV + 256 * part
            out[:, start : start + 256] = held[spot : spot + OWN, :]


def close_kernel(place, in0, in1, in2, in3, weights, duals, shortfall, threshold, work):
    y = place[0]
    for hop, taken in enumerate((in0, in1, in2, in3)):
        work[OWN * hop : OWN * (hop + 1), :] = taken[...]
    start = 0
    for out, width in ((duals, SCEN_DEV), (shortfall, SCEN_DEV), (weights, BLOCK)):
        for left in range(0, width, CHUNK):
            right = min(left + CHUNK, width)
            out[:, left:right] = turn_back(work[:, start + left : start + right], y)
        start += width
    levels = turn_back(work[:, start:], y)
    for spot in range(8):
        threshold[spot] = jnp.max(levels[spot : spot + 1, :])


def kernel(body, name, scalars, arrays, outs, scratch=(), left=0, limit=LIMIT):
    small = pl.BlockSpec(memory_space=pltpu.SMEM)
    large = pl.BlockSpec(memory_space=pltpu.VMEM)
    given = [pl.BlockSpec(memory_space=pltpu.HBM)] * left + [large] * (len(arrays) - left)
    call = pl.pallas_call(
        body,
        name=name,
        in_specs=[small] * len(scalars) + given,
        out_specs=[small if len(shape) == 1 else large for shape, _ in outs],
        out_shape=[jax.ShapeDtypeStruct(shape, dtype) for shape, dtype in outs],
        scratch_shapes=list(scratch),
        compiler_params=pltpu.CompilerParams(vmem_limit_bytes=limit),
    )
    return list(call(*scalars, *arrays))


def along(value, hop):
    return lax.ppermute(value, "y", [(i, (i + hop) % RING) for i in range(RING)])


def across(value):
    return lax.ppermute(value, "c", [(0, 1), (1, 0)])


def exchange(value, axes):
    return lax.all_to_all(value, axes, 0, 0, tiled=True)


def on_device(
    shocks, loadings, greeks, mean_return, weight_start, dual_start, level_start, aversion, primal_step, dual_step, restart_at,
):
    place = jnp.stack([lax.axis_index("y"), lax.axis_index("c")]).astype(jnp.int32)
    rows = OWN * DEPTH
    scen_rows = [((OWN, SCEN_DEV), F32)] * 4
    send, turned, chosen = kernel(
        open_kernel, "open", [place],
        [shocks, dual_start, loadings.T, greeks, weight_start, mean_return[None, :]],
        [((PEERS * FIRST, DEPTH), BF16), ((DEPTH, SCEN_DEV), BF16), ((24 * 16, DEPTH), F32)],
        [
            pltpu.VMEM((PEERS, FIRST, DEPTH), F32), pltpu.VMEM((SCEN_DEV, DEPTH), BF16), pltpu.VMEM((8, SCEN_DEV), F32),
            pltpu.VMEM((2 * PIECE, DEPTH), BF16), pltpu.VMEM((3, 2 * PIECE), BF16), pltpu.VMEM((8, BLOCK), F32),
            pltpu.VMEM((1, BLOCK), F32), pltpu.SemaphoreType.DMA((6,)),
        ],
        left=6,
        limit=56 * 1024 * 1024,
    )
    received = exchange(send, ("x", "z", "c"))
    spread, stat, *packs = kernel(
        sort_kernel, "sort", [], [received, chosen],
        [((rows, DEPTH), F32), ((8, DEPTH), F32)] + [((PACK, DEPTH), BF16)] * RING,
        [pltpu.VMEM((PEERS * FIRST, DEPTH), F32)],
    )
    packs = packs[:1] + [along(packs[hop], hop) for hop in range(1, RING)]
    moment = exchange(spread, ("x", "z", "c"))
    given, loads, sens, returns, weight, weight_sum = kernel(
        first_primal, "first_primal", [place, primal_step, restart_at], [moment, stat, *packs],
        [((264, DEPTH), F32), ((DEPTH, ALL), BF16), ((2, ALL), F32), ((1, ALL), F32), ((OWN, ALL), F32), ((OWN, ALL), F32)],
    )
    other = across(given)
    given, dual, dual_sum, excess, excess_sum, small = kernel(
        first_dual, "first_dual", [place, primal_step, dual_step, aversion, level_start, restart_at],
        [given, other, shocks, turned, dual_start, stat],
        [((264, DEPTH), F32)] + scen_rows + [((8, DEPTH), F32)],
    )
    other = across(given)
    (send,) = kernel(
        partial_back, "partial_back", [], [given, other, loads, sens], [((GRID_Z * SENT, DEPTH), BF16)],
        [pltpu.VMEM((SENT, DEPTH), F32)],
    )
    received = exchange(send, "z")
    (send,) = kernel(sum_z, "sum_z", [], [received], [((GRID_X * SENT, DEPTH), F32)])
    received = exchange(send, "x")
    given, stat = kernel(
        second_primal, "second_primal", [place, primal_step, restart_at],
        [received, *packs, loads, sens, returns, weight, weight_sum, small],
        [((328, DEPTH), F32), ((8, DEPTH), F32)], [pltpu.VMEM((SENT, DEPTH), F32)],
    )
    other = across(given)
    outs = kernel(
        second_dual, "second_dual", [place, primal_step, dual_step, aversion, restart_at],
        [given, other, turned, dual, dual_sum, excess, excess_sum, small, stat],
        [((OWN, 2 * SCEN_DEV + BLOCK + DEPTH), F32)] * RING,
    )
    taken = outs[:1] + [along(outs[hop], -hop) for hop in range(1, RING)]
    weights, duals, shortfall, threshold = kernel(
        close_kernel, "close", [place], taken,
        [((8, BLOCK), F32), ((8, SCEN_DEV), F32), ((8, SCEN_DEV), F32), ((8,), F32)],
        [pltpu.VMEM((8, 2 * SCEN_DEV + BLOCK + DEPTH), F32)],
    )
    return weights, duals, shortfall, threshold


def solution(mesh):
    grid = Mesh(np.asarray(mesh.devices).reshape(GRID_X, GRID_Z, CORES, RING), ("x", "z", "c", "y"))
    scen = ("x", "z", "c")
    placed = (
        P(scen, None),
        P(None, ("y",) + scen),
        P(None, ("y",) + scen),
        P("y"),
        P(None, "y"),
        P(None, scen),
        P(),
        P(),
        P(),
        P(),
        P(),
    )
    return jax.shard_map(
        on_device,
        mesh=grid,
        in_specs=placed,
        out_specs=(P(None, "y"), P(None, scen), P(None, scen), P()),
        check_vma=False,
    )
```

```python
import math

import jax
import jax.numpy as jnp
import numpy as np
from jax import lax
from jax.experimental import pallas as pl
from jax.experimental.pallas import tpu as pltpu
from jax.sharding import Mesh, PartitionSpec as P

F32 = jnp.float32
BF16 = jnp.bfloat16
DEPTH = 128
SCEN_DEV = 4096
GRID_X, GRID_Z, CORES = 4, 8, 2
PEERS = GRID_X * GRID_Z * CORES
RING = 4
OWN = 2
PIECE = 16
HALF = PEERS * PIECE
BLOCK = 2 * HALF
ALL = RING * HALF
TOTAL_SCEN = float(PEERS * SCEN_DEV)
TOTAL_INST = float(RING * BLOCK)
SCALE = 1.0 / math.sqrt(TOTAL_INST)
TAIL = 20.0
CHUNK = 512
NCHUNK = SCEN_DEV // CHUNK
FIRST = 24
LINES = OWN * ALL // DEPTH
SENT = LINES + 16
PACK = HALF + PEERS + 80
LIMIT = 48 * 1024 * 1024


def dot(a, b):
    return jnp.dot(a, b, preferred_element_type=F32)


def dot_nt(a, b):
    return lax.dot_general(a, b, (((1,), (1,)), ((), ())), preferred_element_type=F32)


def split2(value):
    high = value.astype(BF16)
    return high, (value - high.astype(F32)).astype(BF16)


def split3(value):
    high = value.astype(BF16)
    rest = value - high.astype(F32)
    middle = rest.astype(BF16)
    return high, middle, (rest - middle.astype(F32)).astype(BF16)


def grid_iota(shape, axis):
    return lax.broadcasted_iota(jnp.int32, shape, axis)


def identity(size):
    return jnp.where(grid_iota((size, size), 0) == grid_iota((size, size), 1), 1.0, 0.0).astype(BF16)


def column(ref, place):
    return jnp.where(grid_iota((OWN, 1), 0) == 0, ref[OWN * place], ref[OWN * place + 1])


def turn_to(rows, y):
    return pltpu.roll(rows, (8 - OWN * y) & 7, axis=0)


def turn_back(rows, y):
    return pltpu.roll(rows, (OWN * y) & 7, axis=0)


def count_row(mass):
    lane = grid_iota((1, DEPTH), 1)
    row = jnp.zeros((1, DEPTH), F32)
    for own in range(OWN):
        for part, value in enumerate(split3(mass[own : own + 1, :])):
            row = jnp.where(lane == 32 + 3 * own + part, value.astype(F32), row)
    return row


def mass_of(stat):
    first = stat[6:7, 32:33] + stat[6:7, 33:34] + stat[6:7, 34:35]
    second = stat[6:7, 35:36] + stat[6:7, 36:37] + stat[6:7, 37:38]
    return jnp.where(grid_iota((OWN, 1), 0) == 0, first, second)


def tail_rows(rows):
    return jnp.concatenate([rows, jnp.zeros((16 - OWN, rows.shape[1]), rows.dtype)], axis=0)


def moments(dual_of, shocks, turned):
    total = jnp.zeros((OWN * DEPTH + 16, DEPTH), F32)
    mass = jnp.zeros((OWN, 1), F32)
    for step in range(NCHUNK):
        cut = slice(step * CHUNK, (step + 1) * CHUNK)
        dual = dual_of(cut)
        rounded = dual.astype(BF16).astype(F32)
        wide = turned[:, cut].astype(F32)
        left = [(wide * rounded[own : own + 1, :]).astype(BF16) for own in range(OWN)]
        left = jnp.concatenate(left + [tail_rows(rounded).astype(BF16)], axis=0)
        total = total + dot(left, shocks[cut, :])
        mass = mass + jnp.sum(dual, axis=1, keepdims=True)
    return total * (1.0 / TOTAL_SCEN), mass * (1.0 / TOTAL_SCEN)


def open_kernel(shocks_in, dual_in, loadings_in, greeks_in, holdings_in, returns_in, *rest):
    send, turned, chosen, work, shocks, dual, loadings, greeks, holdings, returns, gates = rest
    y, core = lax.axis_index("y"), lax.axis_index("c")
    unit = identity(DEPTH)
    pairs = (
        (shocks_in, shocks), (dual_in, dual), (loadings_in, loadings), (greeks_in, greeks), (holdings_in, holdings),
        (returns_in, returns),
    )
    copies = [pltpu.make_async_copy(a, b, gates.at[n]) for n, (a, b) in enumerate(pairs)]
    for copy in copies:
        copy.start()
    for copy in copies[1:]:
        copy.wait()
    m = grid_iota((2 * DEPTH, DEPTH), 0)
    lane = grid_iota((2 * DEPTH, DEPTH), 1)
    pick = jnp.where(m == (lane >> 4) * 32 + core * PIECE + (lane & 15), 1.0, 0.0).astype(BF16)
    for part in range(BLOCK // 256):
        cut = slice(256 * part, 256 * (part + 1))
        both = jnp.concatenate(
            [turn_to(holdings[:, cut], y), returns[:, cut], jnp.zeros((7, 256), F32)], axis=0
        )
        for level, value in enumerate(split3(both)):
            chosen[16 * (8 * level + part) : 16 * (8 * level + part) + 16, :] = dot(value, pick)

    copies[0].wait()

    for step in range(NCHUNK):
        cut = slice(step * CHUNK, (step + 1) * CHUNK)
        turned[:, cut] = dot_nt(unit, shocks[cut, :]).astype(BF16)
    total, mass = moments(lambda cut: turn_to(dual[:, cut], y)[0:OWN, :], shocks, turned)
    rows = loadings[...].astype(F32)
    sens = greeks[...].astype(F32)
    delta, gamma = sens[0:1, :].astype(BF16), sens[1:2, :].astype(BF16)
    m = grid_iota((2 * PIECE, DEPTH), 0)
    lane = grid_iota((2 * PIECE, DEPTH), 1)
    tally = count_row(mass)
    notes = []
    for half in range(2):
        near = jnp.where((m == lane + PIECE * half) & (lane < PIECE), 1.0, 0.0).astype(BF16)
        far = jnp.where(
            (m == lane - PIECE + PIECE * half) & (lane >= PIECE) & (lane < 2 * PIECE), 1.0, 0.0
        ).astype(BF16)
        notes.append(dot(delta, near) + dot(gamma, far) + tally)
    blank = jnp.zeros((1, DEPTH), F32)
    for peer in range(PEERS):
        half = peer % 2
        work[peer, 0:16, :] = rows[PIECE * half : PIECE * (half + 1), :]
        work[peer, 16:20, :] = total[4 * peer : 4 * peer + 4, :]
        work[peer, 20:24, :] = jnp.concatenate([total[256:258, :], notes[half], blank], axis=0)
    send[...] = work[...].astype(BF16).reshape(PEERS * FIRST, DEPTH)


def sort_kernel(received, chosen, spread, stat, *rest):
    packs, work = rest[:RING], rest[RING]
    work[...] = received[...].astype(F32)
    whole = work[...].reshape(PEERS, FIRST, DEPTH)
    sums = jnp.sum(whole[:, 16:24, :], axis=0)
    stat[...] = sums
    spread[...] = jnp.broadcast_to(sums[0:4, :][None], (PEERS, 4, DEPTH)).reshape(PEERS * 4, DEPTH)
    rows = whole[:, 0:16, :].reshape(HALF, DEPTH).astype(BF16)
    notes = work[pl.ds(22, PEERS, stride=FIRST), :].astype(BF16)
    for hop in range(RING):
        pieces = [chosen[16 * n + OWN * hop : 16 * n + OWN * (hop + 1), :] for n in range(24)]
        pieces += [chosen[16 * n + 8 : 16 * n + 9, :] for n in range(24)]
        pieces.append(jnp.zeros((8, DEPTH), F32))
        packs[hop][0:HALF, :] = rows
        packs[hop][HALF : HALF + PEERS, :] = notes
        packs[hop][HALF + PEERS : PACK, :] = jnp.concatenate(pieces, axis=0).astype(BF16)


def matrix_parts(moment, linear):
    return jnp.concatenate(split2(jnp.concatenate([moment, tail_rows(linear)], axis=0)), axis=1)


def forms(parts, half):
    form = dot(parts, jnp.concatenate([half, half], axis=0))
    wide = half.astype(F32)
    curve = [
        jnp.sum(form[DEPTH * own : DEPTH * (own + 1), :] * wide, axis=0, keepdims=True)
        for own in range(OWN)
    ]
    return jnp.concatenate(curve, axis=0), form[OWN * DEPTH : OWN * DEPTH + OWN, :]


def holdings_matrix(bar, turned, rows, delta, gamma):
    rounded = bar.astype(BF16).astype(F32)
    curve = rounded * gamma
    left = [turned * curve[own : own + 1, :] for own in range(OWN)]
    left = jnp.concatenate(left + [tail_rows(rounded * delta)], axis=0)
    high, low = split2(left)
    return dot(high, rows) + dot(low, rows)


def share_rows(bar_sum):
    return jnp.broadcast_to(bar_sum, (OWN, DEPTH))


def first_primal(
    primal_step, restart_at, moment, stat, pack0, pack1, pack2, pack3,
    given, turned, sens, returns, weight, weight_sum,
):
    y = lax.axis_index("y")
    primal = column(primal_step, y)
    flag = column(restart_at, y) == 0
    parts = matrix_parts(moment[...], stat[4:6, :])
    unit = identity(DEPTH)
    total = jnp.zeros((OWN * DEPTH + 16, DEPTH), F32)
    bar_sum = jnp.zeros((OWN, 1), F32)
    row = grid_iota((PEERS, HALF), 0)
    col = grid_iota((PEERS, HALF), 1)
    mine = row == (col >> 4)
    m = grid_iota((DEPTH, HALF), 0)
    slot = grid_iota((DEPTH, HALF), 1) & 15
    near = jnp.where(m == slot, 1.0, 0.0).astype(BF16)
    far = jnp.where(m == slot + PIECE, 1.0, 0.0).astype(BF16)
    for hop, pack in enumerate((pack0, pack1, pack2, pack3)):
        cut = slice(HALF * hop, HALF * (hop + 1))
        rows = pack[0:HALF, :]
        notes = pack[HALF : HALF + PEERS, :]
        wide = dot_nt(unit, rows)
        half = wide.astype(BF16)
        turned[:, cut] = half
        delta = jnp.sum(jnp.where(mine, dot(notes, near), 0.0), axis=0, keepdims=True)
        gamma = 0.5 * jnp.sum(jnp.where(mine, dot(notes, far), 0.0), axis=0, keepdims=True)
        sens[0:1, cut] = delta
        sens[1:2, cut] = gamma
        more = pack[HALF + PEERS : PACK, :].astype(F32)
        held = [
            more[2 * n : 2 * n + 2, :] + more[2 * n + 16 : 2 * n + 18, :] + more[2 * n + 32 : 2 * n + 34, :]
            for n in range(8)
        ]
        gain = [
            more[48 + n : 49 + n, :] + more[56 + n : 57 + n, :] + more[64 + n : 65 + n, :]
            for n in range(8)
        ]
        held = jnp.concatenate(held, axis=1)
        gain = jnp.concatenate(gain, axis=1)
        returns[:, cut] = gain
        curve, line = forms(parts, half)
        fresh = jnp.maximum(held + primal * (gain + (delta * line + gamma * curve)), 0.0)
        bar = 2.0 * fresh - held
        bar_sum = bar_sum + jnp.sum(bar, axis=1, keepdims=True)
        total = total + holdings_matrix(bar, wide, rows, delta, gamma)
        both = held + fresh
        weight[:, cut] = jnp.where(flag, both / 2.0, fresh)
        weight_sum[:, cut] = jnp.where(flag, both / 2.0, both)
    given[0:256, :] = total[0:256, :]
    given[256:264, :] = jnp.concatenate(
        [total[256:258, :], share_rows(bar_sum), jnp.zeros((4, DEPTH), F32)], axis=0
    )


def partial_back(given, other, turned, sens, send, work):
    whole = given[...] + other[...]
    parts = matrix_parts(whole[0:256, :], whole[256:258, :])
    for hop in range(RING):
        cut = slice(HALF * hop, HALF * (hop + 1))
        curve, line = forms(parts, turned[:, cut])
        back = sens[0:1, cut] * line + sens[1:2, cut] * curve
        for part in range(8):
            spot = OWN * (8 * hop + part)
            work[spot : spot + OWN, :] = back[:, DEPTH * part : DEPTH * (part + 1)]
    work[LINES:SENT, :] = jnp.concatenate([count_row(whole[258:260, 0:1]), jnp.zeros((15, DEPTH), F32)], axis=0)
    rows = work[...].astype(BF16)
    for peer in range(GRID_Z):
        send[SENT * peer : SENT * (peer + 1), :] = rows


def sum_z(received, send):
    rows = received[0:SENT, :].astype(F32)
    for peer in range(1, GRID_Z):
        rows = rows + received[SENT * peer : SENT * (peer + 1), :].astype(F32)
    for peer in range(GRID_X):
        send[SENT * peer : SENT * (peer + 1), :] = rows


def second_primal(
    primal_step, restart_at, received, pack0, pack1, pack2, pack3,
    turned, sens, returns, weight, weight_sum, small, given, stat, work,
):
    y = lax.axis_index("y")
    primal = column(primal_step, y)
    first = column(restart_at, y) == 0
    flag = column(restart_at, y) == 1
    count = jnp.where(first, 2.0, 3.0)
    price = small[4:6, 0:1]
    total = jnp.zeros((OWN * DEPTH + 16, DEPTH), F32)
    bar_sum = jnp.zeros((OWN, 1), F32)
    sums = received[0:SENT, :]
    for peer in range(1, GRID_X):
        sums = sums + received[SENT * peer : SENT * (peer + 1), :]
    work[...] = sums
    stat[...] = jnp.broadcast_to(work[LINES : LINES + 1, :], (8, DEPTH))
    for hop, pack in enumerate((pack0, pack1, pack2, pack3)):
        cut = slice(HALF * hop, HALF * (hop + 1))
        lines = [work[16 * hop + OWN * part : 16 * hop + OWN * (part + 1), :] for part in range(8)]
        back = jnp.concatenate(lines, axis=1)
        wide = turned[:, cut].astype(F32)
        held = weight[:, cut]
        fresh = jnp.maximum(held + primal * (returns[:, cut] + back + price), 0.0)
        bar = 2.0 * fresh - held
        bar_sum = bar_sum + jnp.sum(bar, axis=1, keepdims=True)
        total = total + holdings_matrix(bar, wide, pack[0:HALF, :], sens[0:1, cut], sens[1:2, cut])
        last = jnp.where(flag, (weight_sum[:, cut] + fresh) / count, fresh)
        for part in range(8):
            spot = 264 + OWN * (8 * hop + part)
            given[spot : spot + OWN, :] = last[:, DEPTH * part : DEPTH * (part + 1)]
    given[0:256, :] = total[0:256, :]
    given[256:264, :] = jnp.concatenate(
        [total[256:258, :], share_rows(bar_sum), jnp.zeros((4, DEPTH), F32)], axis=0
    )


def joint(given, other):
    whole = given[0:264, :] + other[0:264, :]
    share = whole[258:260, 0:1] * (1.0 / TOTAL_INST)
    matrix = jnp.concatenate([whole[0:256, :], tail_rows(whole[256:258, :])], axis=0)
    return jnp.concatenate(split2(matrix * SCALE), axis=1), share


def first_dual(
    primal_step, dual_step, aversion, level_start, restart_at, given, other, shocks, turned, dual_start, stat,
    given_moment, dual, dual_sum, excess, excess_sum, small,
):
    y = lax.axis_index("y")
    primal, rate, averse = column(primal_step, y), column(dual_step, y), column(aversion, y)
    level = column(level_start, y)
    flag = column(restart_at, y) == 0
    parts, share = joint(given, other)
    level_new = level - primal * (averse - mass_of(stat))
    level_bar = 2.0 * level_new - level
    price_new = rate * (1.0 - share)

    def settle(old, new):
        both = old + new
        return jnp.where(flag, both / 2.0, new), jnp.where(flag, both / 2.0, both)

    def dual_of(cut):
        old = turn_to(dual_start[:, cut], y)[0:OWN, :]
        curve, line = forms(parts, turned[:, cut])
        loss = curve + line
        extra = jnp.maximum(0.0 - primal * (TAIL * averse - old), 0.0)
        fresh = jnp.maximum(old - rate * (2.0 * extra + level_bar + loss), 0.0)
        state, both = settle(old, fresh)
        dual[:, cut] = state
        dual_sum[:, cut] = both
        state_extra, both_extra = settle(jnp.zeros_like(extra), extra)
        excess[:, cut] = state_extra
        excess_sum[:, cut] = both_extra
        return state

    total, mass = moments(dual_of, shocks, turned)
    pieces = settle(level, level_new) + settle(jnp.zeros_like(price_new), price_new)
    small[...] = jnp.concatenate([jnp.broadcast_to(piece, (OWN, DEPTH)) for piece in pieces], axis=0)
    given_moment[0:256, :] = total[0:256, :]
    given_moment[256:264, :] = jnp.concatenate(
        [total[256:258, :], share_rows(mass), jnp.zeros((4, DEPTH), F32)], axis=0
    )


def second_dual(
    primal_step, dual_step, aversion, restart_at, given, other, turned, dual, dual_sum, excess, excess_sum,
    small, stat, out0, out1, out2, out3,
):
    y, core = lax.axis_index("y"), lax.axis_index("c")
    outs = (out0, out1, out2, out3)
    primal, rate, averse = column(primal_step, y), column(dual_step, y), column(aversion, y)
    flag = column(restart_at, y) == 1
    count = jnp.where(column(restart_at, y) == 0, 2.0, 3.0)
    parts, _ = joint(given, other)
    level = small[0:2, 0:1]
    level_new = level - primal * (averse - mass_of(stat))
    level_bar = 2.0 * level_new - level

    def settle(both, new):
        return jnp.where(flag, (both + new) / count, new)

    for step in range(NCHUNK):
        cut = slice(step * CHUNK, (step + 1) * CHUNK)
        old, old_extra = dual[:, cut], excess[:, cut]
        curve, line = forms(parts, turned[:, cut])
        loss = curve + line
        extra = jnp.maximum(old_extra - primal * (TAIL * averse - old), 0.0)
        fresh = jnp.maximum(old - rate * ((2.0 * extra - old_extra) + level_bar + loss), 0.0)
        last = settle(dual_sum[:, cut], fresh)
        last_extra = settle(excess_sum[:, cut], extra)
        for out in outs:
            out[:, cut] = last
            out[:, SCEN_DEV + step * CHUNK : SCEN_DEV + (step + 1) * CHUNK] = last_extra
    last_level = jnp.broadcast_to(settle(small[2:4, 0:1], level_new), (OWN, DEPTH))
    m = grid_iota((DEPTH, 256), 0)
    lane = grid_iota((DEPTH, 256), 1)
    source = (lane >> 5) * PIECE + (lane & 15)
    mine = ((lane >> 4) & 1) == core
    own_pick = jnp.where((m == source) & mine, 1.0, 0.0).astype(BF16)
    other_pick = jnp.where((m == source) & jnp.logical_not(mine), 1.0, 0.0).astype(BF16)
    own_parts, other_parts = split3(given[264:328, :]), split3(other[264:328, :])
    pieces = [dot(a, own_pick) + dot(b, other_pick) for a, b in zip(own_parts, other_parts)]
    held = pieces[0] + pieces[1] + pieces[2]
    for hop, out in enumerate(outs):
        out[:, 2 * SCEN_DEV + BLOCK :] = last_level
        for part in range(8):
            spot = OWN * (8 * hop + part)
            start = 2 * SCEN_DEV + 256 * part
            out[:, start : start + 256] = held[spot : spot + OWN, :]


def close_kernel(in0, in1, in2, in3, weights, duals, shortfall, threshold, work):
    y = lax.axis_index("y")
    for hop, taken in enumerate((in0, in1, in2, in3)):
        work[OWN * hop : OWN * (hop + 1), :] = taken[...]
    start = 0
    for out, width in ((duals, SCEN_DEV), (shortfall, SCEN_DEV), (weights, BLOCK)):
        for left in range(0, width, CHUNK):
            right = min(left + CHUNK, width)
            out[:, left:right] = turn_back(work[:, start + left : start + right], y)
        start += width
    levels = turn_back(work[:, start:], y)
    for spot in range(8):
        threshold[spot] = jnp.max(levels[spot : spot + 1, :])


def kernel(body, name, scalars, arrays, outs, scratch=(), left=0, limit=LIMIT):
    small = pl.BlockSpec(memory_space=pltpu.SMEM)
    large = pl.BlockSpec(memory_space=pltpu.VMEM)
    given = [pl.BlockSpec(memory_space=pltpu.HBM)] * left + [large] * (len(arrays) - left)
    call = pl.pallas_call(
        body,
        name=name,
        in_specs=[small] * len(scalars) + given,
        out_specs=[small if len(shape) == 1 else large for shape, _ in outs],
        out_shape=[jax.ShapeDtypeStruct(shape, dtype) for shape, dtype in outs],
        scratch_shapes=list(scratch),
        compiler_params=pltpu.CompilerParams(vmem_limit_bytes=limit),
    )
    return list(call(*scalars, *arrays))


def along(value, hop):
    return lax.ppermute(value, "y", [(i, (i + hop) % RING) for i in range(RING)])


def across(value):
    return lax.ppermute(value, "c", [(0, 1), (1, 0)])


def exchange(value, axes):
    return lax.all_to_all(value, axes, 0, 0, tiled=True)


def on_device(
    shocks, loadings, greeks, mean_return, weight_start, dual_start, level_start, aversion, primal_step, dual_step, restart_at,
):
    rows = OWN * DEPTH
    scen_rows = [((OWN, SCEN_DEV), F32)] * 4
    send, turned, chosen = kernel(
        open_kernel, "open", [],
        [shocks, dual_start, loadings.T, greeks, weight_start, mean_return[None, :]],
        [((PEERS * FIRST, DEPTH), BF16), ((DEPTH, SCEN_DEV), BF16), ((24 * 16, DEPTH), F32)],
        [
            pltpu.VMEM((PEERS, FIRST, DEPTH), F32), pltpu.VMEM((SCEN_DEV, DEPTH), BF16), pltpu.VMEM((8, SCEN_DEV), F32),
            pltpu.VMEM((2 * PIECE, DEPTH), BF16), pltpu.VMEM((3, 2 * PIECE), BF16), pltpu.VMEM((8, BLOCK), F32),
            pltpu.VMEM((1, BLOCK), F32), pltpu.SemaphoreType.DMA((6,)),
        ],
        left=6,
        limit=56 * 1024 * 1024,
    )
    received = exchange(send, ("x", "z", "c"))
    spread, stat, *packs = kernel(
        sort_kernel, "sort", [], [received, chosen],
        [((rows, DEPTH), F32), ((8, DEPTH), F32)] + [((PACK, DEPTH), BF16)] * RING,
        [pltpu.VMEM((PEERS * FIRST, DEPTH), F32)],
    )
    packs = packs[:1] + [along(packs[hop], hop) for hop in range(1, RING)]
    moment = exchange(spread, ("x", "z", "c"))
    given, loads, sens, returns, weight, weight_sum = kernel(
        first_primal, "first_primal", [primal_step, restart_at], [moment, stat, *packs],
        [((264, DEPTH), F32), ((DEPTH, ALL), BF16), ((2, ALL), F32), ((1, ALL), F32), ((OWN, ALL), F32), ((OWN, ALL), F32)],
    )
    other = across(given)
    given, dual, dual_sum, excess, excess_sum, small = kernel(
        first_dual, "first_dual", [primal_step, dual_step, aversion, level_start, restart_at],
        [given, other, shocks, turned, dual_start, stat],
        [((264, DEPTH), F32)] + scen_rows + [((8, DEPTH), F32)],
    )
    other = across(given)
    (send,) = kernel(
        partial_back, "partial_back", [], [given, other, loads, sens], [((GRID_Z * SENT, DEPTH), BF16)],
        [pltpu.VMEM((SENT, DEPTH), F32)],
    )
    received = exchange(send, "z")
    (send,) = kernel(sum_z, "sum_z", [], [received], [((GRID_X * SENT, DEPTH), F32)])
    received = exchange(send, "x")
    given, stat = kernel(
        second_primal, "second_primal", [primal_step, restart_at],
        [received, *packs, loads, sens, returns, weight, weight_sum, small],
        [((328, DEPTH), F32), ((8, DEPTH), F32)], [pltpu.VMEM((SENT, DEPTH), F32)],
    )
    other = across(given)
    outs = kernel(
        second_dual, "second_dual", [primal_step, dual_step, aversion, restart_at],
        [given, other, turned, dual, dual_sum, excess, excess_sum, small, stat],
        [((OWN, 2 * SCEN_DEV + BLOCK + DEPTH), F32)] * RING,
    )
    taken = outs[:1] + [along(outs[hop], -hop) for hop in range(1, RING)]
    weights, duals, shortfall, threshold = kernel(
        close_kernel, "close", [], taken,
        [((8, BLOCK), F32), ((8, SCEN_DEV), F32), ((8, SCEN_DEV), F32), ((8,), F32)],
        [pltpu.VMEM((8, 2 * SCEN_DEV + BLOCK + DEPTH), F32)],
    )
    return weights, duals, shortfall, threshold


def solution(mesh):
    grid = Mesh(np.asarray(mesh.devices).reshape(GRID_X, GRID_Z, CORES, RING), ("x", "z", "c", "y"))
    scen = ("x", "z", "c")
    placed = (
        P(scen, None),
        P(None, ("y",) + scen),
        P(None, ("y",) + scen),
        P("y"),
        P(None, "y"),
        P(None, scen),
        P(),
        P(),
        P(),
        P(),
        P(),
    )
    return jax.shard_map(
        on_device,
        mesh=grid,
        in_specs=placed,
        out_specs=(P(None, "y"), P(None, scen), P(None, scen), P()),
        check_vma=False,
    )
```

```python
import math

import jax
import jax.numpy as jnp
import numpy as np
from jax import lax
from jax.experimental import pallas as pl
from jax.experimental.pallas import tpu as pltpu
from jax.sharding import Mesh, PartitionSpec as P

F32 = jnp.float32
BF16 = jnp.bfloat16
DEPTH = 128
SCEN_DEV = 4096
GRID_X, GRID_Z, CORES = 4, 8, 2
CHIPS = GRID_X * GRID_Z
PEERS = CHIPS * CORES
RING = 4
OWN = 2
PIECE = 16
HALF = PEERS * PIECE
BLOCK = 2 * HALF
ALL = RING * HALF
TOTAL_SCEN = float(PEERS * SCEN_DEV)
TOTAL_INST = float(RING * BLOCK)
SCALE = 1.0 / math.sqrt(TOTAL_INST)
TAIL = 20.0
SETTINGS = ("primal", "rate", "averse", "level", "restart")
CHUNK = 512
NCHUNK = SCEN_DEV // CHUNK
FIRST = 24
LINES = OWN * ALL // DEPTH
SENT = LINES + 16
PACK = HALF + PEERS + 80
LIMIT = 48 * 1024 * 1024


def dot(a, b):
    return jnp.dot(a, b, preferred_element_type=F32)


def dot_nt(a, b):
    return lax.dot_general(a, b, (((1,), (1,)), ((), ())), preferred_element_type=F32)


def split2(value):
    high = value.astype(BF16)
    return high, (value - high.astype(F32)).astype(BF16)


def split3(value):
    high = value.astype(BF16)
    rest = value - high.astype(F32)
    middle = rest.astype(BF16)
    return high, middle, (rest - middle.astype(F32)).astype(BF16)


def grid_iota(shape, axis):
    return lax.broadcasted_iota(jnp.int32, shape, axis)


def identity(size):
    return jnp.where(grid_iota((size, size), 0) == grid_iota((size, size), 1), 1.0, 0.0).astype(BF16)


def column(settings, name):
    spot = OWN * SETTINGS.index(name)
    return settings[spot : spot + OWN, 0:1]


def turn_to(rows, y):
    return pltpu.roll(rows, (8 - OWN * y) & 7, axis=0)


def turn_back(rows, y):
    return pltpu.roll(rows, (OWN * y) & 7, axis=0)


def count_row(mass):
    lane = grid_iota((1, DEPTH), 1)
    row = jnp.zeros((1, DEPTH), F32)
    for own in range(OWN):
        for part, value in enumerate(split3(mass[own : own + 1, :])):
            row = jnp.where(lane == 32 + 3 * own + part, value.astype(F32), row)
    return row


def mass_of(stat):
    first = stat[6:7, 32:33] + stat[6:7, 33:34] + stat[6:7, 34:35]
    second = stat[6:7, 35:36] + stat[6:7, 36:37] + stat[6:7, 37:38]
    return jnp.where(grid_iota((OWN, 1), 0) == 0, first, second)


def tail_rows(rows):
    return jnp.concatenate([rows, jnp.zeros((16 - OWN, rows.shape[1]), rows.dtype)], axis=0)


def moments(dual_of, shocks, turned):
    total = jnp.zeros((OWN * DEPTH + 16, DEPTH), F32)
    mass = jnp.zeros((OWN, 1), F32)
    for step in range(NCHUNK):
        cut = slice(step * CHUNK, (step + 1) * CHUNK)
        dual = dual_of(cut)
        rounded = dual.astype(BF16).astype(F32)
        wide = turned[:, cut].astype(F32)
        left = [(wide * rounded[own : own + 1, :]).astype(BF16) for own in range(OWN)]
        left = jnp.concatenate(left + [tail_rows(rounded).astype(BF16)], axis=0)
        total = total + dot(left, shocks[cut, :])
        mass = mass + jnp.sum(dual, axis=1, keepdims=True)
    return total * (1.0 / TOTAL_SCEN), mass * (1.0 / TOTAL_SCEN)


def open_kernel(shocks_in, dual_in, loadings_in, greeks_in, holdings_in, returns_in, *rest):
    given, rest = rest[: len(SETTINGS)], rest[len(SETTINGS) :]
    send, turned, chosen, settings, work, shocks, dual, loadings, greeks, holdings, returns, *taken, gates = rest
    y, core = lax.axis_index("y"), lax.axis_index("c")
    unit = identity(DEPTH)
    pairs = (
        (shocks_in, shocks), (dual_in, dual), (loadings_in, loadings), (greeks_in, greeks), (holdings_in, holdings),
        (returns_in, returns), *zip(given, taken),
    )
    copies = [pltpu.make_async_copy(a, b, gates.at[n]) for n, (a, b) in enumerate(pairs)]
    for copy in copies:
        copy.start()
    for copy in copies[1:]:
        copy.wait()
    pair = grid_iota((OWN, DEPTH), 0)
    for n, ref in enumerate(taken):
        values = jnp.where(pair == 0, ref[OWN * y], ref[OWN * y + 1])
        settings[OWN * n : OWN * (n + 1), :] = values.astype(F32)
    m = grid_iota((2 * DEPTH, DEPTH), 0)
    lane = grid_iota((2 * DEPTH, DEPTH), 1)
    pick = jnp.where(m == (lane >> 4) * 32 + core * PIECE + (lane & 15), 1.0, 0.0).astype(BF16)
    for part in range(BLOCK // 256):
        cut = slice(256 * part, 256 * (part + 1))
        both = jnp.concatenate(
            [turn_to(holdings[:, cut], y), returns[:, cut], jnp.zeros((7, 256), F32)], axis=0
        )
        for level, value in enumerate(split3(both)):
            chosen[16 * (8 * level + part) : 16 * (8 * level + part) + 16, :] = dot(value, pick)

    copies[0].wait()

    for step in range(NCHUNK):
        cut = slice(step * CHUNK, (step + 1) * CHUNK)
        turned[:, cut] = dot_nt(unit, shocks[cut, :]).astype(BF16)
    total, mass = moments(lambda cut: turn_to(dual[:, cut], y)[0:OWN, :], shocks, turned)
    rows = loadings[...].astype(F32)
    sens = greeks[...].astype(F32)
    delta, gamma = sens[0:1, :].astype(BF16), sens[1:2, :].astype(BF16)
    m = grid_iota((2 * PIECE, DEPTH), 0)
    lane = grid_iota((2 * PIECE, DEPTH), 1)
    tally = count_row(mass)
    notes = []
    for half in range(2):
        near = jnp.where((m == lane + PIECE * half) & (lane < PIECE), 1.0, 0.0).astype(BF16)
        far = jnp.where(
            (m == lane - PIECE + PIECE * half) & (lane >= PIECE) & (lane < 2 * PIECE), 1.0, 0.0
        ).astype(BF16)
        notes.append(dot(delta, near) + dot(gamma, far) + tally)
    blank = jnp.zeros((1, DEPTH), F32)
    for peer in range(PEERS):
        half = peer % 2
        work[peer, 0:16, :] = rows[PIECE * half : PIECE * (half + 1), :]
        spot = DEPTH * half + 4 * (peer // 2)
        work[peer, 16:20, :] = total[spot : spot + 4, :]
        work[peer, 20:24, :] = jnp.concatenate([total[256:258, :], notes[half], blank], axis=0)
    send[...] = work[...].astype(BF16).reshape(PEERS * FIRST, DEPTH)


def sort_kernel(received, chosen, spread, stat, *rest):
    packs, work = rest[:RING], rest[RING]
    work[...] = received[...].astype(F32)
    whole = work[...].reshape(PEERS, FIRST, DEPTH)
    sums = jnp.sum(whole[:, 16:24, :], axis=0)
    stat[...] = sums
    spread[...] = jnp.broadcast_to(sums[0:4, :][None], (CHIPS, 4, DEPTH)).reshape(DEPTH, DEPTH)
    rows = whole[:, 0:16, :].reshape(HALF, DEPTH).astype(BF16)
    notes = work[pl.ds(22, PEERS, stride=FIRST), :].astype(BF16)
    for hop in range(RING):
        pieces = [chosen[16 * n + OWN * hop : 16 * n + OWN * (hop + 1), :] for n in range(24)]
        pieces += [chosen[16 * n + 8 : 16 * n + 9, :] for n in range(24)]
        pieces.append(jnp.zeros((8, DEPTH), F32))
        packs[hop][0:HALF, :] = rows
        packs[hop][HALF : HALF + PEERS, :] = notes
        packs[hop][HALF + PEERS : PACK, :] = jnp.concatenate(pieces, axis=0).astype(BF16)


def matrix_parts(moment, linear):
    return jnp.concatenate(split2(jnp.concatenate([moment, tail_rows(linear)], axis=0)), axis=1)


def forms(parts, half):
    form = dot(parts, jnp.concatenate([half, half], axis=0))
    wide = half.astype(F32)
    curve = [
        jnp.sum(form[DEPTH * own : DEPTH * (own + 1), :] * wide, axis=0, keepdims=True)
        for own in range(OWN)
    ]
    return jnp.concatenate(curve, axis=0), form[OWN * DEPTH : OWN * DEPTH + OWN, :]


def holdings_matrix(bar, turned, rows, delta, gamma):
    rounded = bar.astype(BF16).astype(F32)
    curve = rounded * gamma
    left = [turned * curve[own : own + 1, :] for own in range(OWN)]
    left = jnp.concatenate(left + [tail_rows(rounded * delta)], axis=0)
    high, low = split2(left)
    return dot(high, rows) + dot(low, rows)


def share_rows(bar_sum):
    return jnp.broadcast_to(bar_sum, (OWN, DEPTH))


def unpack_kernel(pack0, pack1, pack2, pack3, turned, sens, returns, start):
    unit = identity(DEPTH)
    row = grid_iota((PEERS, HALF), 0)
    col = grid_iota((PEERS, HALF), 1)
    mine = row == (col >> 4)
    m = grid_iota((DEPTH, HALF), 0)
    slot = grid_iota((DEPTH, HALF), 1) & 15
    near = jnp.where(m == slot, 1.0, 0.0).astype(BF16)
    far = jnp.where(m == slot + PIECE, 1.0, 0.0).astype(BF16)
    for hop, pack in enumerate((pack0, pack1, pack2, pack3)):
        cut = slice(HALF * hop, HALF * (hop + 1))
        turned[:, cut] = dot_nt(unit, pack[0:HALF, :]).astype(BF16)
        notes = pack[HALF : HALF + PEERS, :]
        sens[0:1, cut] = jnp.sum(jnp.where(mine, dot(notes, near), 0.0), axis=0, keepdims=True)
        sens[1:2, cut] = 0.5 * jnp.sum(jnp.where(mine, dot(notes, far), 0.0), axis=0, keepdims=True)
        more = pack[HALF + PEERS : PACK, :].astype(F32)
        held = [
            more[2 * n : 2 * n + 2, :] + more[2 * n + 16 : 2 * n + 18, :] + more[2 * n + 32 : 2 * n + 34, :]
            for n in range(8)
        ]
        gain = [
            more[48 + n : 49 + n, :] + more[56 + n : 57 + n, :] + more[64 + n : 65 + n, :]
            for n in range(8)
        ]
        start[:, cut] = jnp.concatenate(held, axis=1)
        returns[:, cut] = jnp.concatenate(gain, axis=1)


def first_primal(
    settings, moment, moment_other, stat, pack0, pack1, pack2, pack3, turned, sens, returns, start,
    given, weight, weight_sum,
):
    core = lax.axis_index("c")
    primal = column(settings, "primal")
    flag = column(settings, "restart") == 0.0
    mine, others = moment[...], moment_other[...]
    both = [jnp.where(core == 0, mine, others), jnp.where(core == 0, others, mine)]
    parts = matrix_parts(jnp.concatenate(both, axis=0), stat[4:6, :])
    total = jnp.zeros((OWN * DEPTH + 16, DEPTH), F32)
    bar_sum = jnp.zeros((OWN, 1), F32)
    for hop in range(RING):
        cut = slice(HALF * hop, HALF * (hop + 1))
        curve, line = forms(parts, turned[:, cut])
        weight[:, cut] = sens[0:1, cut] * line + sens[1:2, cut] * curve
    for hop, pack in enumerate((pack0, pack1, pack2, pack3)):
        cut = slice(HALF * hop, HALF * (hop + 1))
        held = start[:, cut]
        fresh = jnp.maximum(held + primal * (returns[:, cut] + weight[:, cut]), 0.0)
        bar = 2.0 * fresh - held
        bar_sum = bar_sum + jnp.sum(bar, axis=1, keepdims=True)
        wide = turned[:, cut].astype(F32)
        total = total + holdings_matrix(bar, wide, pack[0:HALF, :], sens[0:1, cut], sens[1:2, cut])
        both = held + fresh
        weight[:, cut] = jnp.where(flag, both / 2.0, fresh)
        weight_sum[:, cut] = jnp.where(flag, both / 2.0, both)
    given[0:256, :] = total[0:256, :]
    given[256:264, :] = jnp.concatenate(
        [total[256:258, :], share_rows(bar_sum), jnp.zeros((4, DEPTH), F32)], axis=0
    )


def partial_back(given, other, turned, sens, send, work):
    whole = given[...] + other[...]
    parts = matrix_parts(whole[0:256, :], whole[256:258, :])
    for hop in range(RING):
        cut = slice(HALF * hop, HALF * (hop + 1))
        curve, line = forms(parts, turned[:, cut])
        back = sens[0:1, cut] * line + sens[1:2, cut] * curve
        for part in range(8):
            spot = OWN * (8 * hop + part)
            work[spot : spot + OWN, :] = back[:, DEPTH * part : DEPTH * (part + 1)]
    work[LINES:SENT, :] = jnp.concatenate([count_row(whole[258:260, 0:1]), jnp.zeros((15, DEPTH), F32)], axis=0)
    rows = work[...].astype(BF16)
    for peer in range(GRID_Z):
        send[SENT * peer : SENT * (peer + 1), :] = rows


def sum_z(received, send):
    rows = received[0:SENT, :].astype(F32)
    for peer in range(1, GRID_Z):
        rows = rows + received[SENT * peer : SENT * (peer + 1), :].astype(F32)
    for peer in range(GRID_X):
        send[SENT * peer : SENT * (peer + 1), :] = rows


def second_primal(
    settings, received, pack0, pack1, pack2, pack3,
    turned, sens, returns, weight, weight_sum, small, given, stat, work,
):
    primal, restart = column(settings, "primal"), column(settings, "restart")
    first, flag = restart == 0.0, restart == 1.0
    count = jnp.where(first, 2.0, 3.0)
    price = small[4:6, 0:1]
    total = jnp.zeros((OWN * DEPTH + 16, DEPTH), F32)
    bar_sum = jnp.zeros((OWN, 1), F32)
    sums = received[0:SENT, :]
    for peer in range(1, GRID_X):
        sums = sums + received[SENT * peer : SENT * (peer + 1), :]
    work[...] = sums
    stat[...] = jnp.broadcast_to(work[LINES : LINES + 1, :], (8, DEPTH))
    for hop, pack in enumerate((pack0, pack1, pack2, pack3)):
        cut = slice(HALF * hop, HALF * (hop + 1))
        lines = [work[16 * hop + OWN * part : 16 * hop + OWN * (part + 1), :] for part in range(8)]
        back = jnp.concatenate(lines, axis=1)
        wide = turned[:, cut].astype(F32)
        held = weight[:, cut]
        fresh = jnp.maximum(held + primal * (returns[:, cut] + back + price), 0.0)
        bar = 2.0 * fresh - held
        bar_sum = bar_sum + jnp.sum(bar, axis=1, keepdims=True)
        total = total + holdings_matrix(bar, wide, pack[0:HALF, :], sens[0:1, cut], sens[1:2, cut])
        last = jnp.where(flag, (weight_sum[:, cut] + fresh) / count, fresh)
        for part in range(8):
            spot = 264 + OWN * (8 * hop + part)
            given[spot : spot + OWN, :] = last[:, DEPTH * part : DEPTH * (part + 1)]
    given[0:256, :] = total[0:256, :]
    given[256:264, :] = jnp.concatenate(
        [total[256:258, :], share_rows(bar_sum), jnp.zeros((4, DEPTH), F32)], axis=0
    )


def joint(given, other):
    whole = given[0:264, :] + other[0:264, :]
    share = whole[258:260, 0:1] * (1.0 / TOTAL_INST)
    matrix = jnp.concatenate([whole[0:256, :], tail_rows(whole[256:258, :])], axis=0)
    return jnp.concatenate(split2(matrix * SCALE), axis=1), share


def first_dual(
    settings, given, other, shocks, turned, dual_start, stat,
    given_moment, dual, dual_sum, excess, excess_sum, small,
):
    y = lax.axis_index("y")
    primal, rate, averse, level, restart = (column(settings, name) for name in SETTINGS)
    flag = restart == 0.0
    parts, share = joint(given, other)
    level_new = level - primal * (averse - mass_of(stat))
    level_bar = 2.0 * level_new - level
    price_new = rate * (1.0 - share)

    def settle(old, new):
        both = old + new
        return jnp.where(flag, both / 2.0, new), jnp.where(flag, both / 2.0, both)

    def dual_of(cut):
        old = turn_to(dual_start[:, cut], y)[0:OWN, :]
        curve, line = forms(parts, turned[:, cut])
        loss = curve + line
        extra = jnp.maximum(0.0 - primal * (TAIL * averse - old), 0.0)
        fresh = jnp.maximum(old - rate * (2.0 * extra + level_bar + loss), 0.0)
        state, both = settle(old, fresh)
        dual[:, cut] = state
        dual_sum[:, cut] = both
        state_extra, both_extra = settle(jnp.zeros_like(extra), extra)
        excess[:, cut] = state_extra
        excess_sum[:, cut] = both_extra
        return state

    total, mass = moments(dual_of, shocks, turned)
    pieces = settle(level, level_new) + settle(jnp.zeros_like(price_new), price_new)
    small[...] = jnp.concatenate([jnp.broadcast_to(piece, (OWN, DEPTH)) for piece in pieces], axis=0)
    given_moment[0:256, :] = total[0:256, :]
    given_moment[256:264, :] = jnp.concatenate(
        [total[256:258, :], share_rows(mass), jnp.zeros((4, DEPTH), F32)], axis=0
    )


def second_dual(
    settings, given, other, turned, dual, dual_sum, excess, excess_sum,
    small, stat, out0, out1, out2, out3,
):
    core = lax.axis_index("c")
    outs = (out0, out1, out2, out3)
    primal, rate, averse, _, restart = (column(settings, name) for name in SETTINGS)
    flag = restart == 1.0
    count = jnp.where(restart == 0.0, 2.0, 3.0)
    parts, _ = joint(given, other)
    level = small[0:2, 0:1]
    level_new = level - primal * (averse - mass_of(stat))
    level_bar = 2.0 * level_new - level

    def settle(both, new):
        return jnp.where(flag, (both + new) / count, new)

    for step in range(NCHUNK):
        cut = slice(step * CHUNK, (step + 1) * CHUNK)
        old, old_extra = dual[:, cut], excess[:, cut]
        curve, line = forms(parts, turned[:, cut])
        loss = curve + line
        extra = jnp.maximum(old_extra - primal * (TAIL * averse - old), 0.0)
        fresh = jnp.maximum(old - rate * ((2.0 * extra - old_extra) + level_bar + loss), 0.0)
        last = settle(dual_sum[:, cut], fresh)
        last_extra = settle(excess_sum[:, cut], extra)
        for out in outs:
            out[:, cut] = last
            out[:, SCEN_DEV + step * CHUNK : SCEN_DEV + (step + 1) * CHUNK] = last_extra
    last_level = jnp.broadcast_to(settle(small[2:4, 0:1], level_new), (OWN, DEPTH))
    m = grid_iota((DEPTH, 256), 0)
    lane = grid_iota((DEPTH, 256), 1)
    source = (lane >> 5) * PIECE + (lane & 15)
    mine = ((lane >> 4) & 1) == core
    own_pick = jnp.where((m == source) & mine, 1.0, 0.0).astype(BF16)
    other_pick = jnp.where((m == source) & jnp.logical_not(mine), 1.0, 0.0).astype(BF16)
    own_parts, other_parts = split3(given[264:328, :]), split3(other[264:328, :])
    pieces = [dot(a, own_pick) + dot(b, other_pick) for a, b in zip(own_parts, other_parts)]
    held = pieces[0] + pieces[1] + pieces[2]
    for hop, out in enumerate(outs):
        out[:, 2 * SCEN_DEV + BLOCK :] = last_level
        for part in range(8):
            spot = OWN * (8 * hop + part)
            start = 2 * SCEN_DEV + 256 * part
            out[:, start : start + 256] = held[spot : spot + OWN, :]


def close_kernel(in0, in1, in2, in3, weights, duals, shortfall, threshold, work):
    y = lax.axis_index("y")
    for hop, taken in enumerate((in0, in1, in2, in3)):
        work[OWN * hop : OWN * (hop + 1), :] = taken[...]
    start = 0
    for out, width in ((duals, SCEN_DEV), (shortfall, SCEN_DEV), (weights, BLOCK)):
        for left in range(0, width, CHUNK):
            right = min(left + CHUNK, width)
            out[:, left:right] = turn_back(work[:, start + left : start + right], y)
        start += width
    levels = turn_back(work[:, start:], y)
    for spot in range(8):
        threshold[spot] = jnp.max(levels[spot : spot + 1, :])


def kernel(body, name, arrays, outs, scratch=(), left=0, limit=LIMIT):
    small = pl.BlockSpec(memory_space=pltpu.SMEM)
    large = pl.BlockSpec(memory_space=pltpu.VMEM)
    given = [pl.BlockSpec(memory_space=pltpu.HBM)] * left + [large] * (len(arrays) - left)
    call = pl.pallas_call(
        body,
        name=name,
        in_specs=given,
        out_specs=[small if len(shape) == 1 else large for shape, _ in outs],
        out_shape=[jax.ShapeDtypeStruct(shape, dtype) for shape, dtype in outs],
        scratch_shapes=list(scratch),
        compiler_params=pltpu.CompilerParams(vmem_limit_bytes=limit),
    )
    return list(call(*arrays))


def along(value, hop):
    return lax.ppermute(value, "y", [(i, (i + hop) % RING) for i in range(RING)])


def across(value):
    return lax.ppermute(value, "c", [(0, 1), (1, 0)])


def exchange(value, axes):
    return lax.all_to_all(value, axes, 0, 0, tiled=True)


def on_device(
    shocks, loadings, greeks, mean_return, weight_start, dual_start, level_start, aversion, primal_step, dual_step, restart_at,
):
    scen_rows = [((OWN, SCEN_DEV), F32)] * 4
    send, turned, chosen, settings = kernel(
        open_kernel, "open",
        [
            shocks, dual_start, loadings.T, greeks, weight_start, mean_return[None, :],
            primal_step, dual_step, aversion, level_start, restart_at,
        ],
        [((PEERS * FIRST, DEPTH), BF16), ((DEPTH, SCEN_DEV), BF16), ((24 * 16, DEPTH), F32), ((16, DEPTH), F32)],
        [
            pltpu.VMEM((PEERS, FIRST, DEPTH), F32), pltpu.VMEM((SCEN_DEV, DEPTH), BF16), pltpu.VMEM((8, SCEN_DEV), F32),
            pltpu.VMEM((2 * PIECE, DEPTH), BF16), pltpu.VMEM((3, 2 * PIECE), BF16), pltpu.VMEM((8, BLOCK), F32),
            pltpu.VMEM((1, BLOCK), F32), *[pltpu.SMEM((8,), F32)] * 4, pltpu.SMEM((8,), jnp.int32),
            pltpu.SemaphoreType.DMA((11,)),
        ],
        left=11,
        limit=56 * 1024 * 1024,
    )
    received = exchange(send, ("x", "z", "c"))
    spread, stat, *packs = kernel(
        sort_kernel, "sort", [received, chosen],
        [((DEPTH, DEPTH), F32), ((8, DEPTH), F32)] + [((PACK, DEPTH), BF16)] * RING,
        [pltpu.VMEM((PEERS * FIRST, DEPTH), F32)],
    )
    packs = packs[:1] + [along(packs[hop], hop) for hop in range(1, RING)]
    moment = exchange(spread, ("x", "z"))
    moment_other = across(moment)
    loads, sens, returns, start = kernel(
        unpack_kernel, "unpack", packs, [((DEPTH, ALL), BF16), ((2, ALL), F32), ((1, ALL), F32), ((OWN, ALL), F32)]
    )
    given, weight, weight_sum = kernel(
        first_primal, "first_primal",
        [settings, moment, moment_other, stat, *packs, loads, sens, returns, start],
        [((264, DEPTH), F32), ((OWN, ALL), F32), ((OWN, ALL), F32)],
    )
    other = across(given)
    given, dual, dual_sum, excess, excess_sum, small = kernel(
        first_dual, "first_dual",
        [settings, given, other, shocks, turned, dual_start, stat],
        [((264, DEPTH), F32)] + scen_rows + [((8, DEPTH), F32)],
    )
    other = across(given)
    (send,) = kernel(
        partial_back, "partial_back", [given, other, loads, sens], [((GRID_Z * SENT, DEPTH), BF16)],
        [pltpu.VMEM((SENT, DEPTH), F32)],
    )
    received = exchange(send, "z")
    (send,) = kernel(sum_z, "sum_z", [received], [((GRID_X * SENT, DEPTH), F32)])
    received = exchange(send, "x")
    given, stat = kernel(
        second_primal, "second_primal",
        [settings, received, *packs, loads, sens, returns, weight, weight_sum, small],
        [((328, DEPTH), F32), ((8, DEPTH), F32)], [pltpu.VMEM((SENT, DEPTH), F32)],
    )
    other = across(given)
    outs = kernel(
        second_dual, "second_dual",
        [settings, given, other, turned, dual, dual_sum, excess, excess_sum, small, stat],
        [((OWN, 2 * SCEN_DEV + BLOCK + DEPTH), F32)] * RING,
    )
    taken = outs[:1] + [along(outs[hop], -hop) for hop in range(1, RING)]
    weights, duals, shortfall, threshold = kernel(
        close_kernel, "close", taken,
        [((8, BLOCK), F32), ((8, SCEN_DEV), F32), ((8, SCEN_DEV), F32), ((8,), F32)],
        [pltpu.VMEM((8, 2 * SCEN_DEV + BLOCK + DEPTH), F32)],
    )
    return weights, duals, shortfall, threshold


def solution(mesh):
    grid = Mesh(np.asarray(mesh.devices).reshape(GRID_X, GRID_Z, CORES, RING), ("x", "z", "c", "y"))
    scen = ("x", "z", "c")
    placed = (
        P(scen, None),
        P(None, ("y",) + scen),
        P(None, ("y",) + scen),
        P("y"),
        P(None, "y"),
        P(None, scen),
        P(),
        P(),
        P(),
        P(),
        P(),
    )
    return jax.shard_map(
        on_device,
        mesh=grid,
        in_specs=placed,
        out_specs=(P(None, "y"), P(None, scen), P(None, scen), P()),
        check_vma=False,
    )
```

```python
import math

import jax
import jax.numpy as jnp
import numpy as np
from jax import lax
from jax.experimental import pallas as pl
from jax.experimental.pallas import tpu as pltpu
from jax.sharding import Mesh, PartitionSpec as P

F32 = jnp.float32
BF16 = jnp.bfloat16
DEPTH = 128
SCEN_DEV = 4096
GRID_X, GRID_Z, CORES = 4, 8, 2
CHIPS = GRID_X * GRID_Z
PEERS = CHIPS * CORES
RING = 4
OWN = 2
PIECE = 16
HALF = PEERS * PIECE
BLOCK = 2 * HALF
ALL = RING * HALF
TOTAL_SCEN = float(PEERS * SCEN_DEV)
TOTAL_INST = float(RING * BLOCK)
SCALE = 1.0 / math.sqrt(TOTAL_INST)
SPLIT = 4
CHOSEN = 24 * 16
TAIL = 20.0
SETTINGS = ("primal", "rate", "averse", "level", "restart")
CHUNK = 512
NCHUNK = SCEN_DEV // CHUNK
FIRST = 24
LINES = OWN * ALL // DEPTH
SENT = LINES + 16
PACK = HALF + PEERS + 80
LIMIT = 48 * 1024 * 1024


def dot(a, b):
    return jnp.dot(a, b, preferred_element_type=F32)


def dot_nt(a, b):
    return lax.dot_general(a, b, (((1,), (1,)), ((), ())), preferred_element_type=F32)


def split2(value):
    high = value.astype(BF16)
    return high, (value - high.astype(F32)).astype(BF16)


def split3(value):
    high = value.astype(BF16)
    rest = value - high.astype(F32)
    middle = rest.astype(BF16)
    return high, middle, (rest - middle.astype(F32)).astype(BF16)


def grid_iota(shape, axis):
    return lax.broadcasted_iota(jnp.int32, shape, axis)


def identity(size):
    return jnp.where(grid_iota((size, size), 0) == grid_iota((size, size), 1), 1.0, 0.0).astype(BF16)


def column(settings, name):
    spot = OWN * SETTINGS.index(name)
    return settings[spot : spot + OWN, 0:1]


def turn_to(rows, y):
    return pltpu.roll(rows, (8 - OWN * y) & 7, axis=0)


def turn_back(rows, y):
    return pltpu.roll(rows, (OWN * y) & 7, axis=0)


def count_row(mass):
    lane = grid_iota((1, DEPTH), 1)
    row = jnp.zeros((1, DEPTH), F32)
    for own in range(OWN):
        for part, value in enumerate(split3(mass[own : own + 1, :])):
            row = jnp.where(lane == 32 + 3 * own + part, value.astype(F32), row)
    return row


def mass_of(stat):
    first = stat[6:7, 32:33] + stat[6:7, 33:34] + stat[6:7, 34:35]
    second = stat[6:7, 35:36] + stat[6:7, 36:37] + stat[6:7, 37:38]
    return jnp.where(grid_iota((OWN, 1), 0) == 0, first, second)


def tail_rows(rows):
    return jnp.concatenate([rows, jnp.zeros((16 - OWN, rows.shape[1]), rows.dtype)], axis=0)


def moments(dual_of, shocks, turned):
    total = jnp.zeros((OWN * DEPTH + 16, DEPTH), F32)
    mass = jnp.zeros((OWN, 1), F32)
    for step in range(NCHUNK):
        cut = slice(step * CHUNK, (step + 1) * CHUNK)
        dual = dual_of(cut)
        rounded = dual.astype(BF16).astype(F32)
        wide = turned[:, cut].astype(F32)
        left = [(wide * rounded[own : own + 1, :]).astype(BF16) for own in range(OWN)]
        left = jnp.concatenate(left + [tail_rows(rounded).astype(BF16)], axis=0)
        total = total + dot(left, shocks[cut, :])
        mass = mass + jnp.sum(dual, axis=1, keepdims=True)
    return total * (1.0 / TOTAL_SCEN), mass * (1.0 / TOTAL_SCEN)


def open_kernel(shocks_in, dual_in, loadings_in, greeks_in, holdings_in, returns_in, *rest):
    given, rest = rest[: len(SETTINGS)], rest[len(SETTINGS) :]
    send, turned, chosen, work, shocks, dual, loadings, greeks, holdings, returns, *taken, gates = rest
    y, core = lax.axis_index("y"), lax.axis_index("c")
    unit = identity(DEPTH)
    pairs = [
        (dual_in, dual), (loadings_in, loadings), (greeks_in, greeks), (holdings_in, holdings), (returns_in, returns),
        *zip(given, taken),
    ]
    for n in range(SPLIT):
        cut = pl.ds(SCEN_DEV // SPLIT * n, SCEN_DEV // SPLIT)
        pairs.append((shocks_in.at[cut, :], shocks.at[cut, :]))
    copies = [pltpu.make_async_copy(a, b, gates.at[n]) for n, (a, b) in enumerate(pairs)]
    for copy in copies:
        copy.start()
    for copy in copies[:-SPLIT]:
        copy.wait()
    pair = grid_iota((OWN, DEPTH), 0)
    for n, ref in enumerate(taken):
        values = jnp.where(pair == 0, ref[OWN * y], ref[OWN * y + 1])
        chosen[CHOSEN + OWN * n : CHOSEN + OWN * (n + 1), :] = values.astype(F32)
    m = grid_iota((2 * DEPTH, DEPTH), 0)
    lane = grid_iota((2 * DEPTH, DEPTH), 1)
    pick = jnp.where(m == (lane >> 4) * 32 + core * PIECE + (lane & 15), 1.0, 0.0).astype(BF16)
    for part in range(BLOCK // 256):
        cut = slice(256 * part, 256 * (part + 1))
        both = jnp.concatenate(
            [turn_to(holdings[:, cut], y), returns[:, cut], jnp.zeros((7, 256), F32)], axis=0
        )
        for level, value in enumerate(split3(both)):
            chosen[16 * (8 * level + part) : 16 * (8 * level + part) + 16, :] = dot(value, pick)

    for copy in copies[-SPLIT:]:
        copy.wait()

    for step in range(NCHUNK):
        cut = slice(step * CHUNK, (step + 1) * CHUNK)
        turned[:, cut] = dot_nt(unit, shocks[cut, :]).astype(BF16)
    total, mass = moments(lambda cut: turn_to(dual[:, cut], y)[0:OWN, :], shocks, turned)
    rows = loadings[...].astype(F32)
    sens = greeks[...].astype(F32)
    delta, gamma = sens[0:1, :].astype(BF16), sens[1:2, :].astype(BF16)
    m = grid_iota((2 * PIECE, DEPTH), 0)
    lane = grid_iota((2 * PIECE, DEPTH), 1)
    tally = count_row(mass)
    notes = []
    for half in range(2):
        near = jnp.where((m == lane + PIECE * half) & (lane < PIECE), 1.0, 0.0).astype(BF16)
        far = jnp.where(
            (m == lane - PIECE + PIECE * half) & (lane >= PIECE) & (lane < 2 * PIECE), 1.0, 0.0
        ).astype(BF16)
        notes.append(dot(delta, near) + dot(gamma, far) + tally)
    blank = jnp.zeros((1, DEPTH), F32)
    for peer in range(PEERS):
        half = peer % 2
        work[peer, 0:16, :] = rows[PIECE * half : PIECE * (half + 1), :]
        spot = DEPTH * half + 4 * (peer // 2)
        work[peer, 16:20, :] = total[spot : spot + 4, :]
        work[peer, 20:24, :] = jnp.concatenate([total[256:258, :], notes[half], blank], axis=0)
    send[...] = work[...].astype(BF16).reshape(PEERS * FIRST, DEPTH)


def sort_kernel(received, chosen, spread, stat, settings, *rest):
    settings[...] = chosen[CHOSEN:, :]
    packs, work = rest[:RING], rest[RING]
    work[...] = received[...].astype(F32)
    whole = work[...].reshape(PEERS, FIRST, DEPTH)
    sums = jnp.sum(whole[:, 16:24, :], axis=0)
    stat[...] = sums
    spread[...] = jnp.broadcast_to(sums[0:4, :][None], (CHIPS, 4, DEPTH)).reshape(DEPTH, DEPTH)
    rows = whole[:, 0:16, :].reshape(HALF, DEPTH).astype(BF16)
    notes = work[pl.ds(22, PEERS, stride=FIRST), :].astype(BF16)
    for hop in range(RING):
        pieces = [chosen[16 * n + OWN * hop : 16 * n + OWN * (hop + 1), :] for n in range(24)]
        pieces += [chosen[16 * n + 8 : 16 * n + 9, :] for n in range(24)]
        pieces.append(jnp.zeros((8, DEPTH), F32))
        packs[hop][0:HALF, :] = rows
        packs[hop][HALF : HALF + PEERS, :] = notes
        packs[hop][HALF + PEERS : PACK, :] = jnp.concatenate(pieces, axis=0).astype(BF16)


def matrix_parts(moment, linear):
    return jnp.concatenate(split2(jnp.concatenate([moment, tail_rows(linear)], axis=0)), axis=1)


def forms(parts, half):
    form = dot(parts, jnp.concatenate([half, half], axis=0))
    wide = half.astype(F32)
    curve = [
        jnp.sum(form[DEPTH * own : DEPTH * (own + 1), :] * wide, axis=0, keepdims=True)
        for own in range(OWN)
    ]
    return jnp.concatenate(curve, axis=0), form[OWN * DEPTH : OWN * DEPTH + OWN, :]


def holdings_matrix(bar, turned, rows, delta, gamma, stacked):
    rounded = bar.astype(BF16).astype(F32)
    curve = rounded * gamma
    left = [turned * curve[own : own + 1, :] for own in range(OWN)]
    left = jnp.concatenate(left + [tail_rows(rounded * delta)], axis=0)
    high, low = split2(left)
    if not stacked:
        return dot(high, rows) + dot(low, rows)
    both = dot(jnp.concatenate([high, low], axis=0), rows)
    half = OWN * DEPTH + 16
    return both[0:half, :] + both[half : 2 * half, :]


def share_rows(bar_sum):
    return jnp.broadcast_to(bar_sum, (OWN, DEPTH))


def unpack_kernel(pack0, pack1, pack2, pack3, turned, sens, returns, start):
    unit = identity(DEPTH)
    row = grid_iota((PEERS, HALF), 0)
    col = grid_iota((PEERS, HALF), 1)
    mine = row == (col >> 4)
    m = grid_iota((DEPTH, HALF), 0)
    slot = grid_iota((DEPTH, HALF), 1) & 15
    near = jnp.where(m == slot, 1.0, 0.0).astype(BF16)
    far = jnp.where(m == slot + PIECE, 1.0, 0.0).astype(BF16)
    for hop, pack in enumerate((pack0, pack1, pack2, pack3)):
        cut = slice(HALF * hop, HALF * (hop + 1))
        turned[:, cut] = dot_nt(unit, pack[0:HALF, :]).astype(BF16)
        notes = pack[HALF : HALF + PEERS, :]
        sens[0:1, cut] = jnp.sum(jnp.where(mine, dot(notes, near), 0.0), axis=0, keepdims=True)
        sens[1:2, cut] = 0.5 * jnp.sum(jnp.where(mine, dot(notes, far), 0.0), axis=0, keepdims=True)
        more = pack[HALF + PEERS : PACK, :].astype(F32)
        held = [
            more[2 * n : 2 * n + 2, :] + more[2 * n + 16 : 2 * n + 18, :] + more[2 * n + 32 : 2 * n + 34, :]
            for n in range(8)
        ]
        gain = [
            more[48 + n : 49 + n, :] + more[56 + n : 57 + n, :] + more[64 + n : 65 + n, :]
            for n in range(8)
        ]
        start[:, cut] = jnp.concatenate(held, axis=1)
        returns[:, cut] = jnp.concatenate(gain, axis=1)


def first_primal(
    settings, moment, moment_other, stat, pack0, pack1, pack2, pack3, turned, sens, returns, start,
    given, weight, weight_sum,
):
    core = lax.axis_index("c")
    primal = column(settings, "primal")
    flag = column(settings, "restart") == 0.0
    mine, others = moment[...], moment_other[...]
    both = [jnp.where(core == 0, mine, others), jnp.where(core == 0, others, mine)]
    parts = matrix_parts(jnp.concatenate(both, axis=0), stat[4:6, :])
    total = jnp.zeros((OWN * DEPTH + 16, DEPTH), F32)
    bar_sum = jnp.zeros((OWN, 1), F32)
    for hop in range(RING):
        cut = slice(HALF * hop, HALF * (hop + 1))
        curve, line = forms(parts, turned[:, cut])
        weight[:, cut] = sens[0:1, cut] * line + sens[1:2, cut] * curve
    for hop, pack in enumerate((pack0, pack1, pack2, pack3)):
        cut = slice(HALF * hop, HALF * (hop + 1))
        held = start[:, cut]
        fresh = jnp.maximum(held + primal * (returns[:, cut] + weight[:, cut]), 0.0)
        bar = 2.0 * fresh - held
        bar_sum = bar_sum + jnp.sum(bar, axis=1, keepdims=True)
        wide = turned[:, cut].astype(F32)
        total = total + holdings_matrix(bar, wide, pack[0:HALF, :], sens[0:1, cut], sens[1:2, cut], True)
        both = held + fresh
        weight[:, cut] = jnp.where(flag, both / 2.0, fresh)
        weight_sum[:, cut] = jnp.where(flag, both / 2.0, both)
    given[0:256, :] = total[0:256, :]
    given[256:264, :] = jnp.concatenate(
        [total[256:258, :], share_rows(bar_sum), jnp.zeros((4, DEPTH), F32)], axis=0
    )


def partial_back(given, other, turned, sens, send, work):
    whole = given[...] + other[...]
    parts = matrix_parts(whole[0:256, :], whole[256:258, :])
    for hop in range(RING):
        cut = slice(HALF * hop, HALF * (hop + 1))
        curve, line = forms(parts, turned[:, cut])
        back = sens[0:1, cut] * line + sens[1:2, cut] * curve
        for part in range(8):
            spot = OWN * (8 * hop + part)
            work[spot : spot + OWN, :] = back[:, DEPTH * part : DEPTH * (part + 1)]
    work[LINES:SENT, :] = jnp.concatenate([count_row(whole[258:260, 0:1]), jnp.zeros((15, DEPTH), F32)], axis=0)
    rows = work[...].astype(BF16)
    for peer in range(GRID_Z):
        send[SENT * peer : SENT * (peer + 1), :] = rows


def sum_z(received, send):
    rows = received[0:SENT, :].astype(F32)
    for peer in range(1, GRID_Z):
        rows = rows + received[SENT * peer : SENT * (peer + 1), :].astype(F32)
    for peer in range(GRID_X):
        send[SENT * peer : SENT * (peer + 1), :] = rows


def second_primal(
    settings, received, pack0, pack1, pack2, pack3,
    turned, sens, returns, weight, weight_sum, price_row, given, stat, work,
):
    primal, restart = column(settings, "primal"), column(settings, "restart")
    first, flag = restart == 0.0, restart == 1.0
    count = jnp.where(first, 2.0, 3.0)
    price = price_row[:, 0:1]
    total = jnp.zeros((OWN * DEPTH + 16, DEPTH), F32)
    bar_sum = jnp.zeros((OWN, 1), F32)
    sums = received[0:SENT, :]
    for peer in range(1, GRID_X):
        sums = sums + received[SENT * peer : SENT * (peer + 1), :]
    work[...] = sums
    stat[...] = jnp.broadcast_to(work[LINES : LINES + 1, :], (8, DEPTH))
    for hop, pack in enumerate((pack0, pack1, pack2, pack3)):
        cut = slice(HALF * hop, HALF * (hop + 1))
        lines = [work[16 * hop + OWN * part : 16 * hop + OWN * (part + 1), :] for part in range(8)]
        back = jnp.concatenate(lines, axis=1)
        wide = turned[:, cut].astype(F32)
        held = weight[:, cut]
        fresh = jnp.maximum(held + primal * (returns[:, cut] + back + price), 0.0)
        bar = 2.0 * fresh - held
        bar_sum = bar_sum + jnp.sum(bar, axis=1, keepdims=True)
        total = total + holdings_matrix(bar, wide, pack[0:HALF, :], sens[0:1, cut], sens[1:2, cut], False)
        last = jnp.where(flag, (weight_sum[:, cut] + fresh) / count, fresh)
        for part in range(8):
            spot = 264 + OWN * (8 * hop + part)
            given[spot : spot + OWN, :] = last[:, DEPTH * part : DEPTH * (part + 1)]
    given[0:256, :] = total[0:256, :]
    given[256:264, :] = jnp.concatenate(
        [total[256:258, :], share_rows(bar_sum), jnp.zeros((4, DEPTH), F32)], axis=0
    )


def joint(given, other):
    whole = given[0:264, :] + other[0:264, :]
    share = whole[258:260, 0:1] * (1.0 / TOTAL_INST)
    matrix = jnp.concatenate([whole[0:256, :], tail_rows(whole[256:258, :])], axis=0)
    return jnp.concatenate(split2(matrix * SCALE), axis=1), share


def first_ready(settings, dual_start, stat, after, old, base, excess, excess_sum, small):
    y = lax.axis_index("y")
    primal, rate, averse, level, restart = (column(settings, name) for name in SETTINGS)
    flag = restart == 0.0
    level_new = level - primal * (averse - mass_of(stat))
    level_bar = 2.0 * level_new - level
    for step in range(NCHUNK):
        cut = slice(step * CHUNK, (step + 1) * CHUNK)
        dual = turn_to(dual_start[:, cut], y)[0:OWN, :]
        extra = jnp.maximum(0.0 - primal * (TAIL * averse - dual), 0.0)
        old[:, cut] = dual
        base[:, cut] = dual - rate * (2.0 * extra + level_bar)
        excess[:, cut], excess_sum[:, cut] = settle(flag, jnp.zeros_like(extra), extra)
    pieces = settle(flag, level, level_new)
    small[...] = jnp.concatenate([jnp.broadcast_to(piece, (OWN, DEPTH)) for piece in pieces], axis=0)


def settle(flag, old, new):
    both = old + new
    return jnp.where(flag, both / 2.0, new), jnp.where(flag, both / 2.0, both)


def first_dual(settings, given, other, shocks, turned, old, base, given_moment, dual, dual_sum, price):
    rate, flag = column(settings, "rate"), column(settings, "restart") == 0.0
    parts, share = joint(given, other)

    def dual_of(cut):
        curve, line = forms(parts, turned[:, cut])
        fresh = jnp.maximum(base[:, cut] - rate * (curve + line), 0.0)
        dual[:, cut], dual_sum[:, cut] = state, _ = settle(flag, old[:, cut], fresh)
        return state

    total, mass = moments(dual_of, shocks, turned)
    price_new = rate * (1.0 - share)
    price[...] = jnp.broadcast_to(settle(flag, jnp.zeros_like(price_new), price_new)[0], (OWN, DEPTH))
    given_moment[0:256, :] = total[0:256, :]
    given_moment[256:264, :] = jnp.concatenate(
        [total[256:258, :], share_rows(mass), jnp.zeros((4, DEPTH), F32)], axis=0
    )


def second_ready(settings, dual, excess, excess_sum, small, stat, after, base, extra_last, level_last):
    primal, rate, averse, _, restart = (column(settings, name) for name in SETTINGS)
    flag, count = restart == 1.0, jnp.where(restart == 0.0, 2.0, 3.0)
    level = small[0:2, 0:1]
    level_new = level - primal * (averse - mass_of(stat))
    level_bar = 2.0 * level_new - level
    for step in range(NCHUNK):
        cut = slice(step * CHUNK, (step + 1) * CHUNK)
        old, old_extra = dual[:, cut], excess[:, cut]
        extra = jnp.maximum(old_extra - primal * (TAIL * averse - old), 0.0)
        base[:, cut] = old - rate * ((2.0 * extra - old_extra) + level_bar)
        extra_last[:, cut] = jnp.where(flag, (excess_sum[:, cut] + extra) / count, extra)
    last = jnp.where(flag, (small[2:4, 0:1] + level_new) / count, level_new)
    level_last[...] = jnp.broadcast_to(last, (OWN, DEPTH))


def second_dual(settings, given, other, turned, dual_sum, base, extra_last, level_last, out0, out1, out2, out3):
    core = lax.axis_index("c")
    outs = (out0, out1, out2, out3)
    rate, restart = column(settings, "rate"), column(settings, "restart")
    flag, count = restart == 1.0, jnp.where(restart == 0.0, 2.0, 3.0)
    parts, _ = joint(given, other)
    for step in range(NCHUNK):
        cut = slice(step * CHUNK, (step + 1) * CHUNK)
        curve, line = forms(parts, turned[:, cut])
        fresh = jnp.maximum(base[:, cut] - rate * (curve + line), 0.0)
        last = jnp.where(flag, (dual_sum[:, cut] + fresh) / count, fresh)
        for out in outs:
            out[:, cut] = last
            out[:, SCEN_DEV + step * CHUNK : SCEN_DEV + (step + 1) * CHUNK] = extra_last[:, cut]
    m = grid_iota((DEPTH, 256), 0)
    lane = grid_iota((DEPTH, 256), 1)
    source = (lane >> 5) * PIECE + (lane & 15)
    mine = ((lane >> 4) & 1) == core
    own_pick = jnp.where((m == source) & mine, 1.0, 0.0).astype(BF16)
    other_pick = jnp.where((m == source) & jnp.logical_not(mine), 1.0, 0.0).astype(BF16)
    own_parts, other_parts = split3(given[264:328, :]), split3(other[264:328, :])
    pieces = [dot(a, own_pick) + dot(b, other_pick) for a, b in zip(own_parts, other_parts)]
    held = pieces[0] + pieces[1] + pieces[2]
    for hop, out in enumerate(outs):
        out[:, 2 * SCEN_DEV + BLOCK :] = level_last[...]
        for part in range(8):
            spot = OWN * (8 * hop + part)
            start = 2 * SCEN_DEV + 256 * part
            out[:, start : start + 256] = held[spot : spot + OWN, :]


def close_kernel(in0, in1, in2, in3, weights, duals, shortfall, threshold, work):
    y = lax.axis_index("y")
    for hop, taken in enumerate((in0, in1, in2, in3)):
        work[OWN * hop : OWN * (hop + 1), :] = taken[...]
    start = 0
    for out, width in ((duals, SCEN_DEV), (shortfall, SCEN_DEV), (weights, BLOCK)):
        for left in range(0, width, CHUNK):
            right = min(left + CHUNK, width)
            out[:, left:right] = turn_back(work[:, start + left : start + right], y)
        start += width
    levels = turn_back(work[:, start:], y)
    for spot in range(8):
        threshold[spot] = jnp.max(levels[spot : spot + 1, :])


def kernel(body, name, arrays, outs, scratch=(), left=0, limit=LIMIT):
    small = pl.BlockSpec(memory_space=pltpu.SMEM)
    large = pl.BlockSpec(memory_space=pltpu.VMEM)
    given = [pl.BlockSpec(memory_space=pltpu.HBM)] * left + [large] * (len(arrays) - left)
    call = pl.pallas_call(
        body,
        name=name,
        in_specs=given,
        out_specs=[small if len(shape) == 1 else large for shape, _ in outs],
        out_shape=[jax.ShapeDtypeStruct(shape, dtype) for shape, dtype in outs],
        scratch_shapes=list(scratch),
        compiler_params=pltpu.CompilerParams(vmem_limit_bytes=limit),
    )
    return list(call(*arrays))


def along(value, hop):
    return lax.ppermute(value, "y", [(i, (i + hop) % RING) for i in range(RING)])


def across(value):
    return lax.ppermute(value, "c", [(0, 1), (1, 0)])


def exchange(value, axes):
    return lax.all_to_all(value, axes, 0, 0, tiled=True)


def on_device(
    shocks, loadings, greeks, mean_return, weight_start, dual_start, level_start, aversion, primal_step, dual_step, restart_at,
):
    scen_rows = [((OWN, SCEN_DEV), F32)] * 4
    send, turned, chosen = kernel(
        open_kernel, "open",
        [
            shocks, dual_start, loadings.T, greeks, weight_start, mean_return[None, :],
            primal_step, dual_step, aversion, level_start, restart_at,
        ],
        [((PEERS * FIRST, DEPTH), BF16), ((DEPTH, SCEN_DEV), BF16), ((CHOSEN + 16, DEPTH), F32)],
        [
            pltpu.VMEM((PEERS, FIRST, DEPTH), F32), pltpu.VMEM((SCEN_DEV, DEPTH), BF16), pltpu.VMEM((8, SCEN_DEV), F32),
            pltpu.VMEM((2 * PIECE, DEPTH), BF16), pltpu.VMEM((3, 2 * PIECE), BF16), pltpu.VMEM((8, BLOCK), F32),
            pltpu.VMEM((1, BLOCK), F32), *[pltpu.SMEM((8,), F32)] * 4, pltpu.SMEM((8,), jnp.int32),
            pltpu.SemaphoreType.DMA((10 + SPLIT,)),
        ],
        left=11,
        limit=56 * 1024 * 1024,
    )
    received = exchange(send, ("x", "z", "c"))
    spread, stat, settings, *packs = kernel(
        sort_kernel, "sort", [received, chosen],
        [((DEPTH, DEPTH), F32), ((8, DEPTH), F32), ((16, DEPTH), F32)] + [((PACK, DEPTH), BF16)] * RING,
        [pltpu.VMEM((PEERS * FIRST, DEPTH), F32)],
    )
    packs = packs[:1] + [along(packs[hop], hop) for hop in range(1, RING)]
    moment = exchange(spread, ("x", "z"))
    moment_other = across(moment)
    loads, sens, returns, start = kernel(
        unpack_kernel, "unpack", packs, [((DEPTH, ALL), BF16), ((2, ALL), F32), ((1, ALL), F32), ((OWN, ALL), F32)]
    )
    given, weight, weight_sum = kernel(
        first_primal, "first_primal",
        [settings, moment, moment_other, stat, *packs, loads, sens, returns, start],
        [((264, DEPTH), F32), ((OWN, ALL), F32), ((OWN, ALL), F32)],
    )
    other = across(given)
    old, base, excess, excess_sum, small = kernel(
        first_ready, "first_ready", [settings, dual_start, stat, given], scen_rows + [((4, DEPTH), F32)]
    )
    given, dual, dual_sum, price = kernel(
        first_dual, "first_dual", [settings, given, other, shocks, turned, old, base],
        [((264, DEPTH), F32)] + scen_rows[:2] + [((OWN, DEPTH), F32)],
    )
    other = across(given)
    (send,) = kernel(
        partial_back, "partial_back", [given, other, loads, sens], [((GRID_Z * SENT, DEPTH), BF16)],
        [pltpu.VMEM((SENT, DEPTH), F32)],
    )
    received = exchange(send, "z")
    (send,) = kernel(sum_z, "sum_z", [received], [((GRID_X * SENT, DEPTH), F32)])
    received = exchange(send, "x")
    given, stat = kernel(
        second_primal, "second_primal",
        [settings, received, *packs, loads, sens, returns, weight, weight_sum, price],
        [((328, DEPTH), F32), ((8, DEPTH), F32)], [pltpu.VMEM((SENT, DEPTH), F32)],
    )
    other = across(given)
    base, extra_last, level_last = kernel(
        second_ready, "second_ready", [settings, dual, excess, excess_sum, small, stat, given],
        scen_rows[:2] + [((OWN, DEPTH), F32)],
    )
    outs = kernel(
        second_dual, "second_dual", [settings, given, other, turned, dual_sum, base, extra_last, level_last],
        [((OWN, 2 * SCEN_DEV + BLOCK + DEPTH), F32)] * RING,
    )
    taken = outs[:1] + [along(outs[hop], -hop) for hop in range(1, RING)]
    weights, duals, shortfall, threshold = kernel(
        close_kernel, "close", taken,
        [((8, BLOCK), F32), ((8, SCEN_DEV), F32), ((8, SCEN_DEV), F32), ((8,), F32)],
        [pltpu.VMEM((8, 2 * SCEN_DEV + BLOCK + DEPTH), F32)],
    )
    return weights, duals, shortfall, threshold


def solution(mesh):
    grid = Mesh(np.asarray(mesh.devices).reshape(GRID_X, GRID_Z, CORES, RING), ("x", "z", "c", "y"))
    scen = ("x", "z", "c")
    placed = (
        P(scen, None),
        P(None, ("y",) + scen),
        P(None, ("y",) + scen),
        P("y"),
        P(None, "y"),
        P(None, scen),
        P(),
        P(),
        P(),
        P(),
        P(),
    )
    return jax.shard_map(
        on_device,
        mesh=grid,
        in_specs=placed,
        out_specs=(P(None, "y"), P(None, scen), P(None, scen), P()),
        check_vma=False,
    )
```

```python
import math

import jax
import jax.numpy as jnp
import numpy as np
from jax import lax
from jax.experimental import pallas as pl
from jax.experimental.pallas import tpu as pltpu
from jax.sharding import Mesh, PartitionSpec as P

F32 = jnp.float32
BF16 = jnp.bfloat16
DEPTH = 128
SCEN_DEV = 4096
GRID_X, GRID_Z, CORES = 4, 8, 2
CHIPS = GRID_X * GRID_Z
PEERS = CHIPS * CORES
RING = 4
OWN = 2
PIECE = 16
HALF = PEERS * PIECE
BLOCK = 2 * HALF
ALL = RING * HALF
TOTAL_SCEN = float(PEERS * SCEN_DEV)
TOTAL_INST = float(RING * BLOCK)
SCALE = 1.0 / math.sqrt(TOTAL_INST)
SPLIT = 4
CHOSEN = 24 * 16
TAIL = 20.0
SETTINGS = ("primal", "rate", "averse", "level", "restart")
CHUNK = 512
NCHUNK = SCEN_DEV // CHUNK
FIRST = 5 * DEPTH
LINEAR = 40
LINES = OWN * ALL // DEPTH
SENT = LINES + 16
PACK = HALF + PEERS + 80
LIMIT = 48 * 1024 * 1024


def dot(a, b):
    return jnp.dot(a, b, preferred_element_type=F32)


def dot_nt(a, b):
    return lax.dot_general(a, b, (((1,), (1,)), ((), ())), preferred_element_type=F32)


def split2(value):
    high = value.astype(BF16)
    return high, (value - high.astype(F32)).astype(BF16)


def split3(value):
    high = value.astype(BF16)
    rest = value - high.astype(F32)
    middle = rest.astype(BF16)
    return high, middle, (rest - middle.astype(F32)).astype(BF16)


def grid_iota(shape, axis):
    return lax.broadcasted_iota(jnp.int32, shape, axis)


def identity(size):
    return jnp.where(grid_iota((size, size), 0) == grid_iota((size, size), 1), 1.0, 0.0).astype(BF16)


def column(settings, name):
    spot = OWN * SETTINGS.index(name)
    return settings[spot : spot + OWN, 0:1]


def turn_to(rows, y):
    return pltpu.roll(rows, (8 - OWN * y) & 7, axis=0)


def turn_back(rows, y):
    return pltpu.roll(rows, (OWN * y) & 7, axis=0)


def count_row(mass):
    lane = grid_iota((1, DEPTH), 1)
    row = jnp.zeros((1, DEPTH), F32)
    for own in range(OWN):
        for part, value in enumerate(split3(mass[own : own + 1, :])):
            row = jnp.where(lane == 32 + 3 * own + part, value.astype(F32), row)
    return row


def mass_of(stat):
    first = stat[6:7, 32:33] + stat[6:7, 33:34] + stat[6:7, 34:35]
    second = stat[6:7, 35:36] + stat[6:7, 36:37] + stat[6:7, 37:38]
    return jnp.where(grid_iota((OWN, 1), 0) == 0, first, second)


def tail_rows(rows):
    return jnp.concatenate([rows, jnp.zeros((16 - OWN, rows.shape[1]), rows.dtype)], axis=0)


def moments(dual_of, shocks, turned):
    total = jnp.zeros((OWN * DEPTH + 16, DEPTH), F32)
    mass = jnp.zeros((OWN, 1), F32)
    for step in range(NCHUNK):
        cut = slice(step * CHUNK, (step + 1) * CHUNK)
        dual = dual_of(cut)
        rounded = dual.astype(BF16).astype(F32)
        wide = turned[:, cut].astype(F32)
        left = [(wide * rounded[own : own + 1, :]).astype(BF16) for own in range(OWN)]
        left = jnp.concatenate(left + [tail_rows(rounded).astype(BF16)], axis=0)
        total = total + dot(left, shocks[cut, :])
        mass = mass + jnp.sum(dual, axis=1, keepdims=True)
    return total * (1.0 / TOTAL_SCEN), mass * (1.0 / TOTAL_SCEN)


def open_kernel(shocks_in, dual_in, loadings_in, greeks_in, holdings_in, returns_in, *rest):
    given, rest = rest[: len(SETTINGS)], rest[len(SETTINGS) :]
    send, turned, chosen, work, lines, shocks, dual, loadings, greeks, holdings, returns, *taken, gates = rest
    y, core = lax.axis_index("y"), lax.axis_index("c")
    unit = identity(DEPTH)
    pairs = [
        (dual_in, dual), (loadings_in, loadings), (greeks_in, greeks), (holdings_in, holdings), (returns_in, returns),
        *zip(given, taken),
    ]
    for n in range(SPLIT):
        cut = pl.ds(SCEN_DEV // SPLIT * n, SCEN_DEV // SPLIT)
        pairs.append((shocks_in.at[cut, :], shocks.at[cut, :]))
    copies = [pltpu.make_async_copy(a, b, gates.at[n]) for n, (a, b) in enumerate(pairs)]
    for copy in copies:
        copy.start()
    for copy in copies[:-SPLIT]:
        copy.wait()
    pair = grid_iota((OWN, DEPTH), 0)
    for n, ref in enumerate(taken):
        values = jnp.where(pair == 0, ref[OWN * y], ref[OWN * y + 1])
        chosen[CHOSEN + OWN * n : CHOSEN + OWN * (n + 1), :] = values.astype(F32)
    m = grid_iota((2 * DEPTH, DEPTH), 0)
    lane = grid_iota((2 * DEPTH, DEPTH), 1)
    pick = jnp.where(m == (lane >> 4) * 32 + core * PIECE + (lane & 15), 1.0, 0.0).astype(BF16)
    for part in range(BLOCK // 256):
        cut = slice(256 * part, 256 * (part + 1))
        both = jnp.concatenate(
            [turn_to(holdings[:, cut], y), returns[:, cut], jnp.zeros((7, 256), F32)], axis=0
        )
        for level, value in enumerate(split3(both)):
            chosen[16 * (8 * level + part) : 16 * (8 * level + part) + 16, :] = dot(value, pick)

    for copy in copies[-SPLIT:]:
        copy.wait()

    for step in range(NCHUNK):
        cut = slice(step * CHUNK, (step + 1) * CHUNK)
        turned[:, cut] = dot_nt(unit, shocks[cut, :]).astype(BF16)
    total, mass = moments(lambda cut: turn_to(dual[:, cut], y)[0:OWN, :], shocks, turned)
    rows = loadings[...].astype(F32)
    sens = greeks[...].astype(F32)
    delta, gamma = sens[0:1, :].astype(BF16), sens[1:2, :].astype(BF16)
    m = grid_iota((2 * PIECE, DEPTH), 0)
    lane = grid_iota((2 * PIECE, DEPTH), 1)
    tally = count_row(mass)
    notes = []
    for half in range(2):
        near = jnp.where((m == lane + PIECE * half) & (lane < PIECE), 1.0, 0.0).astype(BF16)
        far = jnp.where(
            (m == lane - PIECE + PIECE * half) & (lane >= PIECE) & (lane < 2 * PIECE), 1.0, 0.0
        ).astype(BF16)
        notes.append(dot(delta, near) + dot(gamma, far) + tally)
    lane = grid_iota((CHIPS, DEPTH), 1)
    share = grid_iota((CHIPS, DEPTH), 0) == (lane >> 2)
    m = grid_iota((DEPTH, DEPTH), 0)
    place = jnp.where(LINEAR + (m & 3) == grid_iota((DEPTH, DEPTH), 1), 1.0, 0.0).astype(BF16)
    for half in range(2):
        base = DEPTH * half
        first, second = total[base + 64 : base + 96, :], total[base + 96 : base + 128, :]
        linear = jnp.where(share, total[256 + half : 257 + half, :], 0.0).astype(BF16)
        lines[base : base + 64, :] = total[base : base + 64, :]
        lines[base + 64 : base + 96, :] = jnp.where(lane < 64, pltpu.roll(first, 64, axis=1), second)
        lines[base + 96 : base + 128, :] = dot(linear, place) + notes[half]
    for peer in range(PEERS):
        half, chip = peer % 2, peer // 2
        for part in range(4):
            spot = PIECE * half + 4 * part
            work[peer, :, DEPTH * part : DEPTH * (part + 1)] = rows[spot : spot + 4, :]
            spot = DEPTH * half + 32 * part + chip
            work[peer, part : part + 1, 4 * DEPTH : FIRST] = lines[spot : spot + 1, :]
    send[...] = work[...].astype(BF16)


def sort_kernel(received, chosen, spread, stat, settings, *rest):
    settings[...] = chosen[CHOSEN:, :]
    packs, (work, placed, tail) = rest[:RING], rest[RING:]
    work[...] = received[...].astype(F32)
    for part in range(4):
        placed[:, 4 * part : 4 * part + 4, :] = work[:, :, DEPTH * part : DEPTH * (part + 1)]
    last = work[:, :, 4 * DEPTH : FIRST]
    sums = jnp.sum(last, axis=0)
    tail[...] = last.reshape(4 * PEERS, DEPTH)
    stat[...] = jnp.broadcast_to(sums[3:4, :], (8, DEPTH))
    spread[...] = jnp.broadcast_to(sums[None], (CHIPS, 4, DEPTH)).reshape(DEPTH, DEPTH)
    rows = placed[...].reshape(HALF, DEPTH).astype(BF16)
    notes = tail[pl.ds(3, PEERS, stride=4), :].astype(BF16)
    for hop in range(RING):
        pieces = [chosen[16 * n + OWN * hop : 16 * n + OWN * (hop + 1), :] for n in range(24)]
        pieces += [chosen[16 * n + 8 : 16 * n + 9, :] for n in range(24)]
        pieces.append(jnp.zeros((8, DEPTH), F32))
        packs[hop][0:HALF, :] = rows
        packs[hop][HALF : HALF + PEERS, :] = notes
        packs[hop][HALF + PEERS : PACK, :] = jnp.concatenate(pieces, axis=0).astype(BF16)


def matrix_parts(moment, linear):
    return jnp.concatenate(split2(jnp.concatenate([moment, tail_rows(linear)], axis=0)), axis=1)


def forms(parts, half):
    form = dot(parts, jnp.concatenate([half, half], axis=0))
    wide = half.astype(F32)
    curve = [
        jnp.sum(form[DEPTH * own : DEPTH * (own + 1), :] * wide, axis=0, keepdims=True)
        for own in range(OWN)
    ]
    return jnp.concatenate(curve, axis=0), form[OWN * DEPTH : OWN * DEPTH + OWN, :]


def holdings_matrix(bar, turned, rows, delta, gamma, stacked):
    rounded = bar.astype(BF16).astype(F32)
    curve = rounded * gamma
    left = [turned * curve[own : own + 1, :] for own in range(OWN)]
    left = jnp.concatenate(left + [tail_rows(rounded * delta)], axis=0)
    high, low = split2(left)
    if not stacked:
        return dot(high, rows) + dot(low, rows)
    both = dot(jnp.concatenate([high, low], axis=0), rows)
    half = OWN * DEPTH + 16
    return both[0:half, :] + both[half : 2 * half, :]


def share_rows(bar_sum):
    return jnp.broadcast_to(bar_sum, (OWN, DEPTH))


def unfold(moment):
    first, second, low, notes = (moment[pl.ds(n, CHIPS, stride=4), :] for n in range(4))
    upper = jnp.concatenate([first, second], axis=0)
    right = jnp.concatenate([pltpu.roll(low, 64, axis=1), low], axis=0)
    mirror = jnp.concatenate([upper, jnp.zeros((64, DEPTH), F32)], axis=0).T
    lower = jnp.where(grid_iota((64, DEPTH), 1) < 64, mirror[64:128, :], right)
    row, lane = grid_iota((DEPTH, DEPTH), 0), grid_iota((DEPTH, DEPTH), 1)
    pick = jnp.where(row == LINEAR + (lane & 3), 1.0, 0.0).astype(BF16)
    high, rest = split2(notes)
    spread = dot(high, pick) + dot(rest, pick)
    mine = grid_iota((CHIPS, DEPTH), 0) == (grid_iota((CHIPS, DEPTH), 1) >> 2)
    linear = jnp.sum(jnp.where(mine, spread, 0.0), axis=0, keepdims=True)
    return jnp.concatenate([upper, lower], axis=0), linear


def unpack_kernel(moment, pack0, pack1, pack2, pack3, turned, sens, returns, start, unfolded):
    matrix, linear = unfold(moment)
    unfolded[0:DEPTH, :] = matrix
    unfolded[DEPTH : DEPTH + 8, :] = jnp.broadcast_to(linear, (8, DEPTH))
    unit = identity(DEPTH)
    row = grid_iota((PEERS, HALF), 0)
    col = grid_iota((PEERS, HALF), 1)
    mine = row == (col >> 4)
    m = grid_iota((DEPTH, HALF), 0)
    slot = grid_iota((DEPTH, HALF), 1) & 15
    near = jnp.where(m == slot, 1.0, 0.0).astype(BF16)
    far = jnp.where(m == slot + PIECE, 1.0, 0.0).astype(BF16)
    for hop, pack in enumerate((pack0, pack1, pack2, pack3)):
        cut = slice(HALF * hop, HALF * (hop + 1))
        turned[:, cut] = dot_nt(unit, pack[0:HALF, :]).astype(BF16)
        notes = pack[HALF : HALF + PEERS, :]
        sens[0:1, cut] = jnp.sum(jnp.where(mine, dot(notes, near), 0.0), axis=0, keepdims=True)
        sens[1:2, cut] = 0.5 * jnp.sum(jnp.where(mine, dot(notes, far), 0.0), axis=0, keepdims=True)
        more = pack[HALF + PEERS : PACK, :].astype(F32)
        held = [
            more[2 * n : 2 * n + 2, :] + more[2 * n + 16 : 2 * n + 18, :] + more[2 * n + 32 : 2 * n + 34, :]
            for n in range(8)
        ]
        gain = [
            more[48 + n : 49 + n, :] + more[56 + n : 57 + n, :] + more[64 + n : 65 + n, :]
            for n in range(8)
        ]
        start[:, cut] = jnp.concatenate(held, axis=1)
        returns[:, cut] = jnp.concatenate(gain, axis=1)


def first_primal(
    settings, moment, moment_other, pack0, pack1, pack2, pack3, turned, sens, returns, start,
    given, weight, weight_sum,
):
    core = lax.axis_index("c")
    primal = column(settings, "primal")
    flag = column(settings, "restart") == 0.0
    mine = moment[0:DEPTH, :], moment[DEPTH : DEPTH + 1, :]
    others = unfold(moment_other)
    first = [jnp.where(core == 0, a, b) for a, b in zip(mine, others)]
    second = [jnp.where(core == 0, b, a) for a, b in zip(mine, others)]
    parts = matrix_parts(*(jnp.concatenate(pair, axis=0) for pair in zip(first, second)))
    total = jnp.zeros((OWN * DEPTH + 16, DEPTH), F32)
    bar_sum = jnp.zeros((OWN, 1), F32)
    for hop in range(RING):
        cut = slice(HALF * hop, HALF * (hop + 1))
        curve, line = forms(parts, turned[:, cut])
        weight[:, cut] = sens[0:1, cut] * line + sens[1:2, cut] * curve
    for hop, pack in enumerate((pack0, pack1, pack2, pack3)):
        cut = slice(HALF * hop, HALF * (hop + 1))
        held = start[:, cut]
        fresh = jnp.maximum(held + primal * (returns[:, cut] + weight[:, cut]), 0.0)
        bar = 2.0 * fresh - held
        bar_sum = bar_sum + jnp.sum(bar, axis=1, keepdims=True)
        wide = turned[:, cut].astype(F32)
        total = total + holdings_matrix(bar, wide, pack[0:HALF, :], sens[0:1, cut], sens[1:2, cut], True)
        both = held + fresh
        weight[:, cut] = jnp.where(flag, both / 2.0, fresh)
        weight_sum[:, cut] = jnp.where(flag, both / 2.0, both)
    given[0:256, :] = total[0:256, :]
    given[256:264, :] = jnp.concatenate(
        [total[256:258, :], share_rows(bar_sum), jnp.zeros((4, DEPTH), F32)], axis=0
    )


def partial_back(given, other, turned, sens, send, work):
    whole = given[...] + other[...]
    parts = matrix_parts(whole[0:256, :], whole[256:258, :])
    for hop in range(RING):
        cut = slice(HALF * hop, HALF * (hop + 1))
        curve, line = forms(parts, turned[:, cut])
        back = sens[0:1, cut] * line + sens[1:2, cut] * curve
        for part in range(8):
            spot = OWN * (8 * hop + part)
            work[spot : spot + OWN, :] = back[:, DEPTH * part : DEPTH * (part + 1)]
    work[LINES:SENT, :] = jnp.concatenate([count_row(whole[258:260, 0:1]), jnp.zeros((15, DEPTH), F32)], axis=0)
    rows = work[...].astype(BF16)
    for peer in range(GRID_Z):
        send[SENT * peer : SENT * (peer + 1), :] = rows


def sum_z(received, send):
    rows = received[0:SENT, :].astype(F32)
    for peer in range(1, GRID_Z):
        rows = rows + received[SENT * peer : SENT * (peer + 1), :].astype(F32)
    for peer in range(GRID_X):
        send[SENT * peer : SENT * (peer + 1), :] = rows


def second_primal(
    settings, received, pack0, pack1, pack2, pack3,
    turned, sens, returns, weight, weight_sum, price_row, given, stat, work,
):
    primal, restart = column(settings, "primal"), column(settings, "restart")
    first, flag = restart == 0.0, restart == 1.0
    count = jnp.where(first, 2.0, 3.0)
    price = price_row[:, 0:1]
    total = jnp.zeros((OWN * DEPTH + 16, DEPTH), F32)
    bar_sum = jnp.zeros((OWN, 1), F32)
    sums = received[0:SENT, :]
    for peer in range(1, GRID_X):
        sums = sums + received[SENT * peer : SENT * (peer + 1), :]
    work[...] = sums
    stat[...] = jnp.broadcast_to(work[LINES : LINES + 1, :], (8, DEPTH))
    for hop, pack in enumerate((pack0, pack1, pack2, pack3)):
        cut = slice(HALF * hop, HALF * (hop + 1))
        lines = [work[16 * hop + OWN * part : 16 * hop + OWN * (part + 1), :] for part in range(8)]
        back = jnp.concatenate(lines, axis=1)
        wide = turned[:, cut].astype(F32)
        held = weight[:, cut]
        fresh = jnp.maximum(held + primal * (returns[:, cut] + back + price), 0.0)
        bar = 2.0 * fresh - held
        bar_sum = bar_sum + jnp.sum(bar, axis=1, keepdims=True)
        total = total + holdings_matrix(bar, wide, pack[0:HALF, :], sens[0:1, cut], sens[1:2, cut], False)
        last = jnp.where(flag, (weight_sum[:, cut] + fresh) / count, fresh)
        for part in range(8):
            spot = 264 + OWN * (8 * hop + part)
            given[spot : spot + OWN, :] = last[:, DEPTH * part : DEPTH * (part + 1)]
    given[0:256, :] = total[0:256, :]
    given[256:264, :] = jnp.concatenate(
        [total[256:258, :], share_rows(bar_sum), jnp.zeros((4, DEPTH), F32)], axis=0
    )


def joint(given, other):
    whole = given[0:264, :] + other[0:264, :]
    share = whole[258:260, 0:1] * (1.0 / TOTAL_INST)
    matrix = jnp.concatenate([whole[0:256, :], tail_rows(whole[256:258, :])], axis=0)
    return jnp.concatenate(split2(matrix * SCALE), axis=1), share


def first_ready(settings, dual_start, stat, after, old, base, excess, excess_sum, small):
    y = lax.axis_index("y")
    primal, rate, averse, level, restart = (column(settings, name) for name in SETTINGS)
    flag = restart == 0.0
    level_new = level - primal * (averse - mass_of(stat))
    level_bar = 2.0 * level_new - level
    for step in range(NCHUNK):
        cut = slice(step * CHUNK, (step + 1) * CHUNK)
        dual = turn_to(dual_start[:, cut], y)[0:OWN, :]
        extra = jnp.maximum(0.0 - primal * (TAIL * averse - dual), 0.0)
        old[:, cut] = dual
        base[:, cut] = dual - rate * (2.0 * extra + level_bar)
        excess[:, cut], excess_sum[:, cut] = settle(flag, jnp.zeros_like(extra), extra)
    pieces = settle(flag, level, level_new)
    small[...] = jnp.concatenate([jnp.broadcast_to(piece, (OWN, DEPTH)) for piece in pieces], axis=0)


def settle(flag, old, new):
    both = old + new
    return jnp.where(flag, both / 2.0, new), jnp.where(flag, both / 2.0, both)


def first_dual(settings, given, other, shocks, turned, old, base, given_moment, dual, dual_sum, price):
    rate, flag = column(settings, "rate"), column(settings, "restart") == 0.0
    parts, share = joint(given, other)

    def dual_of(cut):
        curve, line = forms(parts, turned[:, cut])
        fresh = jnp.maximum(base[:, cut] - rate * (curve + line), 0.0)
        dual[:, cut], dual_sum[:, cut] = state, _ = settle(flag, old[:, cut], fresh)
        return state

    total, mass = moments(dual_of, shocks, turned)
    price_new = rate * (1.0 - share)
    price[...] = jnp.broadcast_to(settle(flag, jnp.zeros_like(price_new), price_new)[0], (OWN, DEPTH))
    given_moment[0:256, :] = total[0:256, :]
    given_moment[256:264, :] = jnp.concatenate(
        [total[256:258, :], share_rows(mass), jnp.zeros((4, DEPTH), F32)], axis=0
    )


def second_ready(settings, dual, excess, excess_sum, small, stat, after, base, extra_last, level_last):
    primal, rate, averse, _, restart = (column(settings, name) for name in SETTINGS)
    flag, count = restart == 1.0, jnp.where(restart == 0.0, 2.0, 3.0)
    level = small[0:2, 0:1]
    level_new = level - primal * (averse - mass_of(stat))
    level_bar = 2.0 * level_new - level
    for step in range(NCHUNK):
        cut = slice(step * CHUNK, (step + 1) * CHUNK)
        old, old_extra = dual[:, cut], excess[:, cut]
        extra = jnp.maximum(old_extra - primal * (TAIL * averse - old), 0.0)
        base[:, cut] = old - rate * ((2.0 * extra - old_extra) + level_bar)
        extra_last[:, cut] = jnp.where(flag, (excess_sum[:, cut] + extra) / count, extra)
    last = jnp.where(flag, (small[2:4, 0:1] + level_new) / count, level_new)
    level_last[...] = jnp.broadcast_to(last, (OWN, DEPTH))


def second_dual(settings, given, other, turned, dual_sum, base, extra_last, level_last, out0, out1, out2, out3):
    core = lax.axis_index("c")
    outs = (out0, out1, out2, out3)
    rate, restart = column(settings, "rate"), column(settings, "restart")
    flag, count = restart == 1.0, jnp.where(restart == 0.0, 2.0, 3.0)
    parts, _ = joint(given, other)
    for step in range(NCHUNK):
        cut = slice(step * CHUNK, (step + 1) * CHUNK)
        curve, line = forms(parts, turned[:, cut])
        fresh = jnp.maximum(base[:, cut] - rate * (curve + line), 0.0)
        last = jnp.where(flag, (dual_sum[:, cut] + fresh) / count, fresh)
        for out in outs:
            out[:, cut] = last
            out[:, SCEN_DEV + step * CHUNK : SCEN_DEV + (step + 1) * CHUNK] = extra_last[:, cut]
    m = grid_iota((DEPTH, 256), 0)
    lane = grid_iota((DEPTH, 256), 1)
    source = (lane >> 5) * PIECE + (lane & 15)
    mine = ((lane >> 4) & 1) == core
    own_pick = jnp.where((m == source) & mine, 1.0, 0.0).astype(BF16)
    other_pick = jnp.where((m == source) & jnp.logical_not(mine), 1.0, 0.0).astype(BF16)
    own_parts, other_parts = split3(given[264:328, :]), split3(other[264:328, :])
    pieces = [dot(a, own_pick) + dot(b, other_pick) for a, b in zip(own_parts, other_parts)]
    held = pieces[0] + pieces[1] + pieces[2]
    for hop, out in enumerate(outs):
        out[:, 2 * SCEN_DEV + BLOCK :] = level_last[...]
        for part in range(8):
            spot = OWN * (8 * hop + part)
            start = 2 * SCEN_DEV + 256 * part
            out[:, start : start + 256] = held[spot : spot + OWN, :]


def close_kernel(in0, in1, in2, in3, weights, duals, shortfall, threshold, work):
    y = lax.axis_index("y")
    for hop, taken in enumerate((in0, in1, in2, in3)):
        work[OWN * hop : OWN * (hop + 1), :] = taken[...]
    start = 0
    for out, width in ((duals, SCEN_DEV), (shortfall, SCEN_DEV), (weights, BLOCK)):
        for left in range(0, width, CHUNK):
            right = min(left + CHUNK, width)
            out[:, left:right] = turn_back(work[:, start + left : start + right], y)
        start += width
    levels = turn_back(work[:, start:], y)
    for spot in range(8):
        threshold[spot] = jnp.max(levels[spot : spot + 1, :])


def kernel(body, name, arrays, outs, scratch=(), left=0, limit=LIMIT):
    small = pl.BlockSpec(memory_space=pltpu.SMEM)
    large = pl.BlockSpec(memory_space=pltpu.VMEM)
    given = [pl.BlockSpec(memory_space=pltpu.HBM)] * left + [large] * (len(arrays) - left)
    call = pl.pallas_call(
        body,
        name=name,
        in_specs=given,
        out_specs=[small if len(shape) == 1 else large for shape, _ in outs],
        out_shape=[jax.ShapeDtypeStruct(shape, dtype) for shape, dtype in outs],
        scratch_shapes=list(scratch),
        compiler_params=pltpu.CompilerParams(vmem_limit_bytes=limit),
    )
    return list(call(*arrays))


def along(value, hop):
    return lax.ppermute(value, "y", [(i, (i + hop) % RING) for i in range(RING)])


def across(value):
    return lax.ppermute(value, "c", [(0, 1), (1, 0)])


def exchange(value, axes):
    return lax.all_to_all(value, axes, 0, 0, tiled=True)


def on_device(
    shocks, loadings, greeks, mean_return, weight_start, dual_start, level_start, aversion, primal_step, dual_step, restart_at,
):
    scen_rows = [((OWN, SCEN_DEV), F32)] * 4
    send, turned, chosen = kernel(
        open_kernel, "open",
        [
            shocks, dual_start, loadings.T, greeks, weight_start, mean_return[None, :],
            primal_step, dual_step, aversion, level_start, restart_at,
        ],
        [((PEERS, 4, FIRST), BF16), ((DEPTH, SCEN_DEV), BF16), ((CHOSEN + 16, DEPTH), F32)],
        [
            pltpu.VMEM((PEERS, 4, FIRST), F32), pltpu.VMEM((OWN * DEPTH, DEPTH), F32), pltpu.VMEM((SCEN_DEV, DEPTH), BF16), pltpu.VMEM((8, SCEN_DEV), F32),
            pltpu.VMEM((2 * PIECE, DEPTH), BF16), pltpu.VMEM((3, 2 * PIECE), BF16), pltpu.VMEM((8, BLOCK), F32),
            pltpu.VMEM((1, BLOCK), F32), *[pltpu.SMEM((8,), F32)] * 4, pltpu.SMEM((8,), jnp.int32),
            pltpu.SemaphoreType.DMA((10 + SPLIT,)),
        ],
        left=11,
        limit=56 * 1024 * 1024,
    )
    received = exchange(send, ("x", "z", "c"))
    spread, stat, settings, *packs = kernel(
        sort_kernel, "sort", [received, chosen],
        [((DEPTH, DEPTH), F32), ((8, DEPTH), F32), ((16, DEPTH), F32)] + [((PACK, DEPTH), BF16)] * RING,
        [pltpu.VMEM((PEERS, 4, FIRST), F32), pltpu.VMEM((PEERS, PIECE, DEPTH), F32), pltpu.VMEM((4 * PEERS, DEPTH), F32)],
    )
    packs = packs[:1] + [along(packs[hop], hop) for hop in range(1, RING)]
    moment = exchange(spread, ("x", "z"))
    moment_other = across(moment)
    loads, sens, returns, start, moment = kernel(
        unpack_kernel, "unpack", [moment, *packs],
        [((DEPTH, ALL), BF16), ((2, ALL), F32), ((1, ALL), F32), ((OWN, ALL), F32), ((DEPTH + 8, DEPTH), F32)],
    )
    given, weight, weight_sum = kernel(
        first_primal, "first_primal",
        [settings, moment, moment_other, *packs, loads, sens, returns, start],
        [((264, DEPTH), F32), ((OWN, ALL), F32), ((OWN, ALL), F32)],
    )
    other = across(given)
    old, base, excess, excess_sum, small = kernel(
        first_ready, "first_ready", [settings, dual_start, stat, given], scen_rows + [((4, DEPTH), F32)]
    )
    given, dual, dual_sum, price = kernel(
        first_dual, "first_dual", [settings, given, other, shocks, turned, old, base],
        [((264, DEPTH), F32)] + scen_rows[:2] + [((OWN, DEPTH), F32)],
    )
    other = across(given)
    (send,) = kernel(
        partial_back, "partial_back", [given, other, loads, sens], [((GRID_Z * SENT, DEPTH), BF16)],
        [pltpu.VMEM((SENT, DEPTH), F32)],
    )
    received = exchange(send, "z")
    (send,) = kernel(sum_z, "sum_z", [received], [((GRID_X * SENT, DEPTH), F32)])
    received = exchange(send, "x")
    given, stat = kernel(
        second_primal, "second_primal",
        [settings, received, *packs, loads, sens, returns, weight, weight_sum, price],
        [((328, DEPTH), F32), ((8, DEPTH), F32)], [pltpu.VMEM((SENT, DEPTH), F32)],
    )
    other = across(given)
    base, extra_last, level_last = kernel(
        second_ready, "second_ready", [settings, dual, excess, excess_sum, small, stat, given],
        scen_rows[:2] + [((OWN, DEPTH), F32)],
    )
    outs = kernel(
        second_dual, "second_dual", [settings, given, other, turned, dual_sum, base, extra_last, level_last],
        [((OWN, 2 * SCEN_DEV + BLOCK + DEPTH), F32)] * RING,
    )
    taken = outs[:1] + [along(outs[hop], -hop) for hop in range(1, RING)]
    weights, duals, shortfall, threshold = kernel(
        close_kernel, "close", taken,
        [((8, BLOCK), F32), ((8, SCEN_DEV), F32), ((8, SCEN_DEV), F32), ((8,), F32)],
        [pltpu.VMEM((8, 2 * SCEN_DEV + BLOCK + DEPTH), F32)],
    )
    return weights, duals, shortfall, threshold


def solution(mesh):
    grid = Mesh(np.asarray(mesh.devices).reshape(GRID_X, GRID_Z, CORES, RING), ("x", "z", "c", "y"))
    scen = ("x", "z", "c")
    placed = (
        P(scen, None),
        P(None, ("y",) + scen),
        P(None, ("y",) + scen),
        P("y"),
        P(None, "y"),
        P(None, scen),
        P(),
        P(),
        P(),
        P(),
        P(),
    )
    return jax.shard_map(
        on_device,
        mesh=grid,
        in_specs=placed,
        out_specs=(P(None, "y"), P(None, scen), P(None, scen), P()),
        check_vma=False,
    )
```

```python
import math

import jax
import jax.numpy as jnp
import numpy as np
from jax import lax
from jax.experimental import pallas as pl
from jax.experimental.pallas import tpu as pltpu
from jax.sharding import Mesh, PartitionSpec as P

F32 = jnp.float32
BF16 = jnp.bfloat16
DEPTH = 128
SCEN_DEV = 4096
GRID_X, GRID_Z, CORES = 4, 8, 2
CHIPS = GRID_X * GRID_Z
PEERS = CHIPS * CORES
RING = 4
OWN = 2
PIECE = 16
HALF = PEERS * PIECE
BLOCK = 2 * HALF
ALL = RING * HALF
TOTAL_SCEN = float(PEERS * SCEN_DEV)
TOTAL_INST = float(RING * BLOCK)
SCALE = 1.0 / math.sqrt(TOTAL_INST)
SPLIT = 4
CHOSEN = 24 * 16
TAIL = 20.0
SETTINGS = ("primal", "rate", "averse", "level", "restart")
CHUNK = 512
NCHUNK = SCEN_DEV // CHUNK
FIRST = 5 * DEPTH
LINEAR = 40
SENT = ALL + DEPTH
PACK = HALF + PEERS + 80
LIMIT = 48 * 1024 * 1024


def dot(a, b):
    return jnp.dot(a, b, preferred_element_type=F32)


def dot_nt(a, b):
    return lax.dot_general(a, b, (((1,), (1,)), ((), ())), preferred_element_type=F32)


def split2(value):
    high = value.astype(BF16)
    return high, (value - high.astype(F32)).astype(BF16)


def split3(value):
    high = value.astype(BF16)
    rest = value - high.astype(F32)
    middle = rest.astype(BF16)
    return high, middle, (rest - middle.astype(F32)).astype(BF16)


def grid_iota(shape, axis):
    return lax.broadcasted_iota(jnp.int32, shape, axis)


def identity(size):
    return jnp.where(grid_iota((size, size), 0) == grid_iota((size, size), 1), 1.0, 0.0).astype(BF16)


def column(settings, name):
    spot = OWN * SETTINGS.index(name)
    return settings[spot : spot + OWN, 0:1]


def turn_to(rows, y):
    return pltpu.roll(rows, (8 - OWN * y) & 7, axis=0)


def turn_back(rows, y):
    return pltpu.roll(rows, (OWN * y) & 7, axis=0)


def count_row(mass):
    lane = grid_iota((1, DEPTH), 1)
    row = jnp.zeros((1, DEPTH), F32)
    for own in range(OWN):
        for part, value in enumerate(split3(mass[own : own + 1, :])):
            row = jnp.where(lane == 32 + 3 * own + part, value.astype(F32), row)
    return row


def mass_of(stat):
    first = stat[6:7, 32:33] + stat[6:7, 33:34] + stat[6:7, 34:35]
    second = stat[6:7, 35:36] + stat[6:7, 36:37] + stat[6:7, 37:38]
    return jnp.where(grid_iota((OWN, 1), 0) == 0, first, second)


def tail_rows(rows):
    return jnp.concatenate([rows, jnp.zeros((16 - OWN, rows.shape[1]), rows.dtype)], axis=0)


def moments(dual_of, shocks, turned):
    total = jnp.zeros((OWN * DEPTH + 16, DEPTH), F32)
    mass = jnp.zeros((OWN, 1), F32)
    for step in range(NCHUNK):
        cut = slice(step * CHUNK, (step + 1) * CHUNK)
        dual = dual_of(cut)
        rounded = dual.astype(BF16).astype(F32)
        wide = turned[:, cut].astype(F32)
        left = [(wide * rounded[own : own + 1, :]).astype(BF16) for own in range(OWN)]
        left = jnp.concatenate(left + [tail_rows(rounded).astype(BF16)], axis=0)
        total = total + dot(left, shocks[cut, :])
        mass = mass + jnp.sum(dual, axis=1, keepdims=True)
    return total * (1.0 / TOTAL_SCEN), mass * (1.0 / TOTAL_SCEN)


def open_kernel(shocks_in, dual_in, loadings_in, greeks_in, holdings_in, returns_in, *rest):
    given, rest = rest[: len(SETTINGS)], rest[len(SETTINGS) :]
    send, turned, chosen, work, lines, shocks, dual, loadings, greeks, holdings, returns, *taken, gates = rest
    y, core = lax.axis_index("y"), lax.axis_index("c")
    unit = identity(DEPTH)
    pairs = [
        (dual_in, dual), (loadings_in, loadings), (greeks_in, greeks), (holdings_in, holdings), (returns_in, returns),
        *zip(given, taken),
    ]
    for n in range(SPLIT):
        cut = pl.ds(SCEN_DEV // SPLIT * n, SCEN_DEV // SPLIT)
        pairs.append((shocks_in.at[cut, :], shocks.at[cut, :]))
    copies = [pltpu.make_async_copy(a, b, gates.at[n]) for n, (a, b) in enumerate(pairs)]
    for copy in copies:
        copy.start()
    for copy in copies[:-SPLIT]:
        copy.wait()
    pair = grid_iota((OWN, DEPTH), 0)
    for n, ref in enumerate(taken):
        values = jnp.where(pair == 0, ref[OWN * y], ref[OWN * y + 1])
        chosen[CHOSEN + OWN * n : CHOSEN + OWN * (n + 1), :] = values.astype(F32)
    m = grid_iota((2 * DEPTH, DEPTH), 0)
    lane = grid_iota((2 * DEPTH, DEPTH), 1)
    pick = jnp.where(m == (lane >> 4) * 32 + core * PIECE + (lane & 15), 1.0, 0.0).astype(BF16)
    for part in range(BLOCK // 256):
        cut = slice(256 * part, 256 * (part + 1))
        both = jnp.concatenate(
            [turn_to(holdings[:, cut], y), returns[:, cut], jnp.zeros((7, 256), F32)], axis=0
        )
        for level, value in enumerate(split3(both)):
            chosen[16 * (8 * level + part) : 16 * (8 * level + part) + 16, :] = dot(value, pick)

    for copy in copies[-SPLIT:]:
        copy.wait()

    for step in range(NCHUNK):
        cut = slice(step * CHUNK, (step + 1) * CHUNK)
        turned[:, cut] = dot_nt(unit, shocks[cut, :]).astype(BF16)
    total, mass = moments(lambda cut: turn_to(dual[:, cut], y)[0:OWN, :], shocks, turned)
    rows = loadings[...].astype(F32)
    sens = greeks[...].astype(F32)
    delta, gamma = sens[0:1, :].astype(BF16), sens[1:2, :].astype(BF16)
    m = grid_iota((2 * PIECE, DEPTH), 0)
    lane = grid_iota((2 * PIECE, DEPTH), 1)
    tally = count_row(mass)
    notes = []
    for half in range(2):
        near = jnp.where((m == lane + PIECE * half) & (lane < PIECE), 1.0, 0.0).astype(BF16)
        far = jnp.where(
            (m == lane - PIECE + PIECE * half) & (lane >= PIECE) & (lane < 2 * PIECE), 1.0, 0.0
        ).astype(BF16)
        notes.append(dot(delta, near) + dot(gamma, far) + tally)
    lane = grid_iota((CHIPS, DEPTH), 1)
    share = grid_iota((CHIPS, DEPTH), 0) == (lane >> 2)
    m = grid_iota((DEPTH, DEPTH), 0)
    place = jnp.where(LINEAR + (m & 3) == grid_iota((DEPTH, DEPTH), 1), 1.0, 0.0).astype(BF16)
    for half in range(2):
        base = DEPTH * half
        first, second = total[base + 64 : base + 96, :], total[base + 96 : base + 128, :]
        linear = jnp.where(share, total[256 + half : 257 + half, :], 0.0).astype(BF16)
        lines[base : base + 64, :] = total[base : base + 64, :]
        lines[base + 64 : base + 96, :] = jnp.where(lane < 64, pltpu.roll(first, 64, axis=1), second)
        lines[base + 96 : base + 128, :] = dot(linear, place) + notes[half]
    for peer in range(PEERS):
        half, chip = peer % 2, peer // 2
        for part in range(4):
            spot = PIECE * half + 4 * part
            work[peer, :, DEPTH * part : DEPTH * (part + 1)] = rows[spot : spot + 4, :]
            spot = DEPTH * half + 32 * part + chip
            work[peer, part : part + 1, 4 * DEPTH : FIRST] = lines[spot : spot + 1, :]
    send[...] = work[...].astype(BF16)


def sort_kernel(received, chosen, spread, stat, settings, *rest):
    settings[...] = chosen[CHOSEN:, :]
    packs, (work, placed, tail) = rest[:RING], rest[RING:]
    work[...] = received[...].astype(F32)
    for part in range(4):
        placed[:, 4 * part : 4 * part + 4, :] = work[:, :, DEPTH * part : DEPTH * (part + 1)]
    last = work[:, :, 4 * DEPTH : FIRST]
    sums = jnp.sum(last, axis=0)
    tail[...] = last.reshape(4 * PEERS, DEPTH)
    stat[...] = jnp.broadcast_to(sums[3:4, :], (8, DEPTH))
    spread[...] = jnp.broadcast_to(sums[None], (CHIPS, 4, DEPTH)).reshape(DEPTH, DEPTH)
    rows = placed[...].reshape(HALF, DEPTH).astype(BF16)
    notes = tail[pl.ds(3, PEERS, stride=4), :].astype(BF16)
    for hop in range(RING):
        pieces = [chosen[16 * n + OWN * hop : 16 * n + OWN * (hop + 1), :] for n in range(24)]
        pieces += [chosen[16 * n + 8 : 16 * n + 9, :] for n in range(24)]
        pieces.append(jnp.zeros((8, DEPTH), F32))
        packs[hop][0:HALF, :] = rows
        packs[hop][HALF : HALF + PEERS, :] = notes
        packs[hop][HALF + PEERS : PACK, :] = jnp.concatenate(pieces, axis=0).astype(BF16)


def matrix_parts(moment, linear):
    return jnp.concatenate(split2(jnp.concatenate([moment, tail_rows(linear)], axis=0)), axis=1)


def forms(parts, half):
    form = dot(parts, jnp.concatenate([half, half], axis=0))
    wide = half.astype(F32)
    curve = [
        jnp.sum(form[DEPTH * own : DEPTH * (own + 1), :] * wide, axis=0, keepdims=True)
        for own in range(OWN)
    ]
    return jnp.concatenate(curve, axis=0), form[OWN * DEPTH : OWN * DEPTH + OWN, :]


def holdings_matrix(bar, turned, rows, delta, gamma, stacked):
    rounded = bar.astype(BF16).astype(F32)
    curve = rounded * gamma
    left = [turned * curve[own : own + 1, :] for own in range(OWN)]
    left = jnp.concatenate(left + [tail_rows(rounded * delta)], axis=0)
    high, low = split2(left)
    if not stacked:
        return dot(high, rows) + dot(low, rows)
    both = dot(jnp.concatenate([high, low], axis=0), rows)
    half = OWN * DEPTH + 16
    return both[0:half, :] + both[half : 2 * half, :]


def share_rows(bar_sum):
    return jnp.broadcast_to(bar_sum, (OWN, DEPTH))


def unfold(moment):
    first, second, low, notes = (moment[pl.ds(n, CHIPS, stride=4), :] for n in range(4))
    upper = jnp.concatenate([first, second], axis=0)
    right = jnp.concatenate([pltpu.roll(low, 64, axis=1), low], axis=0)
    mirror = jnp.concatenate([upper, jnp.zeros((64, DEPTH), F32)], axis=0).T
    lower = jnp.where(grid_iota((64, DEPTH), 1) < 64, mirror[64:128, :], right)
    row, lane = grid_iota((DEPTH, DEPTH), 0), grid_iota((DEPTH, DEPTH), 1)
    pick = jnp.where(row == LINEAR + (lane & 3), 1.0, 0.0).astype(BF16)
    high, rest = split2(notes)
    spread = dot(high, pick) + dot(rest, pick)
    mine = grid_iota((CHIPS, DEPTH), 0) == (grid_iota((CHIPS, DEPTH), 1) >> 2)
    linear = jnp.sum(jnp.where(mine, spread, 0.0), axis=0, keepdims=True)
    return jnp.concatenate([upper, lower], axis=0), linear


def unpack_kernel(moment, pack0, pack1, pack2, pack3, turned, sens, returns, start, unfolded):
    matrix, linear = unfold(moment)
    unfolded[0:DEPTH, :] = matrix
    unfolded[DEPTH : DEPTH + 8, :] = jnp.broadcast_to(linear, (8, DEPTH))
    unit = identity(DEPTH)
    row = grid_iota((PEERS, HALF), 0)
    col = grid_iota((PEERS, HALF), 1)
    mine = row == (col >> 4)
    m = grid_iota((DEPTH, HALF), 0)
    slot = grid_iota((DEPTH, HALF), 1) & 15
    near = jnp.where(m == slot, 1.0, 0.0).astype(BF16)
    far = jnp.where(m == slot + PIECE, 1.0, 0.0).astype(BF16)
    for hop, pack in enumerate((pack0, pack1, pack2, pack3)):
        cut = slice(HALF * hop, HALF * (hop + 1))
        turned[:, cut] = dot_nt(unit, pack[0:HALF, :]).astype(BF16)
        notes = pack[HALF : HALF + PEERS, :]
        sens[0:1, cut] = jnp.sum(jnp.where(mine, dot(notes, near), 0.0), axis=0, keepdims=True)
        sens[1:2, cut] = 0.5 * jnp.sum(jnp.where(mine, dot(notes, far), 0.0), axis=0, keepdims=True)
        more = pack[HALF + PEERS : PACK, :].astype(F32)
        held = [
            more[2 * n : 2 * n + 2, :] + more[2 * n + 16 : 2 * n + 18, :] + more[2 * n + 32 : 2 * n + 34, :]
            for n in range(8)
        ]
        gain = [
            more[48 + n : 49 + n, :] + more[56 + n : 57 + n, :] + more[64 + n : 65 + n, :]
            for n in range(8)
        ]
        start[:, cut] = jnp.concatenate(held, axis=1)
        returns[:, cut] = jnp.concatenate(gain, axis=1)


def first_primal(
    settings, moment, moment_other, pack0, pack1, pack2, pack3, turned, sens, returns, start,
    given, weight, weight_sum,
):
    core = lax.axis_index("c")
    primal = column(settings, "primal")
    flag = column(settings, "restart") == 0.0
    mine = moment[0:DEPTH, :], moment[DEPTH : DEPTH + 1, :]
    others = unfold(moment_other)
    first = [jnp.where(core == 0, a, b) for a, b in zip(mine, others)]
    second = [jnp.where(core == 0, b, a) for a, b in zip(mine, others)]
    parts = matrix_parts(*(jnp.concatenate(pair, axis=0) for pair in zip(first, second)))
    total = jnp.zeros((OWN * DEPTH + 16, DEPTH), F32)
    bar_sum = jnp.zeros((OWN, 1), F32)
    for hop in range(RING):
        cut = slice(HALF * hop, HALF * (hop + 1))
        curve, line = forms(parts, turned[:, cut])
        weight[:, cut] = sens[0:1, cut] * line + sens[1:2, cut] * curve
    for hop, pack in enumerate((pack0, pack1, pack2, pack3)):
        cut = slice(HALF * hop, HALF * (hop + 1))
        held = start[:, cut]
        fresh = jnp.maximum(held + primal * (returns[:, cut] + weight[:, cut]), 0.0)
        bar = 2.0 * fresh - held
        bar_sum = bar_sum + jnp.sum(bar, axis=1, keepdims=True)
        wide = turned[:, cut].astype(F32)
        total = total + holdings_matrix(bar, wide, pack[0:HALF, :], sens[0:1, cut], sens[1:2, cut], True)
        both = held + fresh
        weight[:, cut] = jnp.where(flag, both / 2.0, fresh)
        weight_sum[:, cut] = jnp.where(flag, both / 2.0, both)
    given[0:256, :] = total[0:256, :]
    given[256:264, :] = jnp.concatenate(
        [total[256:258, :], share_rows(bar_sum), jnp.zeros((4, DEPTH), F32)], axis=0
    )


def partial_back(given, other, turned, sens, send):
    whole = given[...] + other[...]
    parts = matrix_parts(whole[0:256, :], whole[256:258, :])
    for hop in range(RING):
        cut = slice(HALF * hop, HALF * (hop + 1))
        curve, line = forms(parts, turned[:, cut])
        back = (sens[0:1, cut] * line + sens[1:2, cut] * curve).astype(BF16)
        for peer in range(GRID_Z):
            send[peer, :, cut] = back
    lane = grid_iota((OWN, DEPTH), 1)
    tally = jnp.zeros((OWN, DEPTH), F32)
    for part, value in enumerate(split3(whole[258:260, 0:1])):
        tally = jnp.where(lane == part, value.astype(F32), tally)
    for peer in range(GRID_Z):
        send[peer, :, ALL:SENT] = tally.astype(BF16)


def sum_z(received, send):
    total = received[0].astype(F32)
    for peer in range(1, GRID_Z):
        total = total + received[peer].astype(F32)
    for peer in range(GRID_X):
        send[peer] = total


def sum_x(received, cut):
    total = received[0, :, cut]
    for peer in range(1, GRID_X):
        total = total + received[peer, :, cut]
    return total


def second_primal(
    settings, received, pack0, pack1, pack2, pack3,
    turned, sens, returns, weight, weight_sum, price_row, given, stat,
):
    primal, restart = column(settings, "primal"), column(settings, "restart")
    first, flag = restart == 0.0, restart == 1.0
    count = jnp.where(first, 2.0, 3.0)
    price = price_row[:, 0:1]
    total = jnp.zeros((OWN * DEPTH + 16, DEPTH), F32)
    bar_sum = jnp.zeros((OWN, 1), F32)
    tally = sum_x(received, slice(ALL, SENT))
    stat[...] = jnp.broadcast_to(tally[:, 0:1] + tally[:, 1:2] + tally[:, 2:3], (OWN, DEPTH))
    for hop, pack in enumerate((pack0, pack1, pack2, pack3)):
        cut = slice(HALF * hop, HALF * (hop + 1))
        back = sum_x(received, cut)
        wide = turned[:, cut].astype(F32)
        held = weight[:, cut]
        fresh = jnp.maximum(held + primal * (returns[:, cut] + back + price), 0.0)
        bar = 2.0 * fresh - held
        bar_sum = bar_sum + jnp.sum(bar, axis=1, keepdims=True)
        total = total + holdings_matrix(bar, wide, pack[0:HALF, :], sens[0:1, cut], sens[1:2, cut], False)
        last = jnp.where(flag, (weight_sum[:, cut] + fresh) / count, fresh)
        for part in range(8):
            spot = 264 + OWN * (8 * hop + part)
            given[spot : spot + OWN, :] = last[:, DEPTH * part : DEPTH * (part + 1)]
    given[0:256, :] = total[0:256, :]
    given[256:264, :] = jnp.concatenate(
        [total[256:258, :], share_rows(bar_sum), jnp.zeros((4, DEPTH), F32)], axis=0
    )


def joint(given, other):
    whole = given[0:264, :] + other[0:264, :]
    share = whole[258:260, 0:1] * (1.0 / TOTAL_INST)
    matrix = jnp.concatenate([whole[0:256, :], tail_rows(whole[256:258, :])], axis=0)
    return jnp.concatenate(split2(matrix * SCALE), axis=1), share


def first_ready(settings, dual_start, stat, after, old, base, excess, excess_sum, small):
    y = lax.axis_index("y")
    primal, rate, averse, level, restart = (column(settings, name) for name in SETTINGS)
    flag = restart == 0.0
    level_new = level - primal * (averse - mass_of(stat))
    level_bar = 2.0 * level_new - level
    for step in range(NCHUNK):
        cut = slice(step * CHUNK, (step + 1) * CHUNK)
        dual = turn_to(dual_start[:, cut], y)[0:OWN, :]
        extra = jnp.maximum(0.0 - primal * (TAIL * averse - dual), 0.0)
        old[:, cut] = dual
        base[:, cut] = dual - rate * (2.0 * extra + level_bar)
        excess[:, cut], excess_sum[:, cut] = settle(flag, jnp.zeros_like(extra), extra)
    pieces = settle(flag, level, level_new)
    small[...] = jnp.concatenate([jnp.broadcast_to(piece, (OWN, DEPTH)) for piece in pieces], axis=0)


def settle(flag, old, new):
    both = old + new
    return jnp.where(flag, both / 2.0, new), jnp.where(flag, both / 2.0, both)


def first_dual(settings, given, other, shocks, turned, old, base, given_moment, dual, dual_sum, price):
    rate, flag = column(settings, "rate"), column(settings, "restart") == 0.0
    parts, share = joint(given, other)

    def dual_of(cut):
        curve, line = forms(parts, turned[:, cut])
        fresh = jnp.maximum(base[:, cut] - rate * (curve + line), 0.0)
        dual[:, cut], dual_sum[:, cut] = state, _ = settle(flag, old[:, cut], fresh)
        return state

    total, mass = moments(dual_of, shocks, turned)
    price_new = rate * (1.0 - share)
    price[...] = jnp.broadcast_to(settle(flag, jnp.zeros_like(price_new), price_new)[0], (OWN, DEPTH))
    given_moment[0:256, :] = total[0:256, :]
    given_moment[256:264, :] = jnp.concatenate(
        [total[256:258, :], share_rows(mass), jnp.zeros((4, DEPTH), F32)], axis=0
    )


def second_ready(settings, dual, excess, excess_sum, small, stat, after, base, extra_last, level_last):
    primal, rate, averse, _, restart = (column(settings, name) for name in SETTINGS)
    flag, count = restart == 1.0, jnp.where(restart == 0.0, 2.0, 3.0)
    level = small[0:2, 0:1]
    level_new = level - primal * (averse - stat[:, 0:1])
    level_bar = 2.0 * level_new - level
    for step in range(NCHUNK):
        cut = slice(step * CHUNK, (step + 1) * CHUNK)
        old, old_extra = dual[:, cut], excess[:, cut]
        extra = jnp.maximum(old_extra - primal * (TAIL * averse - old), 0.0)
        base[:, cut] = old - rate * ((2.0 * extra - old_extra) + level_bar)
        extra_last[:, cut] = jnp.where(flag, (excess_sum[:, cut] + extra) / count, extra)
    last = jnp.where(flag, (small[2:4, 0:1] + level_new) / count, level_new)
    level_last[...] = jnp.broadcast_to(last, (OWN, DEPTH))


def second_dual(settings, given, other, turned, dual_sum, base, extra_last, level_last, out0, out1, out2, out3):
    core = lax.axis_index("c")
    outs = (out0, out1, out2, out3)
    rate, restart = column(settings, "rate"), column(settings, "restart")
    flag, count = restart == 1.0, jnp.where(restart == 0.0, 2.0, 3.0)
    parts, _ = joint(given, other)
    for step in range(NCHUNK):
        cut = slice(step * CHUNK, (step + 1) * CHUNK)
        curve, line = forms(parts, turned[:, cut])
        fresh = jnp.maximum(base[:, cut] - rate * (curve + line), 0.0)
        last = jnp.where(flag, (dual_sum[:, cut] + fresh) / count, fresh)
        for out in outs:
            out[:, cut] = last
            out[:, SCEN_DEV + step * CHUNK : SCEN_DEV + (step + 1) * CHUNK] = extra_last[:, cut]
    m = grid_iota((DEPTH, 256), 0)
    lane = grid_iota((DEPTH, 256), 1)
    source = (lane >> 5) * PIECE + (lane & 15)
    mine = ((lane >> 4) & 1) == core
    own_pick = jnp.where((m == source) & mine, 1.0, 0.0).astype(BF16)
    other_pick = jnp.where((m == source) & jnp.logical_not(mine), 1.0, 0.0).astype(BF16)
    own_parts, other_parts = split3(given[264:328, :]), split3(other[264:328, :])
    pieces = [dot(a, own_pick) + dot(b, other_pick) for a, b in zip(own_parts, other_parts)]
    held = pieces[0] + pieces[1] + pieces[2]
    for hop, out in enumerate(outs):
        out[:, 2 * SCEN_DEV + BLOCK :] = level_last[...]
        for part in range(8):
            spot = OWN * (8 * hop + part)
            start = 2 * SCEN_DEV + 256 * part
            out[:, start : start + 256] = held[spot : spot + OWN, :]


def close_kernel(in0, in1, in2, in3, weights, duals, shortfall, threshold, work):
    y = lax.axis_index("y")
    for hop, taken in enumerate((in0, in1, in2, in3)):
        work[OWN * hop : OWN * (hop + 1), :] = taken[...]
    start = 0
    for out, width in ((duals, SCEN_DEV), (shortfall, SCEN_DEV), (weights, BLOCK)):
        for left in range(0, width, CHUNK):
            right = min(left + CHUNK, width)
            out[:, left:right] = turn_back(work[:, start + left : start + right], y)
        start += width
    levels = turn_back(work[:, start:], y)
    for spot in range(8):
        threshold[spot] = jnp.max(levels[spot : spot + 1, :])


def kernel(body, name, arrays, outs, scratch=(), left=0, limit=LIMIT):
    small = pl.BlockSpec(memory_space=pltpu.SMEM)
    large = pl.BlockSpec(memory_space=pltpu.VMEM)
    given = [pl.BlockSpec(memory_space=pltpu.HBM)] * left + [large] * (len(arrays) - left)
    call = pl.pallas_call(
        body,
        name=name,
        in_specs=given,
        out_specs=[small if len(shape) == 1 else large for shape, _ in outs],
        out_shape=[jax.ShapeDtypeStruct(shape, dtype) for shape, dtype in outs],
        scratch_shapes=list(scratch),
        compiler_params=pltpu.CompilerParams(vmem_limit_bytes=limit),
    )
    return list(call(*arrays))


def along(value, hop):
    return lax.ppermute(value, "y", [(i, (i + hop) % RING) for i in range(RING)])


def across(value):
    return lax.ppermute(value, "c", [(0, 1), (1, 0)])


def exchange(value, axes):
    return lax.all_to_all(value, axes, 0, 0, tiled=True)


def on_device(
    shocks, loadings, greeks, mean_return, weight_start, dual_start, level_start, aversion, primal_step, dual_step, restart_at,
):
    scen_rows = [((OWN, SCEN_DEV), F32)] * 4
    send, turned, chosen = kernel(
        open_kernel, "open",
        [
            shocks, dual_start, loadings.T, greeks, weight_start, mean_return[None, :],
            primal_step, dual_step, aversion, level_start, restart_at,
        ],
        [((PEERS, 4, FIRST), BF16), ((DEPTH, SCEN_DEV), BF16), ((CHOSEN + 16, DEPTH), F32)],
        [
            pltpu.VMEM((PEERS, 4, FIRST), F32), pltpu.VMEM((OWN * DEPTH, DEPTH), F32), pltpu.VMEM((SCEN_DEV, DEPTH), BF16), pltpu.VMEM((8, SCEN_DEV), F32),
            pltpu.VMEM((2 * PIECE, DEPTH), BF16), pltpu.VMEM((3, 2 * PIECE), BF16), pltpu.VMEM((8, BLOCK), F32),
            pltpu.VMEM((1, BLOCK), F32), *[pltpu.SMEM((8,), F32)] * 4, pltpu.SMEM((8,), jnp.int32),
            pltpu.SemaphoreType.DMA((10 + SPLIT,)),
        ],
        left=11,
        limit=56 * 1024 * 1024,
    )
    received = exchange(send, ("x", "z", "c"))
    spread, stat, settings, *packs = kernel(
        sort_kernel, "sort", [received, chosen],
        [((DEPTH, DEPTH), F32), ((8, DEPTH), F32), ((16, DEPTH), F32)] + [((PACK, DEPTH), BF16)] * RING,
        [pltpu.VMEM((PEERS, 4, FIRST), F32), pltpu.VMEM((PEERS, PIECE, DEPTH), F32), pltpu.VMEM((4 * PEERS, DEPTH), F32)],
    )
    packs = packs[:1] + [along(packs[hop], hop) for hop in range(1, RING)]
    moment = exchange(spread, ("x", "z"))
    moment_other = across(moment)
    loads, sens, returns, start, moment = kernel(
        unpack_kernel, "unpack", [moment, *packs],
        [((DEPTH, ALL), BF16), ((2, ALL), F32), ((1, ALL), F32), ((OWN, ALL), F32), ((DEPTH + 8, DEPTH), F32)],
    )
    given, weight, weight_sum = kernel(
        first_primal, "first_primal",
        [settings, moment, moment_other, *packs, loads, sens, returns, start],
        [((264, DEPTH), F32), ((OWN, ALL), F32), ((OWN, ALL), F32)],
    )
    other = across(given)
    old, base, excess, excess_sum, small = kernel(
        first_ready, "first_ready", [settings, dual_start, stat, given], scen_rows + [((4, DEPTH), F32)]
    )
    given, dual, dual_sum, price = kernel(
        first_dual, "first_dual", [settings, given, other, shocks, turned, old, base],
        [((264, DEPTH), F32)] + scen_rows[:2] + [((OWN, DEPTH), F32)],
    )
    other = across(given)
    (send,) = kernel(partial_back, "partial_back", [given, other, loads, sens], [((GRID_Z, OWN, SENT), BF16)])
    received = exchange(send, "z")
    (send,) = kernel(sum_z, "sum_z", [received], [((GRID_X, OWN, SENT), F32)])
    received = exchange(send, "x")
    given, stat = kernel(
        second_primal, "second_primal",
        [settings, received, *packs, loads, sens, returns, weight, weight_sum, price],
        [((328, DEPTH), F32), ((OWN, DEPTH), F32)],
    )
    other = across(given)
    base, extra_last, level_last = kernel(
        second_ready, "second_ready", [settings, dual, excess, excess_sum, small, stat, given],
        scen_rows[:2] + [((OWN, DEPTH), F32)],
    )
    outs = kernel(
        second_dual, "second_dual", [settings, given, other, turned, dual_sum, base, extra_last, level_last],
        [((OWN, 2 * SCEN_DEV + BLOCK + DEPTH), F32)] * RING,
    )
    taken = outs[:1] + [along(outs[hop], -hop) for hop in range(1, RING)]
    weights, duals, shortfall, threshold = kernel(
        close_kernel, "close", taken,
        [((8, BLOCK), F32), ((8, SCEN_DEV), F32), ((8, SCEN_DEV), F32), ((8,), F32)],
        [pltpu.VMEM((8, 2 * SCEN_DEV + BLOCK + DEPTH), F32)],
    )
    return weights, duals, shortfall, threshold


def solution(mesh):
    grid = Mesh(np.asarray(mesh.devices).reshape(GRID_X, GRID_Z, CORES, RING), ("x", "z", "c", "y"))
    scen = ("x", "z", "c")
    placed = (
        P(scen, None),
        P(None, ("y",) + scen),
        P(None, ("y",) + scen),
        P("y"),
        P(None, "y"),
        P(None, scen),
        P(),
        P(),
        P(),
        P(),
        P(),
    )
    return jax.shard_map(
        on_device,
        mesh=grid,
        in_specs=placed,
        out_specs=(P(None, "y"), P(None, scen), P(None, scen), P()),
        check_vma=False,
    )
```

```python
import math

import jax
import jax.numpy as jnp
import numpy as np
from jax import lax
from jax.experimental import pallas as pl
from jax.experimental.pallas import tpu as pltpu
from jax.sharding import Mesh, PartitionSpec as P

F32 = jnp.float32
BF16 = jnp.bfloat16
DEPTH = 128
SCEN_DEV = 4096
GRID_X, GRID_Z, CORES = 4, 8, 2
CHIPS = GRID_X * GRID_Z
PEERS = CHIPS * CORES
RING = 4
OWN = 2
PIECE = 16
HALF = PEERS * PIECE
BLOCK = 2 * HALF
ALL = RING * HALF
TOTAL_SCEN = float(PEERS * SCEN_DEV)
TOTAL_INST = float(RING * BLOCK)
SCALE = 1.0 / math.sqrt(TOTAL_INST)
SPLIT = 4
CHOSEN = 24 * 16
TAIL = 20.0
SETTINGS = ("primal", "rate", "averse", "level", "restart")
CHUNK = 512
NCHUNK = SCEN_DEV // CHUNK
FIRST = 5 * DEPTH
LINEAR = 40
SENT = ALL + DEPTH
PACK = HALF + PEERS + 80
LIMIT = 48 * 1024 * 1024


def dot(a, b):
    return jnp.dot(a, b, preferred_element_type=F32)


def dot_nt(a, b):
    return lax.dot_general(a, b, (((1,), (1,)), ((), ())), preferred_element_type=F32)


def split2(value):
    high = value.astype(BF16)
    return high, (value - high.astype(F32)).astype(BF16)


def split3(value):
    high = value.astype(BF16)
    rest = value - high.astype(F32)
    middle = rest.astype(BF16)
    return high, middle, (rest - middle.astype(F32)).astype(BF16)


def grid_iota(shape, axis):
    return lax.broadcasted_iota(jnp.int32, shape, axis)


def identity(size):
    return jnp.where(grid_iota((size, size), 0) == grid_iota((size, size), 1), 1.0, 0.0).astype(BF16)


def column(settings, name):
    spot = OWN * SETTINGS.index(name)
    return settings[spot : spot + OWN, 0:1]


def turn_to(rows, y):
    return pltpu.roll(rows, (8 - OWN * y) & 7, axis=0)


def turn_back(rows, y):
    return pltpu.roll(rows, (OWN * y) & 7, axis=0)


def count_row(mass):
    lane = grid_iota((1, DEPTH), 1)
    row = jnp.zeros((1, DEPTH), F32)
    for own in range(OWN):
        for part, value in enumerate(split3(mass[own : own + 1, :])):
            row = jnp.where(lane == 32 + 3 * own + part, value.astype(F32), row)
    return row


def mass_of(stat):
    first = stat[6:7, 32:33] + stat[6:7, 33:34] + stat[6:7, 34:35]
    second = stat[6:7, 35:36] + stat[6:7, 36:37] + stat[6:7, 37:38]
    return jnp.where(grid_iota((OWN, 1), 0) == 0, first, second)


def tail_rows(rows):
    return jnp.concatenate([rows, jnp.zeros((16 - OWN, rows.shape[1]), rows.dtype)], axis=0)


def moments(dual_of, shocks, turned):
    total = jnp.zeros((OWN * DEPTH + 16, DEPTH), F32)
    mass = jnp.zeros((OWN, 1), F32)
    for step in range(NCHUNK):
        cut = slice(step * CHUNK, (step + 1) * CHUNK)
        dual = dual_of(cut)
        rounded = dual.astype(BF16).astype(F32)
        wide = turned[:, cut].astype(F32)
        left = [(wide * rounded[own : own + 1, :]).astype(BF16) for own in range(OWN)]
        left = jnp.concatenate(left + [tail_rows(rounded).astype(BF16)], axis=0)
        total = total + dot(left, shocks[cut, :])
        mass = mass + jnp.sum(dual, axis=1, keepdims=True)
    return total * (1.0 / TOTAL_SCEN), mass * (1.0 / TOTAL_SCEN)


def open_kernel(shocks_in, dual_in, loadings_in, greeks_in, holdings_in, returns_in, *rest):
    given, rest = rest[: len(SETTINGS)], rest[len(SETTINGS) :]
    send, turned, chosen, work, lines, shocks, dual, loadings, greeks, holdings, returns, *taken, gates = rest
    y, core = lax.axis_index("y"), lax.axis_index("c")
    unit = identity(DEPTH)
    pairs = [
        (dual_in, dual), (loadings_in, loadings), (greeks_in, greeks), (holdings_in, holdings), (returns_in, returns),
        *zip(given, taken),
    ]
    for n in range(SPLIT):
        cut = pl.ds(SCEN_DEV // SPLIT * n, SCEN_DEV // SPLIT)
        pairs.append((shocks_in.at[cut, :], shocks.at[cut, :]))
    copies = [pltpu.make_async_copy(a, b, gates.at[n]) for n, (a, b) in enumerate(pairs)]
    for copy in copies:
        copy.start()
    for copy in copies[:-SPLIT]:
        copy.wait()
    pair = grid_iota((OWN, DEPTH), 0)
    for n, ref in enumerate(taken):
        values = jnp.where(pair == 0, ref[OWN * y], ref[OWN * y + 1])
        chosen[CHOSEN + OWN * n : CHOSEN + OWN * (n + 1), :] = values.astype(F32)
    m = grid_iota((2 * DEPTH, DEPTH), 0)
    lane = grid_iota((2 * DEPTH, DEPTH), 1)
    pick = jnp.where(m == (lane >> 4) * 32 + core * PIECE + (lane & 15), 1.0, 0.0).astype(BF16)
    for part in range(BLOCK // 256):
        cut = slice(256 * part, 256 * (part + 1))
        both = jnp.concatenate(
            [turn_to(holdings[:, cut], y), returns[:, cut], jnp.zeros((7, 256), F32)], axis=0
        )
        for level, value in enumerate(split3(both)):
            chosen[16 * (8 * level + part) : 16 * (8 * level + part) + 16, :] = dot(value, pick)

    for copy in copies[-SPLIT:]:
        copy.wait()

    for step in range(NCHUNK):
        cut = slice(step * CHUNK, (step + 1) * CHUNK)
        turned[:, cut] = dot_nt(unit, shocks[cut, :]).astype(BF16)
    total, mass = moments(lambda cut: turn_to(dual[:, cut], y)[0:OWN, :], shocks, turned)
    rows = loadings[...].astype(F32)
    sens = greeks[...].astype(F32)
    delta, gamma = sens[0:1, :].astype(BF16), sens[1:2, :].astype(BF16)
    m = grid_iota((2 * PIECE, DEPTH), 0)
    lane = grid_iota((2 * PIECE, DEPTH), 1)
    tally = count_row(mass)
    notes = []
    for half in range(2):
        near = jnp.where((m == lane + PIECE * half) & (lane < PIECE), 1.0, 0.0).astype(BF16)
        far = jnp.where(
            (m == lane - PIECE + PIECE * half) & (lane >= PIECE) & (lane < 2 * PIECE), 1.0, 0.0
        ).astype(BF16)
        notes.append(dot(delta, near) + dot(gamma, far) + tally)
    lane = grid_iota((CHIPS, DEPTH), 1)
    share = grid_iota((CHIPS, DEPTH), 0) == (lane >> 2)
    m = grid_iota((DEPTH, DEPTH), 0)
    place = jnp.where(LINEAR + (m & 3) == grid_iota((DEPTH, DEPTH), 1), 1.0, 0.0).astype(BF16)
    for half in range(2):
        base = DEPTH * half
        first, second = total[base + 64 : base + 96, :], total[base + 96 : base + 128, :]
        linear = jnp.where(share, total[256 + half : 257 + half, :], 0.0).astype(BF16)
        lines[base : base + 64, :] = total[base : base + 64, :]
        lines[base + 64 : base + 96, :] = jnp.where(lane < 64, pltpu.roll(first, 64, axis=1), second)
        lines[base + 96 : base + 128, :] = dot(linear, place) + notes[half]
    for peer in range(PEERS):
        half, chip = peer % 2, peer // 2
        for part in range(4):
            spot = PIECE * half + 4 * part
            work[peer, :, DEPTH * part : DEPTH * (part + 1)] = rows[spot : spot + 4, :]
            spot = DEPTH * half + 32 * part + chip
            work[peer, part : part + 1, 4 * DEPTH : FIRST] = lines[spot : spot + 1, :]
    send[...] = work[...].astype(BF16)


def sort_kernel(received, chosen, spread, stat, settings, *rest):
    settings[...] = chosen[CHOSEN:, :]
    packs, (work, placed, tail) = rest[:RING], rest[RING:]
    work[...] = received[...].astype(F32)
    for part in range(4):
        placed[:, 4 * part : 4 * part + 4, :] = work[:, :, DEPTH * part : DEPTH * (part + 1)]
    last = work[:, :, 4 * DEPTH : FIRST]
    sums = jnp.sum(last, axis=0)
    tail[...] = last.reshape(4 * PEERS, DEPTH)
    stat[...] = jnp.broadcast_to(sums[3:4, :], (8, DEPTH))
    spread[...] = jnp.broadcast_to(sums[None], (CHIPS, 4, DEPTH)).reshape(DEPTH, DEPTH)
    rows = placed[...].reshape(HALF, DEPTH).astype(BF16)
    notes = tail[pl.ds(3, PEERS, stride=4), :].astype(BF16)
    for hop in range(RING):
        pieces = [chosen[16 * n + OWN * hop : 16 * n + OWN * (hop + 1), :] for n in range(24)]
        pieces += [chosen[16 * n + 8 : 16 * n + 9, :] for n in range(24)]
        pieces.append(jnp.zeros((8, DEPTH), F32))
        packs[hop][0:HALF, :] = rows
        packs[hop][HALF : HALF + PEERS, :] = notes
        packs[hop][HALF + PEERS : PACK, :] = jnp.concatenate(pieces, axis=0).astype(BF16)


def matrix_parts(moment, linear):
    return jnp.concatenate(split2(jnp.concatenate([moment, tail_rows(linear)], axis=0)), axis=1)


def forms(parts, half):
    form = dot(parts, jnp.concatenate([half, half], axis=0))
    wide = half.astype(F32)
    curve = [
        jnp.sum(form[DEPTH * own : DEPTH * (own + 1), :] * wide, axis=0, keepdims=True)
        for own in range(OWN)
    ]
    return jnp.concatenate(curve, axis=0), form[OWN * DEPTH : OWN * DEPTH + OWN, :]


def holdings_matrix(bar, turned, rows, delta, gamma, stacked):
    rounded = bar.astype(BF16).astype(F32)
    curve = rounded * gamma
    left = [turned * curve[own : own + 1, :] for own in range(OWN)]
    left = jnp.concatenate(left + [tail_rows(rounded * delta)], axis=0)
    high, low = split2(left)
    if not stacked:
        return dot(high, rows) + dot(low, rows)
    both = dot(jnp.concatenate([high, low], axis=0), rows)
    half = OWN * DEPTH + 16
    return both[0:half, :] + both[half : 2 * half, :]


def share_rows(bar_sum):
    return jnp.broadcast_to(bar_sum, (OWN, DEPTH))


def unfold(moment):
    first, second, low, notes = (moment[pl.ds(n, CHIPS, stride=4), :] for n in range(4))
    upper = jnp.concatenate([first, second], axis=0)
    right = jnp.concatenate([pltpu.roll(low, 64, axis=1), low], axis=0)
    mirror = jnp.concatenate([upper, jnp.zeros((64, DEPTH), F32)], axis=0).T
    lower = jnp.where(grid_iota((64, DEPTH), 1) < 64, mirror[64:128, :], right)
    row, lane = grid_iota((DEPTH, DEPTH), 0), grid_iota((DEPTH, DEPTH), 1)
    pick = jnp.where(row == LINEAR + (lane & 3), 1.0, 0.0).astype(BF16)
    high, rest = split2(notes)
    spread = dot(high, pick) + dot(rest, pick)
    mine = grid_iota((CHIPS, DEPTH), 0) == (grid_iota((CHIPS, DEPTH), 1) >> 2)
    linear = jnp.sum(jnp.where(mine, spread, 0.0), axis=0, keepdims=True)
    return jnp.concatenate([upper, lower], axis=0), linear


def unpack_kernel(moment, pack0, pack1, pack2, pack3, turned, sens, returns, start, unfolded):
    matrix, linear = unfold(moment)
    unfolded[0:DEPTH, :] = matrix
    unfolded[DEPTH : DEPTH + 8, :] = jnp.broadcast_to(linear, (8, DEPTH))
    unit = identity(DEPTH)
    row = grid_iota((PEERS, HALF), 0)
    col = grid_iota((PEERS, HALF), 1)
    mine = row == (col >> 4)
    m = grid_iota((DEPTH, HALF), 0)
    slot = grid_iota((DEPTH, HALF), 1) & 15
    near = jnp.where(m == slot, 1.0, 0.0).astype(BF16)
    far = jnp.where(m == slot + PIECE, 1.0, 0.0).astype(BF16)
    for hop, pack in enumerate((pack0, pack1, pack2, pack3)):
        cut = slice(HALF * hop, HALF * (hop + 1))
        turned[:, cut] = dot_nt(unit, pack[0:HALF, :]).astype(BF16)
        notes = pack[HALF : HALF + PEERS, :]
        sens[0:1, cut] = jnp.sum(jnp.where(mine, dot(notes, near), 0.0), axis=0, keepdims=True)
        sens[1:2, cut] = 0.5 * jnp.sum(jnp.where(mine, dot(notes, far), 0.0), axis=0, keepdims=True)
        more = pack[HALF + PEERS : PACK, :].astype(F32)
        held = [
            more[2 * n : 2 * n + 2, :] + more[2 * n + 16 : 2 * n + 18, :] + more[2 * n + 32 : 2 * n + 34, :]
            for n in range(8)
        ]
        gain = [
            more[48 + n : 49 + n, :] + more[56 + n : 57 + n, :] + more[64 + n : 65 + n, :]
            for n in range(8)
        ]
        start[:, cut] = jnp.concatenate(held, axis=1)
        returns[:, cut] = jnp.concatenate(gain, axis=1)


def first_primal(
    settings, moment, moment_other, pack0, pack1, pack2, pack3, turned, sens, returns, start,
    given, weight, weight_sum,
):
    core = lax.axis_index("c")
    primal = column(settings, "primal")
    flag = column(settings, "restart") == 0.0
    mine = moment[0:DEPTH, :], moment[DEPTH : DEPTH + 1, :]
    others = unfold(moment_other)
    first = [jnp.where(core == 0, a, b) for a, b in zip(mine, others)]
    second = [jnp.where(core == 0, b, a) for a, b in zip(mine, others)]
    parts = matrix_parts(*(jnp.concatenate(pair, axis=0) for pair in zip(first, second)))
    total = jnp.zeros((OWN * DEPTH + 16, DEPTH), F32)
    bar_sum = jnp.zeros((OWN, 1), F32)
    for hop in range(RING):
        cut = slice(HALF * hop, HALF * (hop + 1))
        curve, line = forms(parts, turned[:, cut])
        weight[:, cut] = sens[0:1, cut] * line + sens[1:2, cut] * curve
    for hop, pack in enumerate((pack0, pack1, pack2, pack3)):
        cut = slice(HALF * hop, HALF * (hop + 1))
        held = start[:, cut]
        fresh = jnp.maximum(held + primal * (returns[:, cut] + weight[:, cut]), 0.0)
        bar = 2.0 * fresh - held
        bar_sum = bar_sum + jnp.sum(bar, axis=1, keepdims=True)
        wide = turned[:, cut].astype(F32)
        total = total + holdings_matrix(bar, wide, pack[0:HALF, :], sens[0:1, cut], sens[1:2, cut], True)
        both = held + fresh
        weight[:, cut] = jnp.where(flag, both / 2.0, fresh)
        weight_sum[:, cut] = jnp.where(flag, both / 2.0, both)
    given[0:256, :] = total[0:256, :]
    given[256:264, :] = jnp.concatenate(
        [total[256:258, :], share_rows(bar_sum), jnp.zeros((4, DEPTH), F32)], axis=0
    )


def three_parts(mass):
    lane = grid_iota((OWN, DEPTH), 1)
    tally = jnp.zeros((OWN, DEPTH), F32)
    for part, value in enumerate(split3(mass)):
        tally = jnp.where(lane == part, value.astype(F32), tally)
    return tally


def partial_back(given, other, turned, sens, send):
    others = other[...].astype(F32)
    whole = given[0:258, :] + others[0:258, :]
    mass = given[258:260, 0:1] + others[258:260, 0:1] + others[258:260, 1:2] + others[258:260, 2:3]
    parts = matrix_parts(whole[0:256, :], whole[256:258, :])
    for hop in range(RING):
        cut = slice(HALF * hop, HALF * (hop + 1))
        curve, line = forms(parts, turned[:, cut])
        back = (sens[0:1, cut] * line + sens[1:2, cut] * curve).astype(BF16)
        for peer in range(GRID_Z):
            send[peer, :, cut] = back
    tally = three_parts(mass).astype(BF16)
    for peer in range(GRID_Z):
        send[peer, :, ALL:SENT] = tally


def sum_z(received, send):
    total = received[0].astype(F32)
    for peer in range(1, GRID_Z):
        total = total + received[peer].astype(F32)
    for peer in range(GRID_X):
        send[peer] = total


def sum_x(received, cut):
    total = received[0, :, cut]
    for peer in range(1, GRID_X):
        total = total + received[peer, :, cut]
    return total


def second_primal(
    settings, received, pack0, pack1, pack2, pack3,
    turned, sens, returns, weight, weight_sum, price_row, given, stat,
):
    primal, restart = column(settings, "primal"), column(settings, "restart")
    first, flag = restart == 0.0, restart == 1.0
    count = jnp.where(first, 2.0, 3.0)
    price = price_row[:, 0:1]
    total = jnp.zeros((OWN * DEPTH + 16, DEPTH), F32)
    bar_sum = jnp.zeros((OWN, 1), F32)
    tally = sum_x(received, slice(ALL, SENT))
    stat[...] = jnp.broadcast_to(tally[:, 0:1] + tally[:, 1:2] + tally[:, 2:3], (OWN, DEPTH))
    for hop, pack in enumerate((pack0, pack1, pack2, pack3)):
        cut = slice(HALF * hop, HALF * (hop + 1))
        back = sum_x(received, cut)
        wide = turned[:, cut].astype(F32)
        held = weight[:, cut]
        fresh = jnp.maximum(held + primal * (returns[:, cut] + back + price), 0.0)
        bar = 2.0 * fresh - held
        bar_sum = bar_sum + jnp.sum(bar, axis=1, keepdims=True)
        total = total + holdings_matrix(bar, wide, pack[0:HALF, :], sens[0:1, cut], sens[1:2, cut], False)
        last = jnp.where(flag, (weight_sum[:, cut] + fresh) / count, fresh)
        for part in range(8):
            spot = 264 + OWN * (8 * hop + part)
            given[spot : spot + OWN, :] = last[:, DEPTH * part : DEPTH * (part + 1)]
    given[0:256, :] = total[0:256, :]
    given[256:264, :] = jnp.concatenate(
        [total[256:258, :], share_rows(bar_sum), jnp.zeros((4, DEPTH), F32)], axis=0
    )


def joint(given, other):
    whole = given[0:264, :] + other[0:264, :]
    share = whole[258:260, 0:1] * (1.0 / TOTAL_INST)
    matrix = jnp.concatenate([whole[0:256, :], tail_rows(whole[256:258, :])], axis=0)
    return jnp.concatenate(split2(matrix * SCALE), axis=1), share


def first_ready(settings, dual_start, stat, after, old, base, excess, excess_sum, small):
    y = lax.axis_index("y")
    primal, rate, averse, level, restart = (column(settings, name) for name in SETTINGS)
    flag = restart == 0.0
    level_new = level - primal * (averse - mass_of(stat))
    level_bar = 2.0 * level_new - level
    for step in range(NCHUNK):
        cut = slice(step * CHUNK, (step + 1) * CHUNK)
        dual = turn_to(dual_start[:, cut], y)[0:OWN, :]
        extra = jnp.maximum(0.0 - primal * (TAIL * averse - dual), 0.0)
        old[:, cut] = dual
        base[:, cut] = dual - rate * (2.0 * extra + level_bar)
        excess[:, cut], excess_sum[:, cut] = settle(flag, jnp.zeros_like(extra), extra)
    pieces = settle(flag, level, level_new)
    small[...] = jnp.concatenate([jnp.broadcast_to(piece, (OWN, DEPTH)) for piece in pieces], axis=0)


def settle(flag, old, new):
    both = old + new
    return jnp.where(flag, both / 2.0, new), jnp.where(flag, both / 2.0, both)


def first_dual(settings, given, other, shocks, turned, old, base, given_moment, sent, dual, dual_sum, price):
    rate, flag = column(settings, "rate"), column(settings, "restart") == 0.0
    parts, share = joint(given, other)

    def dual_of(cut):
        curve, line = forms(parts, turned[:, cut])
        fresh = jnp.maximum(base[:, cut] - rate * (curve + line), 0.0)
        dual[:, cut], dual_sum[:, cut] = state, _ = settle(flag, old[:, cut], fresh)
        return state

    total, mass = moments(dual_of, shocks, turned)
    price_new = rate * (1.0 - share)
    price[...] = jnp.broadcast_to(settle(flag, jnp.zeros_like(price_new), price_new)[0], (OWN, DEPTH))
    given_moment[0:256, :] = total[0:256, :]
    given_moment[256:264, :] = jnp.concatenate(
        [total[256:258, :], share_rows(mass), jnp.zeros((4, DEPTH), F32)], axis=0
    )
    last = [total[256:258, :], three_parts(mass), jnp.zeros((12, DEPTH), F32)]
    sent[...] = jnp.concatenate([total[0:256, :]] + last, axis=0).astype(BF16)


def second_ready(settings, dual, excess, excess_sum, small, stat, after, base, extra_last, level_last):
    primal, rate, averse, _, restart = (column(settings, name) for name in SETTINGS)
    flag, count = restart == 1.0, jnp.where(restart == 0.0, 2.0, 3.0)
    level = small[0:2, 0:1]
    level_new = level - primal * (averse - stat[:, 0:1])
    level_bar = 2.0 * level_new - level
    for step in range(NCHUNK):
        cut = slice(step * CHUNK, (step + 1) * CHUNK)
        old, old_extra = dual[:, cut], excess[:, cut]
        extra = jnp.maximum(old_extra - primal * (TAIL * averse - old), 0.0)
        base[:, cut] = old - rate * ((2.0 * extra - old_extra) + level_bar)
        extra_last[:, cut] = jnp.where(flag, (excess_sum[:, cut] + extra) / count, extra)
    last = jnp.where(flag, (small[2:4, 0:1] + level_new) / count, level_new)
    level_last[...] = jnp.broadcast_to(last, (OWN, DEPTH))


def second_dual(settings, given, other, turned, dual_sum, base, extra_last, level_last, out0, out1, out2, out3):
    core = lax.axis_index("c")
    outs = (out0, out1, out2, out3)
    rate, restart = column(settings, "rate"), column(settings, "restart")
    flag, count = restart == 1.0, jnp.where(restart == 0.0, 2.0, 3.0)
    parts, _ = joint(given, other)
    for step in range(NCHUNK):
        cut = slice(step * CHUNK, (step + 1) * CHUNK)
        curve, line = forms(parts, turned[:, cut])
        fresh = jnp.maximum(base[:, cut] - rate * (curve + line), 0.0)
        last = jnp.where(flag, (dual_sum[:, cut] + fresh) / count, fresh)
        for out in outs:
            out[:, cut] = last
            out[:, SCEN_DEV + step * CHUNK : SCEN_DEV + (step + 1) * CHUNK] = extra_last[:, cut]
    m = grid_iota((DEPTH, 256), 0)
    lane = grid_iota((DEPTH, 256), 1)
    source = (lane >> 5) * PIECE + (lane & 15)
    mine = ((lane >> 4) & 1) == core
    own_pick = jnp.where((m == source) & mine, 1.0, 0.0).astype(BF16)
    other_pick = jnp.where((m == source) & jnp.logical_not(mine), 1.0, 0.0).astype(BF16)
    own_parts, other_parts = split3(given[264:328, :]), split3(other[264:328, :])
    pieces = [dot(a, own_pick) + dot(b, other_pick) for a, b in zip(own_parts, other_parts)]
    held = pieces[0] + pieces[1] + pieces[2]
    for hop, out in enumerate(outs):
        out[:, 2 * SCEN_DEV + BLOCK :] = level_last[...]
        for part in range(8):
            spot = OWN * (8 * hop + part)
            start = 2 * SCEN_DEV + 256 * part
            out[:, start : start + 256] = held[spot : spot + OWN, :]


def close_kernel(in0, in1, in2, in3, weights, duals, shortfall, threshold, work):
    y = lax.axis_index("y")
    for hop, taken in enumerate((in0, in1, in2, in3)):
        work[OWN * hop : OWN * (hop + 1), :] = taken[...]
    start = 0
    for out, width in ((duals, SCEN_DEV), (shortfall, SCEN_DEV), (weights, BLOCK)):
        for left in range(0, width, CHUNK):
            right = min(left + CHUNK, width)
            out[:, left:right] = turn_back(work[:, start + left : start + right], y)
        start += width
    levels = turn_back(work[:, start:], y)
    for spot in range(8):
        threshold[spot] = jnp.max(levels[spot : spot + 1, :])


def kernel(body, name, arrays, outs, scratch=(), left=0, limit=LIMIT):
    small = pl.BlockSpec(memory_space=pltpu.SMEM)
    large = pl.BlockSpec(memory_space=pltpu.VMEM)
    given = [pl.BlockSpec(memory_space=pltpu.HBM)] * left + [large] * (len(arrays) - left)
    call = pl.pallas_call(
        body,
        name=name,
        in_specs=given,
        out_specs=[small if len(shape) == 1 else large for shape, _ in outs],
        out_shape=[jax.ShapeDtypeStruct(shape, dtype) for shape, dtype in outs],
        scratch_shapes=list(scratch),
        compiler_params=pltpu.CompilerParams(vmem_limit_bytes=limit),
    )
    return list(call(*arrays))


def along(value, hop):
    return lax.ppermute(value, "y", [(i, (i + hop) % RING) for i in range(RING)])


def across(value):
    return lax.ppermute(value, "c", [(0, 1), (1, 0)])


def exchange(value, axes):
    return lax.all_to_all(value, axes, 0, 0, tiled=True)


def on_device(
    shocks, loadings, greeks, mean_return, weight_start, dual_start, level_start, aversion, primal_step, dual_step, restart_at,
):
    scen_rows = [((OWN, SCEN_DEV), F32)] * 4
    send, turned, chosen = kernel(
        open_kernel, "open",
        [
            shocks, dual_start, loadings.T, greeks, weight_start, mean_return[None, :],
            primal_step, dual_step, aversion, level_start, restart_at,
        ],
        [((PEERS, 4, FIRST), BF16), ((DEPTH, SCEN_DEV), BF16), ((CHOSEN + 16, DEPTH), F32)],
        [
            pltpu.VMEM((PEERS, 4, FIRST), F32), pltpu.VMEM((OWN * DEPTH, DEPTH), F32), pltpu.VMEM((SCEN_DEV, DEPTH), BF16), pltpu.VMEM((8, SCEN_DEV), F32),
            pltpu.VMEM((2 * PIECE, DEPTH), BF16), pltpu.VMEM((3, 2 * PIECE), BF16), pltpu.VMEM((8, BLOCK), F32),
            pltpu.VMEM((1, BLOCK), F32), *[pltpu.SMEM((8,), F32)] * 4, pltpu.SMEM((8,), jnp.int32),
            pltpu.SemaphoreType.DMA((10 + SPLIT,)),
        ],
        left=11,
        limit=56 * 1024 * 1024,
    )
    received = exchange(send, ("x", "z", "c"))
    spread, stat, settings, *packs = kernel(
        sort_kernel, "sort", [received, chosen],
        [((DEPTH, DEPTH), F32), ((8, DEPTH), F32), ((16, DEPTH), F32)] + [((PACK, DEPTH), BF16)] * RING,
        [pltpu.VMEM((PEERS, 4, FIRST), F32), pltpu.VMEM((PEERS, PIECE, DEPTH), F32), pltpu.VMEM((4 * PEERS, DEPTH), F32)],
    )
    packs = packs[:1] + [along(packs[hop], hop) for hop in range(1, RING)]
    moment = exchange(spread, ("x", "z"))
    moment_other = across(moment)
    loads, sens, returns, start, moment = kernel(
        unpack_kernel, "unpack", [moment, *packs],
        [((DEPTH, ALL), BF16), ((2, ALL), F32), ((1, ALL), F32), ((OWN, ALL), F32), ((DEPTH + 8, DEPTH), F32)],
    )
    given, weight, weight_sum = kernel(
        first_primal, "first_primal",
        [settings, moment, moment_other, *packs, loads, sens, returns, start],
        [((264, DEPTH), F32), ((OWN, ALL), F32), ((OWN, ALL), F32)],
    )
    other = across(given)
    old, base, excess, excess_sum, small = kernel(
        first_ready, "first_ready", [settings, dual_start, stat, given], scen_rows + [((4, DEPTH), F32)]
    )
    given, sent, dual, dual_sum, price = kernel(
        first_dual, "first_dual", [settings, given, other, shocks, turned, old, base],
        [((264, DEPTH), F32), ((272, DEPTH), BF16)] + scen_rows[:2] + [((OWN, DEPTH), F32)],
    )
    other = across(sent)
    (send,) = kernel(partial_back, "partial_back", [given, other, loads, sens], [((GRID_Z, OWN, SENT), BF16)])
    received = exchange(send, "z")
    (send,) = kernel(sum_z, "sum_z", [received], [((GRID_X, OWN, SENT), F32)])
    received = exchange(send, "x")
    given, stat = kernel(
        second_primal, "second_primal",
        [settings, received, *packs, loads, sens, returns, weight, weight_sum, price],
        [((328, DEPTH), F32), ((OWN, DEPTH), F32)],
    )
    other = across(given)
    base, extra_last, level_last = kernel(
        second_ready, "second_ready", [settings, dual, excess, excess_sum, small, stat, given],
        scen_rows[:2] + [((OWN, DEPTH), F32)],
    )
    outs = kernel(
        second_dual, "second_dual", [settings, given, other, turned, dual_sum, base, extra_last, level_last],
        [((OWN, 2 * SCEN_DEV + BLOCK + DEPTH), F32)] * RING,
    )
    taken = outs[:1] + [along(outs[hop], -hop) for hop in range(1, RING)]
    weights, duals, shortfall, threshold = kernel(
        close_kernel, "close", taken,
        [((8, BLOCK), F32), ((8, SCEN_DEV), F32), ((8, SCEN_DEV), F32), ((8,), F32)],
        [pltpu.VMEM((8, 2 * SCEN_DEV + BLOCK + DEPTH), F32)],
    )
    return weights, duals, shortfall, threshold


def solution(mesh):
    grid = Mesh(np.asarray(mesh.devices).reshape(GRID_X, GRID_Z, CORES, RING), ("x", "z", "c", "y"))
    scen = ("x", "z", "c")
    placed = (
        P(scen, None),
        P(None, ("y",) + scen),
        P(None, ("y",) + scen),
        P("y"),
        P(None, "y"),
        P(None, scen),
        P(),
        P(),
        P(),
        P(),
        P(),
    )
    return jax.shard_map(
        on_device,
        mesh=grid,
        in_specs=placed,
        out_specs=(P(None, "y"), P(None, scen), P(None, scen), P()),
        check_vma=False,
    )
```

```python
import math

import jax
import jax.numpy as jnp
import numpy as np
from jax import lax
from jax.experimental import pallas as pl
from jax.experimental.pallas import tpu as pltpu
from jax.sharding import Mesh, PartitionSpec as P

F32 = jnp.float32
BF16 = jnp.bfloat16
DEPTH = 128
SCEN_DEV = 4096
GRID_X, GRID_Z, CORES = 4, 8, 2
CHIPS = GRID_X * GRID_Z
PEERS = CHIPS * CORES
RING = 4
OWN = 2
PIECE = 16
HALF = PEERS * PIECE
BLOCK = 2 * HALF
ALL = RING * HALF
TOTAL_SCEN = float(PEERS * SCEN_DEV)
TOTAL_INST = float(RING * BLOCK)
SCALE = 1.0 / math.sqrt(TOTAL_INST)
SPLIT = 4
CHOSEN = 24 * 16
TAIL = 20.0
SETTINGS = ("primal", "rate", "averse", "level", "restart")
CHUNK = 512
NCHUNK = SCEN_DEV // CHUNK
FIRST = 5 * DEPTH
LINEAR = 40
SENT = ALL + DEPTH
PACK = HALF + PEERS + 80
LIMIT = 48 * 1024 * 1024


def dot(a, b):
    return jnp.dot(a, b, preferred_element_type=F32)


def dot_nt(a, b):
    return lax.dot_general(a, b, (((1,), (1,)), ((), ())), preferred_element_type=F32)


def split2(value):
    high = value.astype(BF16)
    return high, (value - high.astype(F32)).astype(BF16)


def split3(value):
    high = value.astype(BF16)
    rest = value - high.astype(F32)
    middle = rest.astype(BF16)
    return high, middle, (rest - middle.astype(F32)).astype(BF16)


def grid_iota(shape, axis):
    return lax.broadcasted_iota(jnp.int32, shape, axis)


def identity(size):
    return jnp.where(grid_iota((size, size), 0) == grid_iota((size, size), 1), 1.0, 0.0).astype(BF16)


def column(settings, name):
    spot = OWN * SETTINGS.index(name)
    return settings[spot : spot + OWN, 0:1]


def turn_to(rows, y):
    return pltpu.roll(rows, (8 - OWN * y) & 7, axis=0)


def turn_back(rows, y):
    return pltpu.roll(rows, (OWN * y) & 7, axis=0)


def count_row(mass):
    lane = grid_iota((1, DEPTH), 1)
    row = jnp.zeros((1, DEPTH), F32)
    for own in range(OWN):
        for part, value in enumerate(split3(mass[own : own + 1, :])):
            row = jnp.where(lane == 32 + 3 * own + part, value.astype(F32), row)
    return row


def mass_of(stat):
    first = stat[6:7, 32:33] + stat[6:7, 33:34] + stat[6:7, 34:35]
    second = stat[6:7, 35:36] + stat[6:7, 36:37] + stat[6:7, 37:38]
    return jnp.where(grid_iota((OWN, 1), 0) == 0, first, second)


def tail_rows(rows):
    return jnp.concatenate([rows, jnp.zeros((16 - OWN, rows.shape[1]), rows.dtype)], axis=0)


def moments(dual_of, shocks, turned):
    total = jnp.zeros((OWN * DEPTH + 16, DEPTH), F32)
    mass = jnp.zeros((OWN, 1), F32)
    for step in range(NCHUNK):
        cut = slice(step * CHUNK, (step + 1) * CHUNK)
        dual = dual_of(cut)
        rounded = dual.astype(BF16).astype(F32)
        wide = turned[:, cut].astype(F32)
        left = [(wide * rounded[own : own + 1, :]).astype(BF16) for own in range(OWN)]
        left = jnp.concatenate(left + [tail_rows(rounded).astype(BF16)], axis=0)
        total = total + dot(left, shocks[cut, :])
        mass = mass + jnp.sum(dual, axis=1, keepdims=True)
    return total * (1.0 / TOTAL_SCEN), mass * (1.0 / TOTAL_SCEN)


def open_kernel(shocks_in, dual_in, loadings_in, greeks_in, holdings_in, returns_in, *rest):
    given, rest = rest[: len(SETTINGS)], rest[len(SETTINGS) :]
    send, turned, chosen, work, lines, shocks, dual, loadings, greeks, holdings, returns, *taken, gates = rest
    y, core = lax.axis_index("y"), lax.axis_index("c")
    unit = identity(DEPTH)
    pairs = [
        (dual_in, dual), (loadings_in, loadings), (greeks_in, greeks), (holdings_in, holdings), (returns_in, returns),
        *zip(given, taken),
    ]
    for n in range(SPLIT):
        cut = pl.ds(SCEN_DEV // SPLIT * n, SCEN_DEV // SPLIT)
        pairs.append((shocks_in.at[cut, :], shocks.at[cut, :]))
    copies = [pltpu.make_async_copy(a, b, gates.at[n]) for n, (a, b) in enumerate(pairs)]
    for copy in copies:
        copy.start()
    for copy in copies[:-SPLIT]:
        copy.wait()
    pair = grid_iota((OWN, DEPTH), 0)
    for n, ref in enumerate(taken):
        values = jnp.where(pair == 0, ref[OWN * y], ref[OWN * y + 1])
        chosen[CHOSEN + OWN * n : CHOSEN + OWN * (n + 1), :] = values.astype(F32)
    m = grid_iota((2 * DEPTH, DEPTH), 0)
    lane = grid_iota((2 * DEPTH, DEPTH), 1)
    pick = jnp.where(m == (lane >> 4) * 32 + core * PIECE + (lane & 15), 1.0, 0.0).astype(BF16)
    for part in range(BLOCK // 256):
        cut = slice(256 * part, 256 * (part + 1))
        both = jnp.concatenate(
            [turn_to(holdings[:, cut], y), returns[:, cut], jnp.zeros((7, 256), F32)], axis=0
        )
        for level, value in enumerate(split3(both)):
            chosen[16 * (8 * level + part) : 16 * (8 * level + part) + 16, :] = dot(value, pick)

    for copy in copies[-SPLIT:]:
        copy.wait()

    for step in range(NCHUNK):
        cut = slice(step * CHUNK, (step + 1) * CHUNK)
        turned[:, cut] = dot_nt(unit, shocks[cut, :]).astype(BF16)
    total, mass = moments(lambda cut: turn_to(dual[:, cut], y)[0:OWN, :], shocks, turned)
    rows = loadings[...].astype(F32)
    sens = greeks[...].astype(F32)
    delta, gamma = sens[0:1, :].astype(BF16), sens[1:2, :].astype(BF16)
    m = grid_iota((2 * PIECE, DEPTH), 0)
    lane = grid_iota((2 * PIECE, DEPTH), 1)
    tally = count_row(mass)
    notes = []
    for half in range(2):
        near = jnp.where((m == lane + PIECE * half) & (lane < PIECE), 1.0, 0.0).astype(BF16)
        far = jnp.where(
            (m == lane - PIECE + PIECE * half) & (lane >= PIECE) & (lane < 2 * PIECE), 1.0, 0.0
        ).astype(BF16)
        notes.append(dot(delta, near) + dot(gamma, far) + tally)
    lane = grid_iota((CHIPS, DEPTH), 1)
    share = grid_iota((CHIPS, DEPTH), 0) == (lane >> 2)
    m = grid_iota((DEPTH, DEPTH), 0)
    place = jnp.where(LINEAR + (m & 3) == grid_iota((DEPTH, DEPTH), 1), 1.0, 0.0).astype(BF16)
    for half in range(2):
        base = DEPTH * half
        first, second = total[base + 64 : base + 96, :], total[base + 96 : base + 128, :]
        linear = jnp.where(share, total[256 + half : 257 + half, :], 0.0).astype(BF16)
        lines[base : base + 64, :] = total[base : base + 64, :]
        lines[base + 64 : base + 96, :] = jnp.where(lane < 64, pltpu.roll(first, 64, axis=1), second)
        lines[base + 96 : base + 128, :] = dot(linear, place) + notes[half]
    for peer in range(PEERS):
        half, chip = peer % 2, peer // 2
        for part in range(4):
            spot = PIECE * half + 4 * part
            work[peer, :, DEPTH * part : DEPTH * (part + 1)] = rows[spot : spot + 4, :]
            spot = DEPTH * half + 32 * part + chip
            work[peer, part : part + 1, 4 * DEPTH : FIRST] = lines[spot : spot + 1, :]
    send[...] = work[...].astype(BF16)


def sort_kernel(received, chosen, spread, stat, settings, *rest):
    settings[...] = chosen[CHOSEN:, :]
    packs, (work, placed, tail) = rest[:RING], rest[RING:]
    work[...] = received[...].astype(F32)
    for part in range(4):
        placed[:, 4 * part : 4 * part + 4, :] = work[:, :, DEPTH * part : DEPTH * (part + 1)]
    last = work[:, :, 4 * DEPTH : FIRST]
    sums = jnp.sum(last, axis=0)
    tail[...] = last.reshape(4 * PEERS, DEPTH)
    stat[...] = jnp.broadcast_to(sums[3:4, :], (8, DEPTH))
    spread[...] = jnp.broadcast_to(sums[None], (CHIPS, 4, DEPTH)).reshape(DEPTH, DEPTH)
    rows = placed[...].reshape(HALF, DEPTH).astype(BF16)
    notes = tail[pl.ds(3, PEERS, stride=4), :].astype(BF16)
    for hop in range(RING):
        pieces = [chosen[16 * n + OWN * hop : 16 * n + OWN * (hop + 1), :] for n in range(24)]
        pieces += [chosen[16 * n + 8 : 16 * n + 9, :] for n in range(24)]
        pieces.append(jnp.zeros((8, DEPTH), F32))
        packs[hop][0:HALF, :] = rows
        packs[hop][HALF : HALF + PEERS, :] = notes
        packs[hop][HALF + PEERS : PACK, :] = jnp.concatenate(pieces, axis=0).astype(BF16)


def matrix_parts(moment, linear):
    return jnp.concatenate(split2(jnp.concatenate([moment, tail_rows(linear)], axis=0)), axis=1)


def forms(parts, half):
    form = dot(parts, jnp.concatenate([half, half], axis=0))
    wide = half.astype(F32)
    curve = [
        jnp.sum(form[DEPTH * own : DEPTH * (own + 1), :] * wide, axis=0, keepdims=True)
        for own in range(OWN)
    ]
    return jnp.concatenate(curve, axis=0), form[OWN * DEPTH : OWN * DEPTH + OWN, :]


def holdings_matrix(bar, turned, rows, delta, gamma, stacked):
    rounded = bar.astype(BF16).astype(F32)
    curve = rounded * gamma
    left = [turned * curve[own : own + 1, :] for own in range(OWN)]
    left = jnp.concatenate(left + [tail_rows(rounded * delta)], axis=0)
    high, low = split2(left)
    if not stacked:
        return dot(high, rows) + dot(low, rows)
    both = dot(jnp.concatenate([high, low], axis=0), rows)
    half = OWN * DEPTH + 16
    return both[0:half, :] + both[half : 2 * half, :]


def share_rows(bar_sum):
    return jnp.broadcast_to(bar_sum, (OWN, DEPTH))


def unfold(moment):
    first, second, low, notes = (moment[pl.ds(n, CHIPS, stride=4), :] for n in range(4))
    upper = jnp.concatenate([first, second], axis=0)
    right = jnp.concatenate([pltpu.roll(low, 64, axis=1), low], axis=0)
    mirror = jnp.concatenate([upper, jnp.zeros((64, DEPTH), F32)], axis=0).T
    lower = jnp.where(grid_iota((64, DEPTH), 1) < 64, mirror[64:128, :], right)
    row, lane = grid_iota((DEPTH, DEPTH), 0), grid_iota((DEPTH, DEPTH), 1)
    pick = jnp.where(row == LINEAR + (lane & 3), 1.0, 0.0).astype(BF16)
    high, rest = split2(notes)
    spread = dot(high, pick) + dot(rest, pick)
    mine = grid_iota((CHIPS, DEPTH), 0) == (grid_iota((CHIPS, DEPTH), 1) >> 2)
    linear = jnp.sum(jnp.where(mine, spread, 0.0), axis=0, keepdims=True)
    return jnp.concatenate([upper, lower], axis=0), linear


def unpack_kernel(moment, pack0, pack1, pack2, pack3, turned, sens, returns, start, unfolded):
    matrix, linear = unfold(moment)
    unfolded[0:DEPTH, :] = matrix
    unfolded[DEPTH : DEPTH + 8, :] = jnp.broadcast_to(linear, (8, DEPTH))
    unit = identity(DEPTH)
    row = grid_iota((PEERS, HALF), 0)
    col = grid_iota((PEERS, HALF), 1)
    mine = row == (col >> 4)
    m = grid_iota((DEPTH, HALF), 0)
    slot = grid_iota((DEPTH, HALF), 1) & 15
    near = jnp.where(m == slot, 1.0, 0.0).astype(BF16)
    far = jnp.where(m == slot + PIECE, 1.0, 0.0).astype(BF16)
    for hop, pack in enumerate((pack0, pack1, pack2, pack3)):
        cut = slice(HALF * hop, HALF * (hop + 1))
        turned[:, cut] = dot_nt(unit, pack[0:HALF, :]).astype(BF16)
        notes = pack[HALF : HALF + PEERS, :]
        sens[0:1, cut] = jnp.sum(jnp.where(mine, dot(notes, near), 0.0), axis=0, keepdims=True)
        sens[1:2, cut] = 0.5 * jnp.sum(jnp.where(mine, dot(notes, far), 0.0), axis=0, keepdims=True)
        more = pack[HALF + PEERS : PACK, :].astype(F32)
        held = [
            more[2 * n : 2 * n + 2, :] + more[2 * n + 16 : 2 * n + 18, :] + more[2 * n + 32 : 2 * n + 34, :]
            for n in range(8)
        ]
        gain = [
            more[48 + n : 49 + n, :] + more[56 + n : 57 + n, :] + more[64 + n : 65 + n, :]
            for n in range(8)
        ]
        start[:, cut] = jnp.concatenate(held, axis=1)
        returns[:, cut] = jnp.concatenate(gain, axis=1)


def first_primal(
    settings, moment, moment_other, pack0, pack1, pack2, pack3, turned, sens, returns, start,
    given, weight, weight_sum,
):
    core = lax.axis_index("c")
    primal = column(settings, "primal")
    flag = column(settings, "restart") == 0.0
    mine = moment[0:DEPTH, :], moment[DEPTH : DEPTH + 1, :]
    others = unfold(moment_other)
    first = [jnp.where(core == 0, a, b) for a, b in zip(mine, others)]
    second = [jnp.where(core == 0, b, a) for a, b in zip(mine, others)]
    parts = matrix_parts(*(jnp.concatenate(pair, axis=0) for pair in zip(first, second)))
    total = jnp.zeros((OWN * DEPTH + 16, DEPTH), F32)
    bar_sum = jnp.zeros((OWN, 1), F32)
    for hop in range(RING):
        cut = slice(HALF * hop, HALF * (hop + 1))
        curve, line = forms(parts, turned[:, cut])
        weight[:, cut] = sens[0:1, cut] * line + sens[1:2, cut] * curve
    for hop, pack in enumerate((pack0, pack1, pack2, pack3)):
        cut = slice(HALF * hop, HALF * (hop + 1))
        held = start[:, cut]
        fresh = jnp.maximum(held + primal * (returns[:, cut] + weight[:, cut]), 0.0)
        bar = 2.0 * fresh - held
        bar_sum = bar_sum + jnp.sum(bar, axis=1, keepdims=True)
        wide = turned[:, cut].astype(F32)
        total = total + holdings_matrix(bar, wide, pack[0:HALF, :], sens[0:1, cut], sens[1:2, cut], True)
        both = held + fresh
        weight[:, cut] = jnp.where(flag, both / 2.0, fresh)
        weight_sum[:, cut] = jnp.where(flag, both / 2.0, both)
    given[0:256, :] = total[0:256, :]
    given[256:264, :] = jnp.concatenate(
        [total[256:258, :], share_rows(bar_sum), jnp.zeros((4, DEPTH), F32)], axis=0
    )


def partial_back(given, other, turned, sens, send):
    whole = given[...] + other[...]
    parts = matrix_parts(whole[0:256, :], whole[256:258, :])
    for hop in range(RING):
        cut = slice(HALF * hop, HALF * (hop + 1))
        curve, line = forms(parts, turned[:, cut])
        back = (sens[0:1, cut] * line + sens[1:2, cut] * curve).astype(BF16)
        for peer in range(GRID_Z):
            send[peer, :, cut] = back
    lane = grid_iota((OWN, DEPTH), 1)
    tally = jnp.zeros((OWN, DEPTH), F32)
    for part, value in enumerate(split3(whole[258:260, 0:1])):
        tally = jnp.where(lane == part, value.astype(F32), tally)
    for peer in range(GRID_Z):
        send[peer, :, ALL:SENT] = tally.astype(BF16)


def sum_z(received, send):
    total = received[0].astype(F32)
    for peer in range(1, GRID_Z):
        total = total + received[peer].astype(F32)
    for peer in range(GRID_X):
        send[peer] = total


def sum_x(received, cut):
    total = received[0, :, cut]
    for peer in range(1, GRID_X):
        total = total + received[peer, :, cut]
    return total


def second_primal(
    settings, received, pack0, pack1, pack2, pack3,
    turned, sens, returns, weight, weight_sum, price_row, given, stat,
):
    primal, restart = column(settings, "primal"), column(settings, "restart")
    first, flag = restart == 0.0, restart == 1.0
    count = jnp.where(first, 2.0, 3.0)
    price = price_row[:, 0:1]
    total = jnp.zeros((OWN * DEPTH + 16, DEPTH), F32)
    bar_sum = jnp.zeros((OWN, 1), F32)
    tally = sum_x(received, slice(ALL, SENT))
    stat[...] = jnp.broadcast_to(tally[:, 0:1] + tally[:, 1:2] + tally[:, 2:3], (OWN, DEPTH))
    for hop, pack in enumerate((pack0, pack1, pack2, pack3)):
        cut = slice(HALF * hop, HALF * (hop + 1))
        back = sum_x(received, cut)
        wide = turned[:, cut].astype(F32)
        held = weight[:, cut]
        fresh = jnp.maximum(held + primal * (returns[:, cut] + back + price), 0.0)
        bar = 2.0 * fresh - held
        bar_sum = bar_sum + jnp.sum(bar, axis=1, keepdims=True)
        total = total + holdings_matrix(bar, wide, pack[0:HALF, :], sens[0:1, cut], sens[1:2, cut], False)
        last = jnp.where(flag, (weight_sum[:, cut] + fresh) / count, fresh)
        for part in range(8):
            spot = 264 + OWN * (8 * hop + part)
            given[spot : spot + OWN, :] = last[:, DEPTH * part : DEPTH * (part + 1)]
    given[0:256, :] = total[0:256, :]
    given[256:264, :] = jnp.concatenate(
        [total[256:258, :], share_rows(bar_sum), jnp.zeros((4, DEPTH), F32)], axis=0
    )


def joint(given, other):
    whole = given[0:264, :] + other[0:264, :]
    share = whole[258:260, 0:1] * (1.0 / TOTAL_INST)
    matrix = jnp.concatenate([whole[0:256, :], tail_rows(whole[256:258, :])], axis=0)
    return jnp.concatenate(split2(matrix * SCALE), axis=1), share


def first_ready(settings, dual_start, stat, after, old, base, excess, excess_sum, small):
    y = lax.axis_index("y")
    primal, rate, averse, level, restart = (column(settings, name) for name in SETTINGS)
    flag = restart == 0.0
    level_new = level - primal * (averse - mass_of(stat))
    level_bar = 2.0 * level_new - level
    for step in range(NCHUNK):
        cut = slice(step * CHUNK, (step + 1) * CHUNK)
        dual = turn_to(dual_start[:, cut], y)[0:OWN, :]
        extra = jnp.maximum(0.0 - primal * (TAIL * averse - dual), 0.0)
        old[:, cut] = dual
        base[:, cut] = dual - rate * (2.0 * extra + level_bar)
        excess[:, cut], excess_sum[:, cut] = settle(flag, jnp.zeros_like(extra), extra)
    pieces = settle(flag, level, level_new)
    small[...] = jnp.concatenate([jnp.broadcast_to(piece, (OWN, DEPTH)) for piece in pieces], axis=0)


def settle(flag, old, new):
    both = old + new
    return jnp.where(flag, both / 2.0, new), jnp.where(flag, both / 2.0, both)


def first_dual(settings, given, other, shocks, turned, old, base, given_moment, dual, dual_sum, price):
    rate, flag = column(settings, "rate"), column(settings, "restart") == 0.0
    parts, share = joint(given, other)

    def dual_of(cut):
        curve, line = forms(parts, turned[:, cut])
        fresh = jnp.maximum(base[:, cut] - rate * (curve + line), 0.0)
        dual[:, cut], dual_sum[:, cut] = state, _ = settle(flag, old[:, cut], fresh)
        return state

    total, mass = moments(dual_of, shocks, turned)
    price_new = rate * (1.0 - share)
    price[...] = jnp.broadcast_to(settle(flag, jnp.zeros_like(price_new), price_new)[0], (OWN, DEPTH))
    given_moment[0:256, :] = total[0:256, :]
    given_moment[256:264, :] = jnp.concatenate(
        [total[256:258, :], share_rows(mass), jnp.zeros((4, DEPTH), F32)], axis=0
    )


def widened(rows, core):
    m = grid_iota((DEPTH, 256), 0)
    lane = grid_iota((DEPTH, 256), 1)
    source = (lane >> 5) * PIECE + (lane & 15)
    pick = jnp.where((m == source) & (((lane >> 4) & 1) == core), 1.0, 0.0).astype(BF16)
    high, middle, low = (dot(part, pick) for part in split3(rows))
    return high + middle + low


def second_ready(settings, dual, excess, excess_sum, small, stat, given, base, extra_last, level_last, own_held):
    own_held[...] = widened(given[264:328, :], lax.axis_index("c"))
    primal, rate, averse, _, restart = (column(settings, name) for name in SETTINGS)
    flag, count = restart == 1.0, jnp.where(restart == 0.0, 2.0, 3.0)
    level = small[0:2, 0:1]
    level_new = level - primal * (averse - stat[:, 0:1])
    level_bar = 2.0 * level_new - level
    for step in range(NCHUNK):
        cut = slice(step * CHUNK, (step + 1) * CHUNK)
        old, old_extra = dual[:, cut], excess[:, cut]
        extra = jnp.maximum(old_extra - primal * (TAIL * averse - old), 0.0)
        base[:, cut] = old - rate * ((2.0 * extra - old_extra) + level_bar)
        extra_last[:, cut] = jnp.where(flag, (excess_sum[:, cut] + extra) / count, extra)
    last = jnp.where(flag, (small[2:4, 0:1] + level_new) / count, level_new)
    level_last[...] = jnp.broadcast_to(last, (OWN, DEPTH))


def second_dual(
    settings, given, other, turned, dual_sum, base, extra_last, level_last, own_held, out0, out1, out2, out3,
):
    core = lax.axis_index("c")
    outs = (out0, out1, out2, out3)
    rate, restart = column(settings, "rate"), column(settings, "restart")
    flag, count = restart == 1.0, jnp.where(restart == 0.0, 2.0, 3.0)
    parts, _ = joint(given, other)
    for step in range(NCHUNK):
        cut = slice(step * CHUNK, (step + 1) * CHUNK)
        curve, line = forms(parts, turned[:, cut])
        fresh = jnp.maximum(base[:, cut] - rate * (curve + line), 0.0)
        last = jnp.where(flag, (dual_sum[:, cut] + fresh) / count, fresh)
        for out in outs:
            out[:, cut] = last
            out[:, SCEN_DEV + step * CHUNK : SCEN_DEV + (step + 1) * CHUNK] = extra_last[:, cut]
    held = own_held[...] + widened(other[264:328, :], 1 - core)
    for hop, out in enumerate(outs):
        out[:, 2 * SCEN_DEV + BLOCK :] = level_last[...]
        for part in range(8):
            spot = OWN * (8 * hop + part)
            start = 2 * SCEN_DEV + 256 * part
            out[:, start : start + 256] = held[spot : spot + OWN, :]


def close_kernel(in0, in1, in2, in3, weights, duals, shortfall, threshold, work):
    y = lax.axis_index("y")
    for hop, taken in enumerate((in0, in1, in2, in3)):
        work[OWN * hop : OWN * (hop + 1), :] = taken[...]
    start = 0
    for out, width in ((duals, SCEN_DEV), (shortfall, SCEN_DEV), (weights, BLOCK)):
        for left in range(0, width, CHUNK):
            right = min(left + CHUNK, width)
            out[:, left:right] = turn_back(work[:, start + left : start + right], y)
        start += width
    levels = turn_back(work[:, start:], y)
    for spot in range(8):
        threshold[spot] = jnp.max(levels[spot : spot + 1, :])


def kernel(body, name, arrays, outs, scratch=(), left=0, limit=LIMIT):
    small = pl.BlockSpec(memory_space=pltpu.SMEM)
    large = pl.BlockSpec(memory_space=pltpu.VMEM)
    given = [pl.BlockSpec(memory_space=pltpu.HBM)] * left + [large] * (len(arrays) - left)
    call = pl.pallas_call(
        body,
        name=name,
        in_specs=given,
        out_specs=[small if len(shape) == 1 else large for shape, _ in outs],
        out_shape=[jax.ShapeDtypeStruct(shape, dtype) for shape, dtype in outs],
        scratch_shapes=list(scratch),
        compiler_params=pltpu.CompilerParams(vmem_limit_bytes=limit),
    )
    return list(call(*arrays))


def along(value, hop):
    return lax.ppermute(value, "y", [(i, (i + hop) % RING) for i in range(RING)])


def across(value):
    return lax.ppermute(value, "c", [(0, 1), (1, 0)])


def exchange(value, axes):
    return lax.all_to_all(value, axes, 0, 0, tiled=True)


def on_device(
    shocks, loadings, greeks, mean_return, weight_start, dual_start, level_start, aversion, primal_step, dual_step, restart_at,
):
    scen_rows = [((OWN, SCEN_DEV), F32)] * 4
    send, turned, chosen = kernel(
        open_kernel, "open",
        [
            shocks, dual_start, loadings.T, greeks, weight_start, mean_return[None, :],
            primal_step, dual_step, aversion, level_start, restart_at,
        ],
        [((PEERS, 4, FIRST), BF16), ((DEPTH, SCEN_DEV), BF16), ((CHOSEN + 16, DEPTH), F32)],
        [
            pltpu.VMEM((PEERS, 4, FIRST), F32), pltpu.VMEM((OWN * DEPTH, DEPTH), F32), pltpu.VMEM((SCEN_DEV, DEPTH), BF16), pltpu.VMEM((8, SCEN_DEV), F32),
            pltpu.VMEM((2 * PIECE, DEPTH), BF16), pltpu.VMEM((3, 2 * PIECE), BF16), pltpu.VMEM((8, BLOCK), F32),
            pltpu.VMEM((1, BLOCK), F32), *[pltpu.SMEM((8,), F32)] * 4, pltpu.SMEM((8,), jnp.int32),
            pltpu.SemaphoreType.DMA((10 + SPLIT,)),
        ],
        left=11,
        limit=56 * 1024 * 1024,
    )
    received = exchange(send, ("x", "z", "c"))
    spread, stat, settings, *packs = kernel(
        sort_kernel, "sort", [received, chosen],
        [((DEPTH, DEPTH), F32), ((8, DEPTH), F32), ((16, DEPTH), F32)] + [((PACK, DEPTH), BF16)] * RING,
        [pltpu.VMEM((PEERS, 4, FIRST), F32), pltpu.VMEM((PEERS, PIECE, DEPTH), F32), pltpu.VMEM((4 * PEERS, DEPTH), F32)],
    )
    packs = packs[:1] + [along(packs[hop], hop) for hop in range(1, RING)]
    moment = exchange(spread, ("x", "z"))
    moment_other = across(moment)
    loads, sens, returns, start, moment = kernel(
        unpack_kernel, "unpack", [moment, *packs],
        [((DEPTH, ALL), BF16), ((2, ALL), F32), ((1, ALL), F32), ((OWN, ALL), F32), ((DEPTH + 8, DEPTH), F32)],
    )
    given, weight, weight_sum = kernel(
        first_primal, "first_primal",
        [settings, moment, moment_other, *packs, loads, sens, returns, start],
        [((264, DEPTH), F32), ((OWN, ALL), F32), ((OWN, ALL), F32)],
    )
    other = across(given)
    old, base, excess, excess_sum, small = kernel(
        first_ready, "first_ready", [settings, dual_start, stat, given], scen_rows + [((4, DEPTH), F32)]
    )
    given, dual, dual_sum, price = kernel(
        first_dual, "first_dual", [settings, given, other, shocks, turned, old, base],
        [((264, DEPTH), F32)] + scen_rows[:2] + [((OWN, DEPTH), F32)],
    )
    other = across(given)
    (send,) = kernel(partial_back, "partial_back", [given, other, loads, sens], [((GRID_Z, OWN, SENT), BF16)])
    received = exchange(send, "z")
    (send,) = kernel(sum_z, "sum_z", [received], [((GRID_X, OWN, SENT), F32)])
    received = exchange(send, "x")
    given, stat = kernel(
        second_primal, "second_primal",
        [settings, received, *packs, loads, sens, returns, weight, weight_sum, price],
        [((328, DEPTH), F32), ((OWN, DEPTH), F32)],
    )
    other = across(given)
    base, extra_last, level_last, own_held = kernel(
        second_ready, "second_ready", [settings, dual, excess, excess_sum, small, stat, given],
        scen_rows[:2] + [((OWN, DEPTH), F32), ((64, 256), F32)],
    )
    outs = kernel(
        second_dual, "second_dual", [settings, given, other, turned, dual_sum, base, extra_last, level_last, own_held],
        [((OWN, 2 * SCEN_DEV + BLOCK + DEPTH), F32)] * RING,
    )
    taken = outs[:1] + [along(outs[hop], -hop) for hop in range(1, RING)]
    weights, duals, shortfall, threshold = kernel(
        close_kernel, "close", taken,
        [((8, BLOCK), F32), ((8, SCEN_DEV), F32), ((8, SCEN_DEV), F32), ((8,), F32)],
        [pltpu.VMEM((8, 2 * SCEN_DEV + BLOCK + DEPTH), F32)],
    )
    return weights, duals, shortfall, threshold


def solution(mesh):
    grid = Mesh(np.asarray(mesh.devices).reshape(GRID_X, GRID_Z, CORES, RING), ("x", "z", "c", "y"))
    scen = ("x", "z", "c")
    placed = (
        P(scen, None),
        P(None, ("y",) + scen),
        P(None, ("y",) + scen),
        P("y"),
        P(None, "y"),
        P(None, scen),
        P(),
        P(),
        P(),
        P(),
        P(),
    )
    return jax.shard_map(
        on_device,
        mesh=grid,
        in_specs=placed,
        out_specs=(P(None, "y"), P(None, scen), P(None, scen), P()),
        check_vma=False,
    )
```
